32 devices in a mesh: gy: 4 (over y, x), gx: 8 (over z, core).
Axes of the slice: x: 2, y: 2, z: 4, core: 2. Of those that a mesh axis runs over, the one named last changes fastest.
Arguments:
- direction: float32 [4, 32, 16, 512], P(None, 'gx', 'gy'), may hold values from -6 to 6
- solution: float32 [4, 32, 16, 512], P(None, 'gx', 'gy'), may hold values from -6 to 6
- residual: float32 [4, 32, 16, 512], P(None, 'gx', 'gy'), may hold values from -6 to 6
- north_coef: float32 [16, 512], P('gy'), may hold values from 0.12 to 0.25
- east_coef: float32 [16, 512], P('gy'), may hold values from 0.12 to 0.25
- ocean: int32 [16, 512], P('gy'), may hold values 0 or 1
- vert_coef: float32 [32, 16, 512], P(None, 'gy', 'gx'), may hold values from 0.1 to 10
- obs_owner: int32 [4, 8, 512, 1], P('gy', 'gx'), may hold values from 0 to 31; in each aligned block of 512 rows (0 to 511, 512 to 1023, ..., all dimensions but the last counted through in order) at most 32 rows name the same one
- obs_row: int32 [4, 8, 512], P('gy', 'gx'), may hold values from 0 to 2
- obs_col: int32 [4, 8, 512], P('gy', 'gx'), may hold values from 0 to 62
- obs_frac: float32 [4, 8, 2, 512], P('gy', 'gx'), may hold values from 0 to 1
- error_inverse: float32 [4, 8, 128, 128], P('gy', 'gx'), may hold values from -3 to 6, as said below
Outputs:
- solution_next: float32 [4, 32, 16, 512], P(None, 'gx', 'gy')
- residual_next: float32 [4, 32, 16, 512], P(None, 'gx', 'gy')
- direction_next: float32 [4, 32, 16, 512], P(None, 'gx', 'gy')
The draws below stay inside these ranges and needn't reach their ends.
Inputs may be any that keep to these rules, and one draw needn't show every extreme that they name: `obs_owner`: the observations of one device name each owner at most 32 times, and in every draw some device names some owner exactly 32 times. `error_inverse`: symmetric positive definite for every owner.
All inputs are finite; a program needn't handle non-finite values. No bound on the sum of `ocean` on one device may be relied on, other than what follows from the above.
Results may differ from the reference program's by a relative error of at most 0.000078.
Values sent between devices are 32-bit elements; how exact they have to be, the bound alone decides.
No kernel may reach another device: no remote copies, remote signals or barrier semaphores. Data moves between devices by JAX's collectives and lax.ppermute only.
A program may use at most 128 MiB of HBM per device.

```python
import math
import jax
import jax.numpy as jnp
import numpy as np
from jax import lax

NVAR = 4
LAT_DEV = 4
LON_DEV = 64
NSTEP = 4
OBS_DEV = 512
NLEV = 32
NLAT = 16
NLON = 512
KV = 128
CAP = 32
N_GY = 4
N_GX = 8


def draw_error_inverse(key, part):
    key_first, key_second = jax.random.split(jax.random.fold_in(key, 17))
    noise_draw = jnp.clip(jax.random.normal(key_first, (N_GY, N_GX, KV, KV), jnp.float32), -6.0, 6.0)
    symmetric = 0.5 * (noise_draw + jnp.swapaxes(noise_draw, 2, 3))
    scales = jnp.exp(jax.random.uniform(key_second, (N_GY, N_GX, 1, 1), jnp.float32, -0.6931472, 0.6931472))
    identity = jnp.eye(KV, dtype=jnp.float32)
    return scales * (1.6 * identity + 0.8 * symmetric / jnp.sqrt(jnp.float32(KV)))


def field_draw(key, salt):
    key_rough = jax.random.fold_in(jax.random.fold_in(key, salt), 0)
    field_shape = (NVAR, NLEV, NLAT, NLON)
    return jnp.clip(jax.random.normal(key_rough, field_shape, jnp.float32), -6.0, 6.0)


def draw_direction(key, part):
    return field_draw(key, 23)


def draw_residual(key, part):
    return field_draw(key, 29)


def with_ends(drawn, key, smallest, largest):
    extent = drawn.shape
    index_at = [jax.random.randint(jax.random.fold_in(key, axis), (), 0, extent[axis]) for axis in range(len(extent))]
    drawn = drawn.at[tuple(index_at)].set(smallest)
    longest = extent.index(max(extent))
    index_at[longest] = (index_at[longest] + 1) % extent[longest]
    return drawn.at[tuple(index_at)].set(largest)


def levels(key, shape, shards, low, high):
    gain, own = 1.0, jax.random.fold_in(key, 6)
    for axis_at, parts in shards:
        draws = jnp.exp(jax.random.uniform(jax.random.fold_in(own, axis_at), (parts,), jnp.float32, low / len(shards), high / len(shards)))
        gain = gain * jnp.repeat(draws, shape[axis_at] // parts).reshape([-1 if axis == axis_at else 1 for axis in range(len(shape))])
    return gain


def assign_block(own_key, own, number, rows, count, top, limit, lean):
    order = jax.random.permutation(own_key, count)
    packed, usual = load_shares(count, rows * top, limit, lean, True), load_shares(count, rows * top, limit, lean, False)
    places = jnp.arange(count)

    def named(tallies, turn):
        used = int((tallies > 0).sum())
        fixed = max(1, used // 4)
        shifted = fixed + (places - fixed + turn * (used - fixed)) % max(1, count - fixed)
        return jnp.zeros((count,), jnp.int32).at[order[jnp.where(places < fixed, places, shifted)]].set(jnp.asarray(tallies, jnp.int32))

    tallies = jnp.where(number % 4 == 0, named(packed, number // 4), named(usual, number - number // 4 - 1))
    mixed = jax.random.permutation(jax.random.fold_in(own, 3), count)
    donor, taker = mixed[0:count // 2 * 2:2], mixed[1:count // 2 * 2:2]
    room = jnp.minimum(tallies[donor] - 1, limit - tallies[taker]) // 2
    room = jnp.where((donor == order[0]) | (taker == order[0]) | (tallies[taker] == 0), 0, jnp.maximum(room, 0))
    shifted = jax.random.randint(jax.random.fold_in(own, 4), (count // 2,), 0, 1 << 20) % (room + 1)
    tallies = tallies.at[donor].add(-shifted).at[taker].add(shifted)
    items = jnp.searchsorted(jnp.cumsum(tallies), jnp.arange(rows * top), side="right").astype(jnp.int32)
    listing = items.reshape(top, rows).T
    listing = listing[jax.random.permutation(jax.random.fold_in(own, 1), rows)]
    turn = jax.random.randint(jax.random.fold_in(own, 2), (rows, 1), 0, top)
    return jnp.take_along_axis(listing, (jnp.arange(top)[None, :] + turn) % top, axis=1)


def load_shares(amount, total, bound, slope, full):
    weights = [(1 << 20) // math.isqrt(standing ** slope) + 1 for standing in range(1, amount + 1)]
    largest = bound if full else min(bound, max(-(-total // amount), total * weights[0] // sum(weights)))
    least = 1 if total - largest >= amount - 1 else 0
    holding, spare = [largest] + [least] * (amount - 1), total - largest - least * (amount - 1)
    while spare > 0:
        free = [i for i in range(1, amount) if holding[i] < largest] or [i for i in range(1, amount) if holding[i] < bound]
        whole, remaining = sum([weights[i] for i in free]), spare
        for i in free:
            addition = min(bound - holding[i], max(1, remaining * weights[i] // whole), spare)
            holding[i] = holding[i] + addition
            spare = spare - addition
    return np.array(holding)


def bell_draw(own_key, extent, scale, bound, shards=(), held_as=jnp.bfloat16):
    entries = jax.random.normal(own_key, extent, jnp.float32) * scale
    if len(shards) > 0:
        entries = levels(own_key, extent, shards, -0.22, 0.18) * entries
    return jnp.clip(entries, min=-bound, max=bound).astype(held_as)


def setup_inputs(seed: int = 0) -> dict:
    key_of = jax.random.split(jax.random.key(seed), 13)
    direction = draw_direction(jax.random.fold_in(key_of[12], 71), 0)
    solution = bell_draw(key_of[1], (NVAR, NLEV, NLAT, NLON), 1.0, 6.0, ((1, 8), (2, 4)), jnp.float32)
    residual = draw_residual(jax.random.fold_in(key_of[12], 71), 0)
    north_coef = jnp.clip(jnp.exp(math.log(0.25) - 0.7339692 * jax.random.uniform(key_of[3], (NLAT, NLON), jnp.float32) ** levels(key_of[3], (NLAT, NLON), ((0, 4),), -0.2, 0.2)), 0.12, 0.25)
    east_coef = jnp.clip(jnp.exp(math.log(0.25) - 0.7339692 * jax.random.uniform(key_of[4], (NLAT, NLON), jnp.float32) ** levels(key_of[4], (NLAT, NLON), ((0, 4),), -0.2, 0.2)), 0.12, 0.25)
    ocean = with_ends((jax.random.randint(key_of[5], (NLAT, NLON), 0, 10) < 9).astype(jnp.int32), jax.random.fold_in(key_of[5], 1), 0, 1)
    vert_coef = jnp.clip(jnp.exp(math.log(10.0) - 4.6051702 * jax.random.uniform(key_of[6], (NLEV, NLAT, NLON), jnp.float32) ** levels(key_of[6], (NLEV, NLAT, NLON), ((1, 4), (2, 8)), -0.2, 0.2)), 0.1, 10.0)
    obs_owner_keys = jax.random.split(jax.random.fold_in(key_of[7], 1), N_GY * N_GX * OBS_DEV // OBS_DEV)
    obs_owner_turns = jax.random.permutation(jax.random.fold_in(key_of[7], 3), N_GY * N_GX * OBS_DEV // OBS_DEV)
    obs_owner = jax.vmap(lambda own, number: assign_block(jax.random.fold_in(key_of[7], 2), own, number, OBS_DEV, N_GY * N_GX, 1, CAP, 2))(obs_owner_keys, obs_owner_turns).reshape((N_GY, N_GX, OBS_DEV, 1))
    obs_row = with_ends(jax.random.randint(key_of[8], (N_GY, N_GX, OBS_DEV), 0, LAT_DEV - 1), jax.random.fold_in(key_of[8], 1), 0, (LAT_DEV - 1) - 1).astype(jnp.int32)
    obs_col = with_ends(jax.random.randint(key_of[9], (N_GY, N_GX, OBS_DEV), 0, LON_DEV - 1), jax.random.fold_in(key_of[9], 1), 0, (LON_DEV - 1) - 1).astype(jnp.int32)
    obs_frac = jnp.clip(1.0 * jax.random.uniform(key_of[10], (N_GY, N_GX, 2, OBS_DEV), jnp.float32) ** levels(key_of[10], (N_GY, N_GX, 2, OBS_DEV), ((0, 4), (1, 8)), -0.2, 0.2), 0.0, 1.0)
    error_inverse = draw_error_inverse(jax.random.fold_in(key_of[12], 71), 0)
    return dict(direction=direction, solution=solution, residual=residual, north_coef=north_coef, east_coef=east_coef, ocean=ocean, vert_coef=vert_coef, obs_owner=obs_owner, obs_row=obs_row, obs_col=obs_col, obs_frac=obs_frac, error_inverse=error_inverse)


def lateral_faces(north_ext, east_ext, ocean_ext):
    ocean_next = jnp.concatenate([ocean_ext[1:], jnp.zeros_like(ocean_ext[:1])], axis=0)
    north_face = north_ext * ocean_ext * ocean_next
    east_face = east_ext * ocean_ext * jnp.roll(ocean_ext, -1, axis=1)
    return north_face, east_face, ocean_ext


def diffuse_once(values_grid, north_face, east_face, ocean_ext):
    north_flux = north_face[:-1] * (values_grid[:, :, 1:, :] - values_grid[:, :, :-1, :])
    east_flux = east_face * (jnp.roll(values_grid, -1, axis=3) - values_grid)
    lateral = east_flux - jnp.roll(east_flux, 1, axis=3)
    return (ocean_ext[1:-1] * values_grid[:, :, 1:-1, :] + north_flux[:, :, 1:, :] - north_flux[:, :, :-1, :]
            + lateral[:, :, 1:-1, :])


def lateral_whole(values_grid, faces):
    north_face, east_face, ocean_ext = faces
    for step_index in range(NSTEP):
        padded = jnp.pad(values_grid, ((0, 0), (0, 0), (1, 1), (0, 0)))
        values_grid = diffuse_once(padded, north_face, east_face, ocean_ext)
    return values_grid


def vertical_factors(vert_coef):
    inverse_rows = []
    upper_ratio = []
    for layer_index in range(vert_coef.shape[0]):
        diagonal = 1.0 + vert_coef[layer_index]
        if layer_index > 0:
            diagonal = diagonal + vert_coef[layer_index - 1] + vert_coef[layer_index - 1] * upper_ratio[-1]
        inverse = 1.0 / diagonal
        inverse_rows.append(inverse)
        upper_ratio.append(-vert_coef[layer_index] * inverse)
    return inverse_rows, upper_ratio


def vertical_solve(values_col, vert_coef, factors):
    inverse_rows, upper_ratio = factors
    layers = values_col.shape[1]
    forward = []
    for layer_index in range(layers):
        source = values_col[:, layer_index]
        if layer_index > 0:
            source = source + vert_coef[layer_index - 1] * forward[-1]
        forward.append(source * inverse_rows[layer_index])
    result = [forward[-1]]
    for layer_index in range(layers - 2, -1, -1):
        result.append(forward[layer_index] - upper_ratio[layer_index] * result[-1])
    return jnp.stack(result[::-1], axis=1)


def reference(direction, solution, residual, north_coef, east_coef, ocean, vert_coef, obs_owner, obs_row,
              obs_col, obs_frac, error_inverse):
    device_count = N_GY * N_GX
    pad_rows = ((1, 1), (0, 0))
    faces = lateral_faces(jnp.pad(north_coef, pad_rows), jnp.pad(east_coef, pad_rows),
                          jnp.pad(ocean.astype(jnp.float32), pad_rows))
    factors = vertical_factors(vert_coef)
    smoothed = vertical_solve(lateral_whole(direction, faces), vert_coef, factors)
    flat = smoothed.reshape(KV, NLAT * NLON)
    glob_row = jnp.arange(N_GY, dtype=jnp.int32)[:, None, None] * LAT_DEV + obs_row
    glob_col = jnp.arange(N_GX, dtype=jnp.int32)[None, :, None] * LON_DEV + obs_col
    cell = glob_row * NLON + glob_col
    corners = (cell, cell + 1, cell + NLON, cell + NLON + 1)
    lat_frac = obs_frac[:, :, 0, :]
    lon_frac = obs_frac[:, :, 1, :]
    weights = ((1.0 - lat_frac) * (1.0 - lon_frac), (1.0 - lat_frac) * lon_frac,
               lat_frac * (1.0 - lon_frac), lat_frac * lon_frac)
    profile = weights[0] * flat[:, corners[0]]
    for corner_index in range(1, 4):
        profile = profile + weights[corner_index] * flat[:, corners[corner_index]]
    owners = obs_owner[..., 0]
    onehot = (owners[..., None] == jnp.arange(device_count, dtype=jnp.int32)).astype(jnp.int32)
    running = jnp.cumsum(onehot, axis=2)
    rank_in = jnp.sum(running * onehot, axis=3) - 1
    source = (jnp.arange(N_GY, dtype=jnp.int32)[:, None, None] * N_GX
              + jnp.arange(N_GX, dtype=jnp.int32)[None, :, None]) + jnp.zeros_like(owners)
    slot = source * CAP + rank_in
    buffer = jnp.zeros((device_count, device_count * CAP, KV), jnp.float32)
    buffer = buffer.at[owners, slot].set(jnp.moveaxis(profile, 0, -1))
    weighted = jnp.einsum('osk,okl->osl', buffer, error_inverse.reshape(device_count, KV, KV),
                          precision=lax.Precision.HIGHEST)
    back = jnp.moveaxis(weighted[owners, slot], -1, 0)
    spread = jnp.zeros((KV, NLAT * NLON), jnp.float32)
    for corner_index in range(4):
        spread = spread.at[:, corners[corner_index]].add(weights[corner_index] * back)
    spread = spread.reshape(NVAR, NLEV, NLAT, NLON)
    image = direction + lateral_whole(vertical_solve(spread, vert_coef, factors), faces)
    norm_now = jnp.sum(residual * residual)
    alpha = norm_now / jnp.sum(direction * image)
    solution_next = solution + alpha * direction
    residual_next = residual - alpha * image
    norm_next = jnp.sum(residual_next * residual_next)
    direction_next = residual_next + (norm_next / norm_now) * direction
    return solution_next, residual_next, direction_next
```

```python
import functools
import math

import jax
import jax.numpy as jnp
from jax import lax
from jax.experimental import pallas as pl
from jax.experimental.pallas import tpu as pltpu
from jax.sharding import PartitionSpec as P

NSTEP = 4
LANES = 128
HIGHEST = lax.Precision.HIGHEST


def to_native(tile):
    kv, rows, lons = tile.shape[0] * tile.shape[1], tile.shape[2], tile.shape[3]
    return tile.reshape(kv, rows, lons // LANES, LANES).swapaxes(1, 2).reshape(-1, LANES)


def from_native(flat, shape):
    kv, rows, lons = shape[0] * shape[1], shape[2], shape[3]
    return flat.reshape(kv, lons // LANES, rows, LANES).swapaxes(1, 2).reshape(shape)


def native_rows(ref, base, row, rows, tiles, half):
    parts = [
        ref[pl.ds(base + (half * 8 * tiles + tile) * rows + row, 8, stride=tiles * rows), :]
        for tile in range(tiles)
    ]
    return jnp.concatenate(parts, axis=1)


def lane_low(shape):
    return lax.broadcasted_iota(jnp.int32, shape, 1) < LANES // 2


def lateral_rows(rows, coef, reach):
    for step in range(reach):
        after = []
        for i in range(1, len(rows) - 1):
            at = step + i
            u = rows[i]
            width = u.shape[1]
            after.append(
                coef[0, at : at + 1, :] * u
                + coef[1, at : at + 1, :] * rows[i + 1]
                + coef[2, at : at + 1, :] * rows[i - 1]
                + coef[3, at : at + 1, :] * pltpu.roll(u, width - 1, 1)
                + coef[4, at : at + 1, :] * pltpu.roll(u, 1, 1)
            )
        rows = after
    return rows


def first_lateral_kernel(kv, rows, tiles, own_ref, low_ref, high_ref, packed_ref, coef_ref, ext_ref):
    lons = tiles * LANES
    cells = kv * tiles * rows
    ext_ref[...] = jnp.zeros_like(ext_ref)
    for kind in range(3):
        for block, ref in enumerate((low_ref, own_ref, high_ref)):
            for tile in range(tiles):
                start = cells + (kind * tiles + tile) * rows
                ext_ref[kind, block * rows : (block + 1) * rows, tile * LANES : (tile + 1) * LANES] = ref[
                    start : start + rows, :
                ]
    total = ext_ref.shape[1]
    north, east, ocean = ext_ref[0], ext_ref[1], ext_ref[2]
    north_face = north * ocean * pltpu.roll(ocean, total - 1, 0)
    east_face = east * ocean * pltpu.roll(ocean, lons - 1, 1)
    south_face = pltpu.roll(north_face, 1, 0)
    west_face = pltpu.roll(east_face, 1, 1)
    coef_ref[0] = ocean - north_face - south_face - east_face - west_face
    coef_ref[1] = north_face
    coef_ref[2] = south_face
    coef_ref[3] = east_face
    coef_ref[4] = west_face
    low = lane_low((8, LANES))
    for half in range(kv // 8):
        grown = [
            native_rows(ref, 0, row, rows, tiles, half)
            for ref in (low_ref, own_ref, high_ref)
            for row in range(rows)
        ]
        done = lateral_rows(grown, coef_ref, rows)
        for pair in range(rows // 2):
            for tile in range(tiles):
                first = done[2 * pair][:, tile * LANES : (tile + 1) * LANES]
                second = done[2 * pair + 1][:, tile * LANES : (tile + 1) * LANES]
                at = pair * kv + half * 8
                packed_ref[2 * tile, at : at + 8, :] = jnp.where(
                    low, first, pltpu.roll(second, LANES // 2, 1)
                )
                packed_ref[2 * tile + 1, at : at + 8, :] = jnp.where(
                    low, pltpu.roll(first, LANES // 2, 1), second
                )


def second_lateral_kernel(
    kv, rows, tiles, own_ref, low_ref, high_ref, coef_ref, direction_ref, residual_ref, image_ref, sums_ref
):
    low = lane_low((8, LANES))
    totals = [jnp.zeros((8, tiles * LANES), jnp.float32) for _ in range(4)]
    for half in range(kv // 8):
        grown = []
        for ref in (low_ref, own_ref, high_ref):
            for pair in range(rows // 2):
                firsts, seconds = [], []
                at = pair * kv + half * 8
                for tile in range(tiles):
                    even = ref[2 * tile, at : at + 8, :]
                    odd = ref[2 * tile + 1, at : at + 8, :]
                    firsts.append(jnp.where(low, even, pltpu.roll(odd, LANES // 2, 1)))
                    seconds.append(jnp.where(low, pltpu.roll(even, LANES // 2, 1), odd))
                grown.append(jnp.concatenate(firsts, axis=1))
                grown.append(jnp.concatenate(seconds, axis=1))
        done = lateral_rows(grown, coef_ref, rows)
        for row in range(rows):
            direction = native_rows(direction_ref, 0, row, rows, tiles, half)
            residual = native_rows(residual_ref, 0, row, rows, tiles, half)
            image = direction + done[row]
            for tile in range(tiles):
                image_ref[pl.ds((half * 8 * tiles + tile) * rows + row, 8, stride=tiles * rows), :] = image[
                    :, tile * LANES : (tile + 1) * LANES
                ]
            totals[0] = totals[0] + residual * residual
            totals[1] = totals[1] + direction * image
            totals[2] = totals[2] + residual * image
            totals[3] = totals[3] + image * image
    lane = lax.broadcasted_iota(jnp.int32, (1, LANES), 1)
    line = jnp.zeros((1, LANES), jnp.float32)
    for at, total in enumerate(totals):
        line = jnp.where(lane == at, jnp.sum(total), line)
    for device in range(sums_ref.shape[0]):
        sums_ref[device] = line


def update_kernel(sums_ref, direction_ref, solution_ref, residual_ref, image_ref, sol_ref, res_ref, dir_ref):
    line = jnp.sum(sums_ref[...], axis=0)
    lane = lax.broadcasted_iota(jnp.int32, line.shape, 1)

    def pick(at):
        return jnp.sum(jnp.where(lane == at, line, 0.0), axis=1, keepdims=True)

    norm_now, curvature, cross, square = pick(0), pick(1), pick(2), pick(3)
    alpha = norm_now / curvature
    norm_next = norm_now - 2.0 * alpha * cross + alpha * alpha * square
    beta = norm_next / norm_now
    direction = direction_ref[...]
    residual_next = residual_ref[...] - alpha * image_ref[...]
    sol_ref[...] = solution_ref[...] + alpha * direction
    res_ref[...] = residual_next
    dir_ref[...] = residual_next + beta * direction


def prepare_kernel(
    strides, capacity, lon_cols, me_ref, vert_ref, owner_ref, row_ref, col_ref, frac_ref, factor_ref, interp_ref
):
    layers = vert_ref.shape[0]
    top = lax.broadcasted_iota(jnp.int32, (8, LANES), 0) < 4
    coef = [
        jnp.where(top, vert_ref[layer, 0:1, :], vert_ref[layer, 1:2, :]) for layer in range(layers)
    ]
    ratio = None
    for layer in range(layers):
        diagonal = 1.0 + coef[layer]
        if layer > 0:
            diagonal = diagonal + coef[layer - 1] - coef[layer - 1] * ratio
        inverse = 1.0 / diagonal
        ratio = coef[layer] * inverse
        factor_ref[0, layer] = inverse
        factor_ref[1, layer] = coef[layer - 1] * inverse if layer > 0 else jnp.zeros_like(inverse)
        factor_ref[2, layer] = ratio
    count = owner_ref.shape[1]
    devices = 1 << len(strides)
    slots = devices * capacity
    apart = jnp.bitwise_xor(owner_ref[...], me_ref[0])
    place = jnp.zeros_like(apart)
    for bit, stride in enumerate(strides):
        place = place + jnp.where(jnp.bitwise_and(apart, stride) != 0, 1 << bit, 0)
    named = jnp.where(
        lax.broadcasted_iota(jnp.int32, (devices, count), 0) == place, 1.0, 0.0
    )
    before = jnp.where(
        lax.broadcasted_iota(jnp.int32, (count, count), 0)
        <= lax.broadcasted_iota(jnp.int32, (count, count), 1),
        1.0,
        0.0,
    )
    running = jnp.dot(named, before, preferred_element_type=jnp.float32)
    rank = jnp.sum(named * running, axis=0, keepdims=True) - 1.0
    slot = place * capacity + rank.astype(jnp.int32)
    chosen = jnp.where(
        lax.broadcasted_iota(jnp.int32, (slots, count), 0) == slot, 1.0, 0.0
    )
    lat_frac = frac_ref[0:1, :]
    lon_frac = frac_ref[1:2, :]
    cell = (row_ref[...] * lon_cols + col_ref[...]).astype(jnp.float32)
    values = jnp.concatenate(
        [
            (1.0 - lat_frac) * (1.0 - lon_frac),
            (1.0 - lat_frac) * lon_frac,
            lat_frac * (1.0 - lon_frac),
            lat_frac * lon_frac,
            cell,
            jnp.zeros((3, count), jnp.float32),
        ],
        axis=0,
    )
    placed = lax.dot_general(
        values, chosen, (((1,), (1,)), ((), ())), precision=HIGHEST, preferred_element_type=jnp.float32
    )
    first = jnp.round(placed[4:5, :]).astype(jnp.int32)
    index = lax.broadcasted_iota(jnp.int32, interp_ref.shape, 0)
    away = index - first
    interp_ref[...] = jnp.where(
        away == 0,
        placed[0:1, :],
        jnp.where(
            away == 1,
            placed[1:2, :],
            jnp.where(away == lon_cols, placed[2:3, :], jnp.where(away == lon_cols + 1, placed[3:4, :], 0.0)),
        ),
    )


def solve_columns(read, write, factor_ref, layers):
    forward = []
    for layer in range(layers):
        value = read(layer) * factor_ref[0, layer]
        if layer > 0:
            value = value + factor_ref[1, layer] * forward[-1]
        forward.append(value)
    value = forward[-1]
    write(layers - 1, value)
    for layer in range(layers - 2, -1, -1):
        value = forward[layer] + factor_ref[2, layer] * value
        write(layer, value)


def observe_kernel(
    layers, held, capacity, packed_ref, factor_ref, interp_ref, near_ref, far_ref, out_ref, column_ref
):
    kv = near_ref.shape[1]
    block = 8 * held

    def packed_at(layer):
        return pl.ds((layer // held) * block + layer % held, 8, stride=held)

    def column_at(layer):
        return pl.ds(layer, 8, stride=layers)

    def read_packed(layer):
        return packed_ref[packed_at(layer), :]

    def write_column(layer, value):
        column_ref[column_at(layer), :] = value

    solve_columns(read_packed, write_column, factor_ref, layers)
    columns = jnp.concatenate([column_ref[0:kv, :], column_ref[kv : 2 * kv, :]], axis=1)
    interp = interp_ref[...]
    profile = jnp.dot(columns, interp, precision=HIGHEST, preferred_element_type=jnp.float32)
    owners = LANES // capacity
    mine = lax.broadcasted_iota(jnp.int32, (kv, LANES), 1) // capacity
    near = near_ref.shape[0]
    parts = []
    for tile in range(profile.shape[1] // LANES):
        values = profile[:, tile * LANES : (tile + 1) * LANES]
        first = tile * owners
        ref, at = (near_ref, first) if first < near else (far_ref, first - near)
        matrices = ref[at : at + owners].reshape(owners * kv, kv)
        product = jnp.dot(matrices, values, precision=HIGHEST, preferred_element_type=jnp.float32)
        kept = product[0:kv]
        for owner in range(1, owners):
            kept = jnp.where(mine == owner, product[owner * kv : (owner + 1) * kv], kept)
        parts.append(kept)
    weighted = jnp.concatenate(parts, axis=1)
    spread = lax.dot_general(
        weighted, interp, (((1,), (1,)), ((), ())), precision=HIGHEST, preferred_element_type=jnp.float32
    )
    column_ref[0:kv, :] = spread[:, :LANES]
    column_ref[kv : 2 * kv, :] = spread[:, LANES:]

    def read_column(layer):
        return column_ref[column_at(layer), :]

    def write_packed(layer, value):
        out_ref[packed_at(layer), :] = value

    solve_columns(read_column, write_packed, factor_ref, layers)


def vmem(count):
    return [pl.BlockSpec(memory_space=pltpu.VMEM)] * count


def call(kernel, out_shape, inputs, scratch=(), smem_first=False, flops=1_000_000):
    specs = vmem(len(inputs))
    if smem_first:
        specs[0] = pl.BlockSpec(memory_space=pltpu.SMEM)
    many = isinstance(out_shape, (list, tuple))
    moved = sum(math.prod(x.shape) * 4 for x in inputs)
    return pl.pallas_call(
        kernel,
        out_shape=out_shape,
        in_specs=specs,
        out_specs=tuple(vmem(len(out_shape))) if many else vmem(1)[0],
        scratch_shapes=list(scratch),
        compiler_params=pltpu.CompilerParams(vmem_limit_bytes=32 * 1024 * 1024),
        cost_estimate=pl.CostEstimate(flops=flops, bytes_accessed=moved, transcendentals=0),
    )(*inputs)


def f32(*shape):
    return jax.ShapeDtypeStruct(shape, jnp.float32)


def from_neighbours(block):
    count = lax.axis_size("gy")
    low = lax.ppermute(block, "gy", [(i, i + 1) for i in range(count - 1)])
    high = lax.ppermute(block, "gy", [(i + 1, i) for i in range(count - 1)])
    return low, high


def gather_order(rows_y, cols_x):
    order = []
    stride = cols_x // 2
    while stride > 1:
        order.append(("gx", stride))
        stride //= 2
    stride = rows_y // 2
    while stride >= 1:
        order.append(("gy", stride))
        stride //= 2
    if cols_x > 1:
        order.append(("gx", 1))
    numbers = [stride * (cols_x if axis == "gy" else 1) for axis, stride in order]
    return order, numbers


def per_device_gathered(
    direction,
    solution,
    residual,
    north_coef,
    east_coef,
    ocean,
    vert_coef,
    obs_owner,
    obs_row,
    obs_col,
    obs_frac,
    error_inverse,
):
    var_count, held, rows, lons = direction.shape
    kv = var_count * held
    tiles = lons // LANES
    layers, _, lon_cols = vert_coef.shape
    rows_y, cols_x = lax.axis_size("gy"), lax.axis_size("gx")
    device_count = rows_y * cols_x
    obs_count = obs_row.shape[-1]
    capacity = 2 * obs_count // device_count
    wide = error_inverse.shape[-1]
    cells = rows * lon_cols
    order, numbers = gather_order(rows_y, cols_x)

    direction_n = to_native(direction)
    residual_n = to_native(residual)
    solution_n = to_native(solution)
    lateral = jnp.stack([north_coef, east_coef, ocean.astype(jnp.float32)])[:, None]
    own = jnp.concatenate([direction_n, to_native(lateral)], axis=0)
    low, high = from_neighbours(own)

    blocks = error_inverse.reshape(1, wide, wide)
    other = None
    for axis, stride in order:
        if other is not None:
            blocks = jnp.concatenate([blocks, other], axis=0)
        other = lax.ppermute(blocks, axis, [(i, i ^ stride) for i in range(lax.axis_size(axis))])

    me = (lax.axis_index("gy") * cols_x + lax.axis_index("gx")).astype(jnp.int32).reshape(1)
    factors, interp = call(
        functools.partial(prepare_kernel, tuple(numbers), capacity, lon_cols),
        (f32(3, layers, 8, LANES), f32(cells, device_count * capacity)),
        (
            me,
            vert_coef.reshape(layers, cells // LANES, LANES),
            obs_owner.reshape(1, obs_count),
            obs_row.reshape(1, obs_count),
            obs_col.reshape(1, obs_count),
            obs_frac.reshape(2, obs_count),
        ),
        smem_first=True,
        flops=20_000_000,
    )

    extended = 3 * rows + (-3 * rows) % 8
    packed, coef = call(
        functools.partial(first_lateral_kernel, kv, rows, tiles),
        (f32(cols_x, 2 * kv, LANES), f32(5, extended, lons)),
        (own, low, high),
        scratch=(pltpu.VMEM((3, extended, lons), jnp.float32),),
        flops=4_000_000,
    )
    columns = lax.all_to_all(packed, "gx", split_axis=0, concat_axis=0, tiled=True)
    spread = call(
        functools.partial(observe_kernel, layers, held, capacity),
        f32(cols_x * 2 * kv, LANES),
        (columns.reshape(cols_x * 2 * kv, LANES), factors, interp, blocks, other),
        scratch=(pltpu.VMEM((2 * wide, LANES), jnp.float32),),
        flops=1_000_000_000,
    )
    tile = lax.all_to_all(
        spread.reshape(cols_x, 2 * kv, LANES), "gx", split_axis=0, concat_axis=0, tiled=True
    )
    low, high = from_neighbours(tile)
    image, sums = call(
        functools.partial(second_lateral_kernel, kv, rows, tiles),
        (f32(*direction_n.shape), f32(device_count, 1, LANES)),
        (tile, low, high, coef, direction_n, residual_n),
        flops=4_000_000,
    )
    sums = lax.all_to_all(sums, ("gy", "gx"), split_axis=0, concat_axis=0, tiled=True)
    after = call(
        update_kernel,
        (f32(*direction_n.shape),) * 3,
        (sums, direction_n, solution_n, residual_n, image),
    )
    return tuple(from_native(x, direction.shape) for x in after)


def gathers(mesh, shapes):
    rows_y, cols_x = mesh.shape["gy"], mesh.shape["gx"]
    devices = rows_y * cols_x
    direction, vert_coef, obs_row, error_inverse = shapes
    var_count, layers, lat_rows, lons = direction
    rows, held = lat_rows // rows_y, layers // cols_x
    obs_count, wide = obs_row[-1], error_inverse[-1]
    capacity = 2 * obs_count // devices
    return (
        devices & (devices - 1) == 0
        and devices > 1
        and rows == NSTEP == 4
        and var_count == 4
        and (var_count * held) % 8 == 0
        and lons // cols_x * 2 == LANES
        and wide == LANES
        and capacity > 0
        and LANES % capacity == 0
        and devices // 2 % (LANES // capacity) == 0
        and devices * wide * wide * 4 <= 8 * 1024 * 1024
    )


def padded(cells, sides, width):
    for axis, dim in sides:
        count = lax.axis_size(axis)
        ends = count - 1
        head = lax.slice_in_dim(cells, 0, width, axis=dim)
        tail = lax.slice_in_dim(cells, cells.shape[dim] - width, cells.shape[dim], axis=dim)
        cells = jnp.concatenate(
            [
                lax.ppermute(tail, axis, [(i, (i + 1) % count) for i in range(ends)]),
                cells,
                lax.ppermute(head, axis, [((i + 1) % count, i) for i in range(ends)]),
            ],
            axis=dim,
        )
    return cells


def lateral_faces(north_ext, east_ext, ocean_ext):
    ocean_next = jnp.concatenate([ocean_ext[1:], jnp.zeros_like(ocean_ext[:1])], axis=0)
    north_face = north_ext * ocean_ext * ocean_next
    east_face = east_ext * ocean_ext * jnp.roll(ocean_ext, -1, axis=1)
    return (north_face, east_face, ocean_ext)


def diffuse_once(values_grid, north_face, east_face, ocean_ext):
    north_flux = north_face[:-1] * (values_grid[:, :, 1:, :] - values_grid[:, :, :-1, :])
    east_flux = east_face * (jnp.roll(values_grid, -1, axis=3) - values_grid)
    lateral = east_flux - jnp.roll(east_flux, 1, axis=3)
    return (
        ocean_ext[1:-1] * values_grid[:, :, 1:-1, :]
        + north_flux[:, :, 1:, :]
        - north_flux[:, :, :-1, :]
        + lateral[:, :, 1:-1, :]
    )


def lateral_pass(values_tile, faces):
    north_face, east_face, ocean_ext = faces
    grown = padded(values_tile, (("gy", 2),), NSTEP)
    total_rows = grown.shape[2]
    for step_index in range(NSTEP):
        upper = total_rows - step_index
        grown = diffuse_once(
            grown,
            north_face[step_index:upper],
            east_face[step_index:upper],
            ocean_ext[step_index:upper],
        )
    return grown


def vertical_factors(vert_coef):
    inverse_rows = []
    upper_ratio = []
    for layer_index in range(vert_coef.shape[0]):
        diagonal = 1.0 + vert_coef[layer_index]
        if layer_index > 0:
            diagonal = (
                diagonal + vert_coef[layer_index - 1] + vert_coef[layer_index - 1] * upper_ratio[-1]
            )
        inverse = 1.0 / diagonal
        inverse_rows.append(inverse)
        upper_ratio.append(-vert_coef[layer_index] * inverse)
    return (inverse_rows, upper_ratio)


def vertical_solve(values_col, vert_coef, factors):
    inverse_rows, upper_ratio = factors
    layers = values_col.shape[1]
    forward = []
    for layer_index in range(layers):
        source = values_col[:, layer_index]
        if layer_index > 0:
            source = source + vert_coef[layer_index - 1] * forward[-1]
        forward.append(source * inverse_rows[layer_index])
    result = [forward[-1]]
    for layer_index in range(layers - 2, -1, -1):
        result.append(forward[layer_index] - upper_ratio[layer_index] * result[-1])
    return jnp.stack(result[::-1], axis=1)


def observe_weigh_spread(columns, obs_owner, obs_row, obs_col, obs_frac, error_inverse):
    var_count, lev_count, lat_rows, lon_cols = columns.shape
    kv_width = var_count * lev_count
    rows_y = lax.axis_size("gy")
    cols_x = lax.axis_size("gx")
    device_count = rows_y * cols_x
    obs_count = obs_row.shape[-1]
    capacity = 2 * obs_count // device_count
    flat = columns.reshape(kv_width, lat_rows * lon_cols)
    cell = obs_row.reshape(-1) * lon_cols + obs_col.reshape(-1)
    corners = (cell, cell + 1, cell + lon_cols, cell + lon_cols + 1)
    lat_frac = obs_frac[0, 0, 0]
    lon_frac = obs_frac[0, 0, 1]
    weights = (
        (1.0 - lat_frac) * (1.0 - lon_frac),
        (1.0 - lat_frac) * lon_frac,
        lat_frac * (1.0 - lon_frac),
        lat_frac * lon_frac,
    )
    profile = weights[0] * jnp.take(flat, corners[0], axis=1)
    for corner_index in range(1, 4):
        profile = profile + weights[corner_index] * jnp.take(flat, corners[corner_index], axis=1)
    owners = obs_owner.reshape(-1)
    onehot = (owners[:, None] == jnp.arange(device_count, dtype=jnp.int32)[None, :]).astype(
        jnp.int32
    )
    running = jnp.cumsum(onehot, axis=0)
    rank_in = jnp.sum(running * onehot, axis=1) - 1
    slot = owners * capacity + rank_in
    outgoing = jnp.zeros((device_count * capacity, kv_width), jnp.float32).at[slot].set(profile.T)
    outgoing = outgoing.reshape(rows_y, cols_x, capacity, kv_width)
    matrix = error_inverse.reshape(kv_width, kv_width)
    arrived = lax.all_to_all(
        lax.all_to_all(outgoing, "gy", split_axis=0, concat_axis=0, tiled=True),
        "gx",
        split_axis=1,
        concat_axis=1,
        tiled=True,
    )
    weighted = jnp.dot(
        arrived.reshape(-1, kv_width),
        matrix,
        precision=lax.Precision.HIGHEST,
        preferred_element_type=jnp.float32,
    ).reshape(rows_y, cols_x, capacity, kv_width)
    returned = lax.all_to_all(
        lax.all_to_all(weighted, "gy", split_axis=0, concat_axis=0, tiled=True),
        "gx",
        split_axis=1,
        concat_axis=1,
        tiled=True,
    )
    back = returned.reshape(device_count * capacity, kv_width)[slot].T
    spread = jnp.zeros((kv_width, lat_rows * lon_cols), jnp.float32)
    for corner_index in range(4):
        spread = spread.at[:, corners[corner_index]].add(weights[corner_index] * back)
    return spread.reshape(var_count, lev_count, lat_rows, lon_cols)


def per_device(
    direction,
    solution,
    residual,
    north_coef,
    east_coef,
    ocean,
    vert_coef,
    obs_owner,
    obs_row,
    obs_col,
    obs_frac,
    error_inverse,
):
    stacked = jnp.stack([north_coef, east_coef, ocean.astype(jnp.float32)])
    reach = NSTEP
    grown_coef = padded(stacked, (("gy", 1),), reach)
    faces = lateral_faces(grown_coef[0], grown_coef[1], grown_coef[2])
    factors = vertical_factors(vert_coef)
    smoothed = lateral_pass(direction, faces)
    columns = lax.all_to_all(smoothed, "gx", split_axis=3, concat_axis=1, tiled=True)
    columns = vertical_solve(columns, vert_coef, factors)
    spread = observe_weigh_spread(columns, obs_owner, obs_row, obs_col, obs_frac, error_inverse)
    spread = vertical_solve(spread, vert_coef, factors)
    tiles = lax.all_to_all(spread, "gx", split_axis=1, concat_axis=3, tiled=True)
    image = direction + lateral_pass(tiles, faces)
    norm_now, curvature = lax.psum(
        (jnp.sum(residual * residual), jnp.sum(direction * image)), ("gy", "gx")
    )
    alpha = norm_now / curvature
    residual_next = residual - alpha * image
    norm_next = lax.psum(jnp.sum(residual_next * residual_next), ("gy", "gx"))
    solution_next = solution + alpha * direction
    direction_next = residual_next + norm_next / norm_now * direction
    return (solution_next, residual_next, direction_next)


def solution(mesh):
    in_specs = (
        P(None, "gx", "gy", None),
        P(None, "gx", "gy", None),
        P(None, "gx", "gy", None),
        P("gy", None),
        P("gy", None),
        P("gy", None),
        P(None, "gy", "gx"),
        P("gy", "gx", None, None),
        P("gy", "gx", None),
        P("gy", "gx", None),
        P("gy", "gx", None, None),
        P("gy", "gx", None, None),
    )
    out_specs = (P(None, "gx", "gy", None),) * 3

    def step(*arrays):
        shapes = [arrays[at].shape for at in (0, 6, 8, 11)]
        local = per_device_gathered if gathers(mesh, shapes) else per_device
        return jax.shard_map(
            local, mesh=mesh, in_specs=in_specs, out_specs=out_specs, check_vma=False
        )(*arrays)

    return step
```

```python
import functools
import math

import jax
import jax.numpy as jnp
from jax import lax
from jax.experimental import pallas as pl
from jax.experimental.pallas import tpu as pltpu
from jax.sharding import PartitionSpec as P

NSTEP = 4
LANES = 128
HIGHEST = lax.Precision.HIGHEST


def to_native(tile):
    kv, rows, lons = tile.shape[0] * tile.shape[1], tile.shape[2], tile.shape[3]
    return tile.reshape(kv, rows, lons // LANES, LANES).swapaxes(1, 2).reshape(-1, LANES)


def from_native(flat, shape):
    kv, rows, lons = shape[0] * shape[1], shape[2], shape[3]
    return flat.reshape(kv, lons // LANES, rows, LANES).swapaxes(1, 2).reshape(shape)


def native_rows(ref, base, row, rows, tiles, half):
    parts = [
        ref[pl.ds(base + (half * 8 * tiles + tile) * rows + row, 8, stride=tiles * rows), :]
        for tile in range(tiles)
    ]
    return jnp.concatenate(parts, axis=1)


def lane_low(shape):
    return lax.broadcasted_iota(jnp.int32, shape, 1) < LANES // 2


def lateral_rows(rows, coef, reach):
    for step in range(reach):
        after = []
        for i in range(1, len(rows) - 1):
            at = step + i
            u = rows[i]
            width = u.shape[1]
            after.append(
                coef[0, at : at + 1, :] * u
                + coef[1, at : at + 1, :] * rows[i + 1]
                + coef[2, at : at + 1, :] * rows[i - 1]
                + coef[3, at : at + 1, :] * pltpu.roll(u, width - 1, 1)
                + coef[4, at : at + 1, :] * pltpu.roll(u, 1, 1)
            )
        rows = after
    return rows


def sort_halo(flags_ref, pair_ref, cross_ref, low_ref, high_ref):
    odd = flags_ref[1] == 1

    @pl.when(odd)
    def _():
        low_ref[...] = pair_ref[...]
        high_ref[...] = cross_ref[...]

    @pl.when(jnp.logical_not(odd))
    def _():
        low_ref[...] = cross_ref[...]
        high_ref[...] = pair_ref[...]

    @pl.when(flags_ref[2] == 1)
    def _():
        low_ref[...] = jnp.zeros_like(low_ref)

    @pl.when(flags_ref[3] == 1)
    def _():
        high_ref[...] = jnp.zeros_like(high_ref)


def first_lateral_kernel(kv, rows, tiles, count, flags_ref, own_ref, pair_ref, cross_ref, *refs):
    blocks, (packed_ref, coef_ref, held_ref, ext_ref, low_ref, high_ref) = refs[:count], refs[count:]
    lons = tiles * LANES
    cells = kv * tiles * rows
    for at, block in enumerate(blocks):
        held_ref[at] = block[0]
    sort_halo(flags_ref, pair_ref, cross_ref, low_ref, high_ref)
    ext_ref[...] = jnp.zeros_like(ext_ref)
    for kind in range(3):
        for block, ref in enumerate((low_ref, own_ref, high_ref)):
            for tile in range(tiles):
                start = cells + (kind * tiles + tile) * rows
                ext_ref[kind, block * rows : (block + 1) * rows, tile * LANES : (tile + 1) * LANES] = ref[
                    start : start + rows, :
                ]
    total = ext_ref.shape[1]
    north, east, ocean = ext_ref[0], ext_ref[1], ext_ref[2]
    north_face = north * ocean * pltpu.roll(ocean, total - 1, 0)
    east_face = east * ocean * pltpu.roll(ocean, lons - 1, 1)
    south_face = pltpu.roll(north_face, 1, 0)
    west_face = pltpu.roll(east_face, 1, 1)
    coef_ref[0] = ocean - north_face - south_face - east_face - west_face
    coef_ref[1] = north_face
    coef_ref[2] = south_face
    coef_ref[3] = east_face
    coef_ref[4] = west_face
    low = lane_low((8, LANES))
    for half in range(kv // 8):
        grown = [
            native_rows(ref, 0, row, rows, tiles, half)
            for ref in (low_ref, own_ref, high_ref)
            for row in range(rows)
        ]
        done = lateral_rows(grown, coef_ref, rows)
        for pair in range(rows // 2):
            for tile in range(tiles):
                first = done[2 * pair][:, tile * LANES : (tile + 1) * LANES]
                second = done[2 * pair + 1][:, tile * LANES : (tile + 1) * LANES]
                at = pair * kv + half * 8
                packed_ref[2 * tile, at : at + 8, :] = jnp.where(
                    low, first, pltpu.roll(second, LANES // 2, 1)
                )
                packed_ref[2 * tile + 1, at : at + 8, :] = jnp.where(
                    low, pltpu.roll(first, LANES // 2, 1), second
                )


def second_lateral_kernel(
    kv,
    rows,
    tiles,
    flags_ref,
    own_ref,
    pair_ref,
    cross_ref,
    coef_ref,
    direction_ref,
    residual_ref,
    image_ref,
    sums_ref,
    low_ref,
    high_ref,
):
    sort_halo(flags_ref, pair_ref, cross_ref, low_ref, high_ref)
    low = lane_low((8, LANES))
    totals = [jnp.zeros((8, tiles * LANES), jnp.float32) for _ in range(4)]
    for half in range(kv // 8):
        grown = []
        for ref in (low_ref, own_ref, high_ref):
            for pair in range(rows // 2):
                firsts, seconds = [], []
                at = pair * kv + half * 8
                for tile in range(tiles):
                    even = ref[2 * tile, at : at + 8, :]
                    odd = ref[2 * tile + 1, at : at + 8, :]
                    firsts.append(jnp.where(low, even, pltpu.roll(odd, LANES // 2, 1)))
                    seconds.append(jnp.where(low, pltpu.roll(even, LANES // 2, 1), odd))
                grown.append(jnp.concatenate(firsts, axis=1))
                grown.append(jnp.concatenate(seconds, axis=1))
        done = lateral_rows(grown, coef_ref, rows)
        for row in range(rows):
            direction = native_rows(direction_ref, 0, row, rows, tiles, half)
            residual = native_rows(residual_ref, 0, row, rows, tiles, half)
            image = direction + done[row]
            for tile in range(tiles):
                image_ref[pl.ds((half * 8 * tiles + tile) * rows + row, 8, stride=tiles * rows), :] = image[
                    :, tile * LANES : (tile + 1) * LANES
                ]
            totals[0] = totals[0] + residual * residual
            totals[1] = totals[1] + direction * image
            totals[2] = totals[2] + residual * image
            totals[3] = totals[3] + image * image
    lane = lax.broadcasted_iota(jnp.int32, (1, LANES), 1)
    line = jnp.zeros((1, LANES), jnp.float32)
    for at, total in enumerate(totals):
        line = jnp.where(lane == at, jnp.sum(total), line)
    for device in range(sums_ref.shape[0]):
        sums_ref[device] = line


def update_kernel(sums_ref, direction_ref, solution_ref, residual_ref, image_ref, sol_ref, res_ref, dir_ref):
    line = jnp.sum(sums_ref[...], axis=0)
    lane = lax.broadcasted_iota(jnp.int32, line.shape, 1)

    def pick(at):
        return jnp.sum(jnp.where(lane == at, line, 0.0), axis=1, keepdims=True)

    norm_now, curvature, cross, square = pick(0), pick(1), pick(2), pick(3)
    alpha = norm_now / curvature
    norm_next = norm_now - 2.0 * alpha * cross + alpha * alpha * square
    beta = norm_next / norm_now
    direction = direction_ref[...]
    residual_next = residual_ref[...] - alpha * image_ref[...]
    sol_ref[...] = solution_ref[...] + alpha * direction
    res_ref[...] = residual_next
    dir_ref[...] = residual_next + beta * direction


def prepare_kernel(
    devices, capacity, lon_cols, flags_ref, vert_ref, owner_ref, row_ref, col_ref, frac_ref, factor_ref, interp_ref
):
    layers = vert_ref.shape[0]
    top = lax.broadcasted_iota(jnp.int32, (8, LANES), 0) < 4
    coef = [
        jnp.where(top, vert_ref[layer, 0:1, :], vert_ref[layer, 1:2, :]) for layer in range(layers)
    ]
    ratio = None
    for layer in range(layers):
        diagonal = 1.0 + coef[layer]
        if layer > 0:
            diagonal = diagonal + coef[layer - 1] - coef[layer - 1] * ratio
        inverse = 1.0 / diagonal
        ratio = coef[layer] * inverse
        factor_ref[0, layer] = inverse
        factor_ref[1, layer] = coef[layer - 1] * inverse if layer > 0 else jnp.zeros_like(inverse)
        factor_ref[2, layer] = ratio
    count = owner_ref.shape[1]
    slots = devices * capacity
    apart = jnp.bitwise_xor(owner_ref[...], flags_ref[0])
    place = jnp.bitwise_and(apart, 1) * (devices // 2) + jnp.right_shift(apart, 1)
    named = jnp.where(
        lax.broadcasted_iota(jnp.int32, (devices, count), 0) == place, 1.0, 0.0
    )
    before = jnp.where(
        lax.broadcasted_iota(jnp.int32, (count, count), 0)
        <= lax.broadcasted_iota(jnp.int32, (count, count), 1),
        1.0,
        0.0,
    )
    running = jnp.dot(named, before, preferred_element_type=jnp.float32)
    rank = jnp.sum(named * running, axis=0, keepdims=True) - 1.0
    slot = place * capacity + rank.astype(jnp.int32)
    chosen = jnp.where(
        lax.broadcasted_iota(jnp.int32, (slots, count), 0) == slot, 1.0, 0.0
    )
    lat_frac = frac_ref[0:1, :]
    lon_frac = frac_ref[1:2, :]
    cell = (row_ref[...] * lon_cols + col_ref[...]).astype(jnp.float32)
    values = jnp.concatenate(
        [
            (1.0 - lat_frac) * (1.0 - lon_frac),
            (1.0 - lat_frac) * lon_frac,
            lat_frac * (1.0 - lon_frac),
            lat_frac * lon_frac,
            cell,
            jnp.zeros((3, count), jnp.float32),
        ],
        axis=0,
    )
    placed = lax.dot_general(
        values, chosen, (((1,), (1,)), ((), ())), precision=HIGHEST, preferred_element_type=jnp.float32
    )
    first = jnp.round(placed[4:5, :]).astype(jnp.int32)
    index = lax.broadcasted_iota(jnp.int32, interp_ref.shape, 0)
    away = index - first
    interp_ref[...] = jnp.where(
        away == 0,
        placed[0:1, :],
        jnp.where(
            away == 1,
            placed[1:2, :],
            jnp.where(away == lon_cols, placed[2:3, :], jnp.where(away == lon_cols + 1, placed[3:4, :], 0.0)),
        ),
    )


def solve_columns(read, write, factor_ref, layers):
    forward = []
    for layer in range(layers):
        value = read(layer) * factor_ref[0, layer]
        if layer > 0:
            value = value + factor_ref[1, layer] * forward[-1]
        forward.append(value)
    value = forward[-1]
    write(layers - 1, value)
    for layer in range(layers - 2, -1, -1):
        value = forward[layer] + factor_ref[2, layer] * value
        write(layer, value)


def observe_kernel(
    layers, held, capacity, packed_ref, factor_ref, interp_ref, near_ref, far_ref, out_ref, column_ref
):
    kv = near_ref.shape[1]
    block = 8 * held

    def packed_at(layer):
        return pl.ds((layer // held) * block + layer % held, 8, stride=held)

    def column_at(layer):
        return pl.ds(layer, 8, stride=layers)

    def read_packed(layer):
        return packed_ref[packed_at(layer), :]

    def write_column(layer, value):
        column_ref[column_at(layer), :] = value

    solve_columns(read_packed, write_column, factor_ref, layers)
    columns = jnp.concatenate([column_ref[0:kv, :], column_ref[kv : 2 * kv, :]], axis=1)
    interp = interp_ref[...]
    profile = jnp.dot(columns, interp, precision=HIGHEST, preferred_element_type=jnp.float32)
    owners = LANES // capacity
    mine = lax.broadcasted_iota(jnp.int32, (kv, LANES), 1) // capacity
    near = near_ref.shape[0]
    parts = []
    for tile in range(profile.shape[1] // LANES):
        values = profile[:, tile * LANES : (tile + 1) * LANES]
        first = tile * owners
        ref, at = (near_ref, first) if first < near else (far_ref, first - near)
        matrices = ref[at : at + owners].reshape(owners * kv, kv)
        product = jnp.dot(matrices, values, precision=HIGHEST, preferred_element_type=jnp.float32)
        kept = product[0:kv]
        for owner in range(1, owners):
            kept = jnp.where(mine == owner, product[owner * kv : (owner + 1) * kv], kept)
        parts.append(kept)
    weighted = jnp.concatenate(parts, axis=1)
    spread = lax.dot_general(
        weighted, interp, (((1,), (1,)), ((), ())), precision=HIGHEST, preferred_element_type=jnp.float32
    )
    column_ref[0:kv, :] = spread[:, :LANES]
    column_ref[kv : 2 * kv, :] = spread[:, LANES:]

    def read_column(layer):
        return column_ref[column_at(layer), :]

    def write_packed(layer, value):
        out_ref[packed_at(layer), :] = value

    solve_columns(read_column, write_packed, factor_ref, layers)


def vmem(count):
    return [pl.BlockSpec(memory_space=pltpu.VMEM)] * count


def call(kernel, out_shape, inputs, scratch=(), smem_first=False, flops=1_000_000, mib=8):
    specs = vmem(len(inputs))
    if smem_first:
        specs[0] = pl.BlockSpec(memory_space=pltpu.SMEM)
    moved = sum(math.prod(x.shape) * 4 for x in inputs)
    return pl.pallas_call(
        kernel,
        out_shape=out_shape,
        in_specs=specs,
        out_specs=tuple(vmem(len(out_shape))) if isinstance(out_shape, tuple) else vmem(1)[0],
        scratch_shapes=list(scratch),
        compiler_params=pltpu.CompilerParams(vmem_limit_bytes=mib * 1024 * 1024),
        cost_estimate=pl.CostEstimate(flops=flops, bytes_accessed=moved, transcendentals=0),
    )(*inputs)


def f32(*shape):
    return jax.ShapeDtypeStruct(shape, jnp.float32)


def from_neighbours(block):
    count = lax.axis_size("gy")
    pair = lax.ppermute(block, "gy", [(i, i ^ 1) for i in range(count)])
    cross = lax.ppermute(block, "gy", [(i, (i + (1 if i % 2 else -1)) % count) for i in range(count)])
    return pair, cross


def apart_by(block, axis, stride):
    return lax.ppermute(block, axis, [(i, i ^ stride) for i in range(lax.axis_size(axis))])


def per_device_gathered(
    direction,
    solution,
    residual,
    north_coef,
    east_coef,
    ocean,
    vert_coef,
    obs_owner,
    obs_row,
    obs_col,
    obs_frac,
    error_inverse,
):
    var_count, held, rows, lons = direction.shape
    kv = var_count * held
    tiles = lons // LANES
    layers, _, lon_cols = vert_coef.shape
    rows_y, cols_x = lax.axis_size("gy"), lax.axis_size("gx")
    device_count = rows_y * cols_x
    obs_count = obs_row.shape[-1]
    capacity = 2 * obs_count // device_count
    wide = error_inverse.shape[-1]
    cells = rows * lon_cols

    at_y, at_x = lax.axis_index("gy"), lax.axis_index("gx")
    flags = jnp.stack([at_y * cols_x + at_x, at_y % 2, at_y == 0, at_y == rows_y - 1]).astype(jnp.int32)
    direction_n = to_native(direction)
    residual_n = to_native(residual)
    solution_n = to_native(solution)
    lateral = jnp.stack([north_coef, east_coef, ocean.astype(jnp.float32)])[:, None]
    own = jnp.concatenate([direction_n, to_native(lateral)], axis=0)
    pair, cross = from_neighbours(own)

    matrix = error_inverse.reshape(1, wide, wide)
    blocks = [matrix] + [apart_by(matrix, "gx", stride) for stride in range(2, cols_x, 2)]
    factors, interp = call(
        functools.partial(prepare_kernel, device_count, capacity, lon_cols),
        (f32(3, layers, 8, LANES), f32(cells, device_count * capacity)),
        (
            flags,
            vert_coef.reshape(layers, cells // LANES, LANES),
            obs_owner.reshape(1, obs_count),
            obs_row.reshape(1, obs_count),
            obs_col.reshape(1, obs_count),
            obs_frac.reshape(2, obs_count),
        ),
        smem_first=True,
        flops=20_000_000,
        mib=16,
    )

    extended = 3 * rows + (-3 * rows) % 8
    packed, coef, held_blocks = call(
        functools.partial(first_lateral_kernel, kv, rows, tiles, len(blocks)),
        (f32(cols_x, 2 * kv, LANES), f32(5, extended, lons), f32(len(blocks), wide, wide)),
        (flags, own, pair, cross, *blocks),
        scratch=(
            pltpu.VMEM((3, extended, lons), jnp.float32),
            pltpu.VMEM(own.shape, jnp.float32),
            pltpu.VMEM(own.shape, jnp.float32),
        ),
        smem_first=True,
        flops=4_000_000,
    )
    near = jnp.concatenate(
        [held_blocks] + [apart_by(held_blocks, "gy", stride) for stride in range(1, rows_y)], axis=0
    )
    far = apart_by(near, "gx", 1)
    columns = lax.all_to_all(packed, "gx", split_axis=0, concat_axis=0, tiled=True)
    spread = call(
        functools.partial(observe_kernel, layers, held, capacity),
        f32(cols_x * 2 * kv, LANES),
        (columns.reshape(cols_x * 2 * kv, LANES), factors, interp, near, far),
        scratch=(pltpu.VMEM((2 * wide, LANES), jnp.float32),),
        flops=1_000_000_000,
        mib=16,
    )
    tile = lax.all_to_all(
        spread.reshape(cols_x, 2 * kv, LANES), "gx", split_axis=0, concat_axis=0, tiled=True
    )
    pair, cross = from_neighbours(tile)
    image, sums = call(
        functools.partial(second_lateral_kernel, kv, rows, tiles),
        (f32(*direction_n.shape), f32(device_count, 1, LANES)),
        (flags, tile, pair, cross, coef, direction_n, residual_n),
        scratch=(pltpu.VMEM(tile.shape, jnp.float32), pltpu.VMEM(tile.shape, jnp.float32)),
        smem_first=True,
        flops=4_000_000,
    )
    sums = lax.all_to_all(sums, ("gy", "gx"), split_axis=0, concat_axis=0, tiled=True)
    after = call(
        update_kernel,
        (f32(*direction_n.shape),) * 3,
        (sums, direction_n, solution_n, residual_n, image),
    )
    return tuple(from_native(x, direction.shape) for x in after)


def gathers(mesh, shapes):
    rows_y, cols_x = mesh.shape["gy"], mesh.shape["gx"]
    devices = rows_y * cols_x
    if any(size < 2 or size & (size - 1) for size in (rows_y, cols_x)):
        return False
    direction, vert_coef, obs_row, error_inverse = shapes
    var_count, layers, lat_rows, lons = direction
    rows, held = lat_rows // rows_y, layers // cols_x
    obs_count, wide = obs_row[-1], error_inverse[-1]
    capacity = 2 * obs_count // devices
    return (
        rows == NSTEP == 4
        and var_count == 4
        and (var_count * held) % 8 == 0
        and lons // cols_x * 2 == LANES
        and wide == LANES
        and capacity > 0
        and LANES % capacity == 0
        and devices // 2 % (LANES // capacity) == 0
        and devices * wide * wide * 4 <= 8 * 1024 * 1024
    )


def padded(cells, sides, width):
    for axis, dim in sides:
        count = lax.axis_size(axis)
        ends = count - 1
        head = lax.slice_in_dim(cells, 0, width, axis=dim)
        tail = lax.slice_in_dim(cells, cells.shape[dim] - width, cells.shape[dim], axis=dim)
        cells = jnp.concatenate(
            [
                lax.ppermute(tail, axis, [(i, (i + 1) % count) for i in range(ends)]),
                cells,
                lax.ppermute(head, axis, [((i + 1) % count, i) for i in range(ends)]),
            ],
            axis=dim,
        )
    return cells


def lateral_faces(north_ext, east_ext, ocean_ext):
    ocean_next = jnp.concatenate([ocean_ext[1:], jnp.zeros_like(ocean_ext[:1])], axis=0)
    north_face = north_ext * ocean_ext * ocean_next
    east_face = east_ext * ocean_ext * jnp.roll(ocean_ext, -1, axis=1)
    return (north_face, east_face, ocean_ext)


def diffuse_once(values_grid, north_face, east_face, ocean_ext):
    north_flux = north_face[:-1] * (values_grid[:, :, 1:, :] - values_grid[:, :, :-1, :])
    east_flux = east_face * (jnp.roll(values_grid, -1, axis=3) - values_grid)
    lateral = east_flux - jnp.roll(east_flux, 1, axis=3)
    return (
        ocean_ext[1:-1] * values_grid[:, :, 1:-1, :]
        + north_flux[:, :, 1:, :]
        - north_flux[:, :, :-1, :]
        + lateral[:, :, 1:-1, :]
    )


def lateral_pass(values_tile, faces):
    north_face, east_face, ocean_ext = faces
    grown = padded(values_tile, (("gy", 2),), NSTEP)
    total_rows = grown.shape[2]
    for step_index in range(NSTEP):
        upper = total_rows - step_index
        grown = diffuse_once(
            grown,
            north_face[step_index:upper],
            east_face[step_index:upper],
            ocean_ext[step_index:upper],
        )
    return grown


def vertical_factors(vert_coef):
    inverse_rows = []
    upper_ratio = []
    for layer_index in range(vert_coef.shape[0]):
        diagonal = 1.0 + vert_coef[layer_index]
        if layer_index > 0:
            diagonal = (
                diagonal + vert_coef[layer_index - 1] + vert_coef[layer_index - 1] * upper_ratio[-1]
            )
        inverse = 1.0 / diagonal
        inverse_rows.append(inverse)
        upper_ratio.append(-vert_coef[layer_index] * inverse)
    return (inverse_rows, upper_ratio)


def vertical_solve(values_col, vert_coef, factors):
    inverse_rows, upper_ratio = factors
    layers = values_col.shape[1]
    forward = []
    for layer_index in range(layers):
        source = values_col[:, layer_index]
        if layer_index > 0:
            source = source + vert_coef[layer_index - 1] * forward[-1]
        forward.append(source * inverse_rows[layer_index])
    result = [forward[-1]]
    for layer_index in range(layers - 2, -1, -1):
        result.append(forward[layer_index] - upper_ratio[layer_index] * result[-1])
    return jnp.stack(result[::-1], axis=1)


def observe_weigh_spread(columns, obs_owner, obs_row, obs_col, obs_frac, error_inverse):
    var_count, lev_count, lat_rows, lon_cols = columns.shape
    kv_width = var_count * lev_count
    rows_y = lax.axis_size("gy")
    cols_x = lax.axis_size("gx")
    device_count = rows_y * cols_x
    obs_count = obs_row.shape[-1]
    capacity = 2 * obs_count // device_count
    flat = columns.reshape(kv_width, lat_rows * lon_cols)
    cell = obs_row.reshape(-1) * lon_cols + obs_col.reshape(-1)
    corners = (cell, cell + 1, cell + lon_cols, cell + lon_cols + 1)
    lat_frac = obs_frac[0, 0, 0]
    lon_frac = obs_frac[0, 0, 1]
    weights = (
        (1.0 - lat_frac) * (1.0 - lon_frac),
        (1.0 - lat_frac) * lon_frac,
        lat_frac * (1.0 - lon_frac),
        lat_frac * lon_frac,
    )
    profile = weights[0] * jnp.take(flat, corners[0], axis=1)
    for corner_index in range(1, 4):
        profile = profile + weights[corner_index] * jnp.take(flat, corners[corner_index], axis=1)
    owners = obs_owner.reshape(-1)
    onehot = (owners[:, None] == jnp.arange(device_count, dtype=jnp.int32)[None, :]).astype(
        jnp.int32
    )
    running = jnp.cumsum(onehot, axis=0)
    rank_in = jnp.sum(running * onehot, axis=1) - 1
    slot = owners * capacity + rank_in
    outgoing = jnp.zeros((device_count * capacity, kv_width), jnp.float32).at[slot].set(profile.T)
    outgoing = outgoing.reshape(rows_y, cols_x, capacity, kv_width)
    matrix = error_inverse.reshape(kv_width, kv_width)
    arrived = lax.all_to_all(
        lax.all_to_all(outgoing, "gy", split_axis=0, concat_axis=0, tiled=True),
        "gx",
        split_axis=1,
        concat_axis=1,
        tiled=True,
    )
    weighted = jnp.dot(
        arrived.reshape(-1, kv_width),
        matrix,
        precision=lax.Precision.HIGHEST,
        preferred_element_type=jnp.float32,
    ).reshape(rows_y, cols_x, capacity, kv_width)
    returned = lax.all_to_all(
        lax.all_to_all(weighted, "gy", split_axis=0, concat_axis=0, tiled=True),
        "gx",
        split_axis=1,
        concat_axis=1,
        tiled=True,
    )
    back = returned.reshape(device_count * capacity, kv_width)[slot].T
    spread = jnp.zeros((kv_width, lat_rows * lon_cols), jnp.float32)
    for corner_index in range(4):
        spread = spread.at[:, corners[corner_index]].add(weights[corner_index] * back)
    return spread.reshape(var_count, lev_count, lat_rows, lon_cols)


def per_device(
    direction,
    solution,
    residual,
    north_coef,
    east_coef,
    ocean,
    vert_coef,
    obs_owner,
    obs_row,
    obs_col,
    obs_frac,
    error_inverse,
):
    stacked = jnp.stack([north_coef, east_coef, ocean.astype(jnp.float32)])
    reach = NSTEP
    grown_coef = padded(stacked, (("gy", 1),), reach)
    faces = lateral_faces(grown_coef[0], grown_coef[1], grown_coef[2])
    factors = vertical_factors(vert_coef)
    smoothed = lateral_pass(direction, faces)
    columns = lax.all_to_all(smoothed, "gx", split_axis=3, concat_axis=1, tiled=True)
    columns = vertical_solve(columns, vert_coef, factors)
    spread = observe_weigh_spread(columns, obs_owner, obs_row, obs_col, obs_frac, error_inverse)
    spread = vertical_solve(spread, vert_coef, factors)
    tiles = lax.all_to_all(spread, "gx", split_axis=1, concat_axis=3, tiled=True)
    image = direction + lateral_pass(tiles, faces)
    norm_now, curvature = lax.psum(
        (jnp.sum(residual * residual), jnp.sum(direction * image)), ("gy", "gx")
    )
    alpha = norm_now / curvature
    residual_next = residual - alpha * image
    norm_next = lax.psum(jnp.sum(residual_next * residual_next), ("gy", "gx"))
    solution_next = solution + alpha * direction
    direction_next = residual_next + norm_next / norm_now * direction
    return (solution_next, residual_next, direction_next)


def solution(mesh):
    in_specs = (
        P(None, "gx", "gy", None),
        P(None, "gx", "gy", None),
        P(None, "gx", "gy", None),
        P("gy", None),
        P("gy", None),
        P("gy", None),
        P(None, "gy", "gx"),
        P("gy", "gx", None, None),
        P("gy", "gx", None),
        P("gy", "gx", None),
        P("gy", "gx", None, None),
        P("gy", "gx", None, None),
    )
    out_specs = (P(None, "gx", "gy", None),) * 3

    def step(*arrays):
        shapes = [arrays[at].shape for at in (0, 6, 8, 11)]
        local = per_device_gathered if gathers(mesh, shapes) else per_device
        return jax.shard_map(
            local, mesh=mesh, in_specs=in_specs, out_specs=out_specs, check_vma=False
        )(*arrays)

    return step
```

```python
import functools
import math

import jax
import jax.numpy as jnp
from jax import lax
from jax.experimental import pallas as pl
from jax.experimental.pallas import tpu as pltpu
from jax.sharding import PartitionSpec as P

NSTEP = 4
LANES = 128
HIGHEST = lax.Precision.HIGHEST


def to_native(tile):
    kv, rows, lons = tile.shape[0] * tile.shape[1], tile.shape[2], tile.shape[3]
    return tile.reshape(kv, rows, lons // LANES, LANES).swapaxes(1, 2).reshape(-1, LANES)


def from_native(flat, shape):
    kv, rows, lons = shape[0] * shape[1], shape[2], shape[3]
    return flat.reshape(kv, lons // LANES, rows, LANES).swapaxes(1, 2).reshape(shape)


def native_rows(ref, base, row, rows, tiles, half):
    parts = [
        ref[pl.ds(base + (half * 8 * tiles + tile) * rows + row, 8, stride=tiles * rows), :]
        for tile in range(tiles)
    ]
    return jnp.concatenate(parts, axis=1)


def lane_low(shape):
    return lax.broadcasted_iota(jnp.int32, shape, 1) < LANES // 2


def lateral_rows(rows, coef, reach):
    for step in range(reach):
        after = []
        for i in range(1, len(rows) - 1):
            at = step + i
            u = rows[i]
            width = u.shape[1]
            after.append(
                coef[0, at : at + 1, :] * u
                + coef[1, at : at + 1, :] * rows[i + 1]
                + coef[2, at : at + 1, :] * rows[i - 1]
                + coef[3, at : at + 1, :] * pltpu.roll(u, width - 1, 1)
                + coef[4, at : at + 1, :] * pltpu.roll(u, 1, 1)
            )
        rows = after
    return rows


def sort_halo(pair_ref, cross_ref, low_ref, high_ref):
    at_y, rows_y = lax.axis_index("gy"), lax.axis_size("gy")
    odd = lax.rem(at_y, 2) == 1

    @pl.when(odd)
    def _():
        low_ref[...] = pair_ref[...]
        high_ref[...] = cross_ref[...]

    @pl.when(jnp.logical_not(odd))
    def _():
        low_ref[...] = cross_ref[...]
        high_ref[...] = pair_ref[...]

    @pl.when(at_y == 0)
    def _():
        low_ref[...] = jnp.zeros_like(low_ref)

    @pl.when(at_y == rows_y - 1)
    def _():
        high_ref[...] = jnp.zeros_like(high_ref)


def halo_kernel(direction_ref, north_ref, east_ref, ocean_ref, own_ref, mask_ref, sems):
    cells, size = direction_ref.shape[0], north_ref.shape[0]
    moves = (
        (ocean_ref, mask_ref),
        (direction_ref, own_ref.at[pl.ds(0, cells)]),
        (north_ref, own_ref.at[pl.ds(cells, size)]),
        (east_ref, own_ref.at[pl.ds(cells + size, size)]),
    )
    copies = [pltpu.make_async_copy(*move, sems.at[at]) for at, move in enumerate(moves)]
    for copy in copies:
        copy.start()
    for copy in copies:
        copy.wait()
    own_ref[cells + 2 * size : cells + 3 * size, :] = mask_ref[...].astype(jnp.float32)


def join_kernel(count, _, *refs):
    blocks, (near_ref,) = refs[:count], refs[count:]
    size = blocks[0].shape[0]
    for at, block in enumerate(blocks):
        near_ref[at * size : (at + 1) * size] = block[...]


def first_lateral_kernel(kv, rows, tiles, count, _, own_ref, pair_ref, cross_ref, *refs):
    blocks, (packed_ref, coef_ref, held_ref, ext_ref, low_ref, high_ref) = refs[:count], refs[count:]
    lons = tiles * LANES
    cells = kv * tiles * rows
    for at, block in enumerate(blocks):
        held_ref[at] = block[0]
    sort_halo(pair_ref, cross_ref, low_ref, high_ref)
    ext_ref[...] = jnp.zeros_like(ext_ref)
    for kind in range(3):
        for block, ref in enumerate((low_ref, own_ref, high_ref)):
            for tile in range(tiles):
                start = cells + (kind * tiles + tile) * rows
                ext_ref[kind, block * rows : (block + 1) * rows, tile * LANES : (tile + 1) * LANES] = ref[
                    start : start + rows, :
                ]
    total = ext_ref.shape[1]
    north, east, ocean = ext_ref[0], ext_ref[1], ext_ref[2]
    north_face = north * ocean * pltpu.roll(ocean, total - 1, 0)
    east_face = east * ocean * pltpu.roll(ocean, lons - 1, 1)
    south_face = pltpu.roll(north_face, 1, 0)
    west_face = pltpu.roll(east_face, 1, 1)
    coef_ref[0] = ocean - north_face - south_face - east_face - west_face
    coef_ref[1] = north_face
    coef_ref[2] = south_face
    coef_ref[3] = east_face
    coef_ref[4] = west_face
    low = lane_low((8, LANES))
    for half in range(kv // 8):
        grown = [
            native_rows(ref, 0, row, rows, tiles, half)
            for ref in (low_ref, own_ref, high_ref)
            for row in range(rows)
        ]
        done = lateral_rows(grown, coef_ref, rows)
        for pair in range(rows // 2):
            for tile in range(tiles):
                first = done[2 * pair][:, tile * LANES : (tile + 1) * LANES]
                second = done[2 * pair + 1][:, tile * LANES : (tile + 1) * LANES]
                at = pair * kv + half * 8
                packed_ref[2 * tile, at : at + 8, :] = jnp.where(
                    low, first, pltpu.roll(second, LANES // 2, 1)
                )
                packed_ref[2 * tile + 1, at : at + 8, :] = jnp.where(
                    low, pltpu.roll(first, LANES // 2, 1), second
                )


def second_lateral_kernel(
    kv,
    rows,
    tiles,
    own_ref,
    pair_ref,
    cross_ref,
    coef_ref,
    direction_ref,
    residual_ref,
    image_ref,
    sums_ref,
    low_ref,
    high_ref,
):
    sort_halo(pair_ref, cross_ref, low_ref, high_ref)
    low = lane_low((8, LANES))
    totals = [jnp.zeros((8, tiles * LANES), jnp.float32) for _ in range(4)]
    for half in range(kv // 8):
        grown = []
        for ref in (low_ref, own_ref, high_ref):
            for pair in range(rows // 2):
                firsts, seconds = [], []
                at = pair * kv + half * 8
                for tile in range(tiles):
                    even = ref[2 * tile, at : at + 8, :]
                    odd = ref[2 * tile + 1, at : at + 8, :]
                    firsts.append(jnp.where(low, even, pltpu.roll(odd, LANES // 2, 1)))
                    seconds.append(jnp.where(low, pltpu.roll(even, LANES // 2, 1), odd))
                grown.append(jnp.concatenate(firsts, axis=1))
                grown.append(jnp.concatenate(seconds, axis=1))
        done = lateral_rows(grown, coef_ref, rows)
        for row in range(rows):
            direction = native_rows(direction_ref, 0, row, rows, tiles, half)
            residual = native_rows(residual_ref, 0, row, rows, tiles, half)
            image = direction + done[row]
            for tile in range(tiles):
                image_ref[pl.ds((half * 8 * tiles + tile) * rows + row, 8, stride=tiles * rows), :] = image[
                    :, tile * LANES : (tile + 1) * LANES
                ]
            totals[0] = totals[0] + residual * residual
            totals[1] = totals[1] + direction * image
            totals[2] = totals[2] + residual * image
            totals[3] = totals[3] + image * image
    lane = lax.broadcasted_iota(jnp.int32, (1, LANES), 1)
    line = jnp.zeros((1, LANES), jnp.float32)
    for at, total in enumerate(totals):
        line = jnp.where(lane == at, jnp.sum(total), line)
    for device in range(sums_ref.shape[0]):
        sums_ref[device] = line


def update_kernel(sums_ref, direction_ref, solution_ref, residual_ref, image_ref, sol_ref, res_ref, dir_ref):
    line = jnp.sum(sums_ref[...], axis=0)
    lane = lax.broadcasted_iota(jnp.int32, line.shape, 1)

    def pick(at):
        return jnp.sum(jnp.where(lane == at, line, 0.0), axis=1, keepdims=True)

    norm_now, curvature, cross, square = pick(0), pick(1), pick(2), pick(3)
    alpha = norm_now / curvature
    norm_next = norm_now - 2.0 * alpha * cross + alpha * alpha * square
    beta = norm_next / norm_now
    direction = direction_ref[...]
    residual_next = residual_ref[...] - alpha * image_ref[...]
    sol_ref[...] = solution_ref[...] + alpha * direction
    res_ref[...] = residual_next
    dir_ref[...] = residual_next + beta * direction


def prepare_kernel(
    devices, capacity, lon_cols, vert_ref, owner_ref, row_ref, col_ref, frac_ref, factor_ref, interp_ref
):
    layers = vert_ref.shape[0]
    top = lax.broadcasted_iota(jnp.int32, (8, LANES), 0) < 4
    coef = [
        jnp.where(top, vert_ref[layer, 0:1, :], vert_ref[layer, 1:2, :]) for layer in range(layers)
    ]
    ratio = None
    for layer in range(layers):
        diagonal = 1.0 + coef[layer]
        if layer > 0:
            diagonal = diagonal + coef[layer - 1] - coef[layer - 1] * ratio
        inverse = 1.0 / diagonal
        ratio = coef[layer] * inverse
        factor_ref[0, layer] = inverse
        factor_ref[1, layer] = coef[layer - 1] * inverse if layer > 0 else jnp.zeros_like(inverse)
        factor_ref[2, layer] = ratio
    count = owner_ref.shape[1]
    slots = devices * capacity
    me = lax.axis_index("gy") * lax.axis_size("gx") + lax.axis_index("gx")
    apart = jnp.bitwise_xor(owner_ref[...], me)
    place = jnp.bitwise_and(apart, 1) * (devices // 2) + jnp.right_shift(apart, 1)
    named = jnp.where(
        lax.broadcasted_iota(jnp.int32, (devices, count), 0) == place, 1.0, 0.0
    )
    before = jnp.where(
        lax.broadcasted_iota(jnp.int32, (count, count), 0)
        <= lax.broadcasted_iota(jnp.int32, (count, count), 1),
        1.0,
        0.0,
    )
    running = jnp.dot(named, before, preferred_element_type=jnp.float32)
    rank = jnp.sum(named * running, axis=0, keepdims=True) - 1.0
    slot = place * capacity + rank.astype(jnp.int32)
    chosen = jnp.where(
        lax.broadcasted_iota(jnp.int32, (slots, count), 0) == slot, 1.0, 0.0
    )
    lat_frac = frac_ref[0:1, :]
    lon_frac = frac_ref[1:2, :]
    cell = (row_ref[...] * lon_cols + col_ref[...]).astype(jnp.float32)
    values = jnp.concatenate(
        [
            (1.0 - lat_frac) * (1.0 - lon_frac),
            (1.0 - lat_frac) * lon_frac,
            lat_frac * (1.0 - lon_frac),
            lat_frac * lon_frac,
            cell,
            jnp.zeros((3, count), jnp.float32),
        ],
        axis=0,
    )
    placed = lax.dot_general(
        values, chosen, (((1,), (1,)), ((), ())), precision=HIGHEST, preferred_element_type=jnp.float32
    )
    first = jnp.round(placed[4:5, :]).astype(jnp.int32)
    index = lax.broadcasted_iota(jnp.int32, interp_ref.shape, 0)
    away = index - first
    interp_ref[...] = jnp.where(
        away == 0,
        placed[0:1, :],
        jnp.where(
            away == 1,
            placed[1:2, :],
            jnp.where(away == lon_cols, placed[2:3, :], jnp.where(away == lon_cols + 1, placed[3:4, :], 0.0)),
        ),
    )


def solve_columns(read, write, factor_ref, layers):
    forward = []
    for layer in range(layers):
        value = read(layer) * factor_ref[0, layer]
        if layer > 0:
            value = value + factor_ref[1, layer] * forward[-1]
        forward.append(value)
    value = forward[-1]
    write(layers - 1, value)
    for layer in range(layers - 2, -1, -1):
        value = forward[layer] + factor_ref[2, layer] * value
        write(layer, value)


def packed_at(layer, held):
    return pl.ds((layer // held) * 8 * held + layer % held, 8, stride=held)


def profile_kernel(layers, held, packed_ref, factor_ref, interp_ref, profile_ref, column_ref):
    kv = profile_ref.shape[0]

    def read(layer):
        return packed_ref[packed_at(layer, held), :]

    def write(layer, value):
        column_ref[pl.ds(layer, 8, stride=layers), :] = value

    solve_columns(read, write, factor_ref, layers)
    columns = jnp.concatenate([column_ref[0:kv, :], column_ref[kv : 2 * kv, :]], axis=1)
    profile_ref[...] = jnp.dot(
        columns, interp_ref[...], precision=HIGHEST, preferred_element_type=jnp.float32
    )


def spread_kernel(
    layers, held, capacity, profile_ref, factor_ref, interp_ref, near_ref, far_ref, out_ref, column_ref
):
    kv = near_ref.shape[1]
    owners = LANES // capacity
    mine = lax.broadcasted_iota(jnp.int32, (kv, LANES), 1) // capacity
    near = near_ref.shape[0]
    parts = []
    for tile in range(profile_ref.shape[1] // LANES):
        values = profile_ref[:, tile * LANES : (tile + 1) * LANES]
        first = tile * owners
        ref, at = (near_ref, first) if first < near else (far_ref, first - near)
        matrices = ref[at : at + owners].reshape(owners * kv, kv)
        product = jnp.dot(matrices, values, precision=HIGHEST, preferred_element_type=jnp.float32)
        kept = product[0:kv]
        for owner in range(1, owners):
            kept = jnp.where(mine == owner, product[owner * kv : (owner + 1) * kv], kept)
        parts.append(kept)
    spread = lax.dot_general(
        jnp.concatenate(parts, axis=1),
        interp_ref[...],
        (((1,), (1,)), ((), ())),
        precision=HIGHEST,
        preferred_element_type=jnp.float32,
    )
    column_ref[0:kv, :] = spread[:, :LANES]
    column_ref[kv : 2 * kv, :] = spread[:, LANES:]

    def read(layer):
        return column_ref[pl.ds(layer, 8, stride=layers), :]

    def write(layer, value):
        out_ref[packed_at(layer, held), :] = value

    solve_columns(read, write, factor_ref, layers)


def vmem(count):
    return [pl.BlockSpec(memory_space=pltpu.VMEM)] * count


def call(kernel, out_shape, inputs, scratch=(), after=False, hbm=False, flops=1_000_000, mib=8):
    specs = vmem(len(inputs))
    if after:
        specs[0] = pl.BlockSpec(memory_space=pl.ANY)
    if hbm:
        specs = [pl.BlockSpec(memory_space=pltpu.HBM)] * len(inputs)
    moved = sum(math.prod(x.shape) * 4 for x in inputs)
    return pl.pallas_call(
        kernel,
        out_shape=out_shape,
        in_specs=specs,
        out_specs=tuple(vmem(len(out_shape))) if isinstance(out_shape, tuple) else vmem(1)[0],
        scratch_shapes=list(scratch),
        compiler_params=pltpu.CompilerParams(vmem_limit_bytes=mib * 1024 * 1024),
        cost_estimate=pl.CostEstimate(flops=flops, bytes_accessed=moved, transcendentals=0),
    )(*inputs)


def f32(*shape):
    return jax.ShapeDtypeStruct(shape, jnp.float32)


def from_neighbours(block):
    count = lax.axis_size("gy")
    pair = lax.ppermute(block, "gy", [(i, i ^ 1) for i in range(count)])
    cross = lax.ppermute(block, "gy", [(i, (i + (1 if i % 2 else -1)) % count) for i in range(count)])
    return pair, cross


def apart_by(block, axis, stride):
    return lax.ppermute(block, axis, [(i, i ^ stride) for i in range(lax.axis_size(axis))])


def per_device_gathered(
    direction,
    solution,
    residual,
    north_coef,
    east_coef,
    ocean,
    vert_coef,
    obs_owner,
    obs_row,
    obs_col,
    obs_frac,
    error_inverse,
):
    var_count, held, rows, lons = direction.shape
    kv = var_count * held
    tiles = lons // LANES
    layers, _, lon_cols = vert_coef.shape
    rows_y, cols_x = lax.axis_size("gy"), lax.axis_size("gx")
    device_count = rows_y * cols_x
    obs_count = obs_row.shape[-1]
    capacity = 2 * obs_count // device_count
    wide = error_inverse.shape[-1]
    cells = rows * lon_cols

    direction_n = to_native(direction)
    residual_n = to_native(residual)
    solution_n = to_native(solution)
    faces = [to_native(x[None, None]) for x in (north_coef, east_coef, ocean)]
    own = call(
        halo_kernel,
        f32(direction_n.shape[0] + 3 * faces[0].shape[0], LANES),
        (direction_n, *faces),
        scratch=(pltpu.VMEM(faces[0].shape, jnp.int32), pltpu.SemaphoreType.DMA((4,))),
        hbm=True,
    )
    pair, cross = from_neighbours(own)

    matrix = error_inverse.reshape(1, wide, wide)
    blocks = [matrix] + [apart_by(matrix, "gx", stride) for stride in range(2, cols_x, 2)]
    factors, interp = call(
        functools.partial(prepare_kernel, device_count, capacity, lon_cols),
        (f32(3, layers, 8, LANES), f32(cells, device_count * capacity)),
        (
            vert_coef.reshape(layers, cells // LANES, LANES),
            obs_owner.reshape(1, obs_count),
            obs_row.reshape(1, obs_count),
            obs_col.reshape(1, obs_count),
            obs_frac.reshape(2, obs_count),
        ),
        flops=20_000_000,
        mib=16,
    )

    extended = 3 * rows + (-3 * rows) % 8
    packed, coef, held_blocks = call(
        functools.partial(first_lateral_kernel, kv, rows, tiles, len(blocks)),
        (f32(cols_x, 2 * kv, LANES), f32(5, extended, lons), f32(len(blocks), wide, wide)),
        (factors, own, pair, cross, *blocks),
        scratch=(
            pltpu.VMEM((3, extended, lons), jnp.float32),
            pltpu.VMEM(own.shape, jnp.float32),
            pltpu.VMEM(own.shape, jnp.float32),
        ),
        after=True,
        flops=4_000_000,
    )
    fetched = [held_blocks] + [apart_by(held_blocks, "gy", stride) for stride in range(1, rows_y)]
    columns = lax.all_to_all(packed, "gx", split_axis=0, concat_axis=0, tiled=True)
    columns = columns.reshape(cols_x * 2 * kv, LANES)
    near = call(
        functools.partial(join_kernel, len(fetched)),
        f32(device_count // 2, wide, wide),
        (columns, *fetched),
        after=True,
    )
    far = apart_by(near, "gx", 1)
    profile = call(
        functools.partial(profile_kernel, layers, held),
        f32(wide, device_count * capacity),
        (columns, factors, interp),
        scratch=(pltpu.VMEM((2 * wide, LANES), jnp.float32),),
        flops=400_000_000,
        mib=16,
    )
    spread = call(
        functools.partial(spread_kernel, layers, held, capacity),
        f32(cols_x * 2 * kv, LANES),
        (profile, factors, interp, near, far),
        scratch=(pltpu.VMEM((2 * wide, LANES), jnp.float32),),
        flops=1_000_000_000,
        mib=16,
    )
    tile = lax.all_to_all(
        spread.reshape(cols_x, 2 * kv, LANES), "gx", split_axis=0, concat_axis=0, tiled=True
    )
    pair, cross = from_neighbours(tile)
    image, sums = call(
        functools.partial(second_lateral_kernel, kv, rows, tiles),
        (f32(*direction_n.shape), f32(device_count, 1, LANES)),
        (tile, pair, cross, coef, direction_n, residual_n),
        scratch=(pltpu.VMEM(tile.shape, jnp.float32), pltpu.VMEM(tile.shape, jnp.float32)),
        flops=4_000_000,
    )
    sums = lax.all_to_all(sums, ("gy", "gx"), split_axis=0, concat_axis=0, tiled=True)
    after = call(
        update_kernel,
        (f32(*direction_n.shape),) * 3,
        (sums, direction_n, solution_n, residual_n, image),
    )
    return tuple(from_native(x, direction.shape) for x in after)


def gathers(mesh, shapes):
    rows_y, cols_x = mesh.shape["gy"], mesh.shape["gx"]
    devices = rows_y * cols_x
    if any(size < 2 or size & (size - 1) for size in (rows_y, cols_x)):
        return False
    direction, vert_coef, obs_row, error_inverse = shapes
    var_count, layers, lat_rows, lons = direction
    rows, held = lat_rows // rows_y, layers // cols_x
    obs_count, wide = obs_row[-1], error_inverse[-1]
    capacity = 2 * obs_count // devices
    return (
        rows == NSTEP == 4
        and var_count == 4
        and (var_count * held) % 8 == 0
        and lons // cols_x * 2 == LANES
        and wide == LANES
        and capacity > 0
        and LANES % capacity == 0
        and devices // 2 % (LANES // capacity) == 0
        and devices * wide * wide * 4 <= 8 * 1024 * 1024
    )


def padded(cells, sides, width):
    for axis, dim in sides:
        count = lax.axis_size(axis)
        ends = count - 1
        head = lax.slice_in_dim(cells, 0, width, axis=dim)
        tail = lax.slice_in_dim(cells, cells.shape[dim] - width, cells.shape[dim], axis=dim)
        cells = jnp.concatenate(
            [
                lax.ppermute(tail, axis, [(i, (i + 1) % count) for i in range(ends)]),
                cells,
                lax.ppermute(head, axis, [((i + 1) % count, i) for i in range(ends)]),
            ],
            axis=dim,
        )
    return cells


def lateral_faces(north_ext, east_ext, ocean_ext):
    ocean_next = jnp.concatenate([ocean_ext[1:], jnp.zeros_like(ocean_ext[:1])], axis=0)
    north_face = north_ext * ocean_ext * ocean_next
    east_face = east_ext * ocean_ext * jnp.roll(ocean_ext, -1, axis=1)
    return (north_face, east_face, ocean_ext)


def diffuse_once(values_grid, north_face, east_face, ocean_ext):
    north_flux = north_face[:-1] * (values_grid[:, :, 1:, :] - values_grid[:, :, :-1, :])
    east_flux = east_face * (jnp.roll(values_grid, -1, axis=3) - values_grid)
    lateral = east_flux - jnp.roll(east_flux, 1, axis=3)
    return (
        ocean_ext[1:-1] * values_grid[:, :, 1:-1, :]
        + north_flux[:, :, 1:, :]
        - north_flux[:, :, :-1, :]
        + lateral[:, :, 1:-1, :]
    )


def lateral_pass(values_tile, faces):
    north_face, east_face, ocean_ext = faces
    grown = padded(values_tile, (("gy", 2),), NSTEP)
    total_rows = grown.shape[2]
    for step_index in range(NSTEP):
        upper = total_rows - step_index
        grown = diffuse_once(
            grown,
            north_face[step_index:upper],
            east_face[step_index:upper],
            ocean_ext[step_index:upper],
        )
    return grown


def vertical_factors(vert_coef):
    inverse_rows = []
    upper_ratio = []
    for layer_index in range(vert_coef.shape[0]):
        diagonal = 1.0 + vert_coef[layer_index]
        if layer_index > 0:
            diagonal = (
                diagonal + vert_coef[layer_index - 1] + vert_coef[layer_index - 1] * upper_ratio[-1]
            )
        inverse = 1.0 / diagonal
        inverse_rows.append(inverse)
        upper_ratio.append(-vert_coef[layer_index] * inverse)
    return (inverse_rows, upper_ratio)


def vertical_solve(values_col, vert_coef, factors):
    inverse_rows, upper_ratio = factors
    layers = values_col.shape[1]
    forward = []
    for layer_index in range(layers):
        source = values_col[:, layer_index]
        if layer_index > 0:
            source = source + vert_coef[layer_index - 1] * forward[-1]
        forward.append(source * inverse_rows[layer_index])
    result = [forward[-1]]
    for layer_index in range(layers - 2, -1, -1):
        result.append(forward[layer_index] - upper_ratio[layer_index] * result[-1])
    return jnp.stack(result[::-1], axis=1)


def observe_weigh_spread(columns, obs_owner, obs_row, obs_col, obs_frac, error_inverse):
    var_count, lev_count, lat_rows, lon_cols = columns.shape
    kv_width = var_count * lev_count
    rows_y = lax.axis_size("gy")
    cols_x = lax.axis_size("gx")
    device_count = rows_y * cols_x
    obs_count = obs_row.shape[-1]
    capacity = 2 * obs_count // device_count
    flat = columns.reshape(kv_width, lat_rows * lon_cols)
    cell = obs_row.reshape(-1) * lon_cols + obs_col.reshape(-1)
    corners = (cell, cell + 1, cell + lon_cols, cell + lon_cols + 1)
    lat_frac = obs_frac[0, 0, 0]
    lon_frac = obs_frac[0, 0, 1]
    weights = (
        (1.0 - lat_frac) * (1.0 - lon_frac),
        (1.0 - lat_frac) * lon_frac,
        lat_frac * (1.0 - lon_frac),
        lat_frac * lon_frac,
    )
    profile = weights[0] * jnp.take(flat, corners[0], axis=1)
    for corner_index in range(1, 4):
        profile = profile + weights[corner_index] * jnp.take(flat, corners[corner_index], axis=1)
    owners = obs_owner.reshape(-1)
    onehot = (owners[:, None] == jnp.arange(device_count, dtype=jnp.int32)[None, :]).astype(
        jnp.int32
    )
    running = jnp.cumsum(onehot, axis=0)
    rank_in = jnp.sum(running * onehot, axis=1) - 1
    slot = owners * capacity + rank_in
    outgoing = jnp.zeros((device_count * capacity, kv_width), jnp.float32).at[slot].set(profile.T)
    outgoing = outgoing.reshape(rows_y, cols_x, capacity, kv_width)
    matrix = error_inverse.reshape(kv_width, kv_width)
    arrived = lax.all_to_all(
        lax.all_to_all(outgoing, "gy", split_axis=0, concat_axis=0, tiled=True),
        "gx",
        split_axis=1,
        concat_axis=1,
        tiled=True,
    )
    weighted = jnp.dot(
        arrived.reshape(-1, kv_width),
        matrix,
        precision=lax.Precision.HIGHEST,
        preferred_element_type=jnp.float32,
    ).reshape(rows_y, cols_x, capacity, kv_width)
    returned = lax.all_to_all(
        lax.all_to_all(weighted, "gy", split_axis=0, concat_axis=0, tiled=True),
        "gx",
        split_axis=1,
        concat_axis=1,
        tiled=True,
    )
    back = returned.reshape(device_count * capacity, kv_width)[slot].T
    spread = jnp.zeros((kv_width, lat_rows * lon_cols), jnp.float32)
    for corner_index in range(4):
        spread = spread.at[:, corners[corner_index]].add(weights[corner_index] * back)
    return spread.reshape(var_count, lev_count, lat_rows, lon_cols)


def per_device(
    direction,
    solution,
    residual,
    north_coef,
    east_coef,
    ocean,
    vert_coef,
    obs_owner,
    obs_row,
    obs_col,
    obs_frac,
    error_inverse,
):
    stacked = jnp.stack([north_coef, east_coef, ocean.astype(jnp.float32)])
    reach = NSTEP
    grown_coef = padded(stacked, (("gy", 1),), reach)
    faces = lateral_faces(grown_coef[0], grown_coef[1], grown_coef[2])
    factors = vertical_factors(vert_coef)
    smoothed = lateral_pass(direction, faces)
    columns = lax.all_to_all(smoothed, "gx", split_axis=3, concat_axis=1, tiled=True)
    columns = vertical_solve(columns, vert_coef, factors)
    spread = observe_weigh_spread(columns, obs_owner, obs_row, obs_col, obs_frac, error_inverse)
    spread = vertical_solve(spread, vert_coef, factors)
    tiles = lax.all_to_all(spread, "gx", split_axis=1, concat_axis=3, tiled=True)
    image = direction + lateral_pass(tiles, faces)
    norm_now, curvature = lax.psum(
        (jnp.sum(residual * residual), jnp.sum(direction * image)), ("gy", "gx")
    )
    alpha = norm_now / curvature
    residual_next = residual - alpha * image
    norm_next = lax.psum(jnp.sum(residual_next * residual_next), ("gy", "gx"))
    solution_next = solution + alpha * direction
    direction_next = residual_next + norm_next / norm_now * direction
    return (solution_next, residual_next, direction_next)


def solution(mesh):
    in_specs = (
        P(None, "gx", "gy", None),
        P(None, "gx", "gy", None),
        P(None, "gx", "gy", None),
        P("gy", None),
        P("gy", None),
        P("gy", None),
        P(None, "gy", "gx"),
        P("gy", "gx", None, None),
        P("gy", "gx", None),
        P("gy", "gx", None),
        P("gy", "gx", None, None),
        P("gy", "gx", None, None),
    )
    out_specs = (P(None, "gx", "gy", None),) * 3

    def step(*arrays):
        shapes = [arrays[at].shape for at in (0, 6, 8, 11)]
        local = per_device_gathered if gathers(mesh, shapes) else per_device
        return jax.shard_map(
            local, mesh=mesh, in_specs=in_specs, out_specs=out_specs, check_vma=False
        )(*arrays)

    return step
```

```python
import functools
import math

import jax
import jax.numpy as jnp
from jax import lax
from jax.experimental import pallas as pl
from jax.experimental.pallas import tpu as pltpu
from jax.sharding import PartitionSpec as P

NSTEP = 4
LANES = 128


def to_native(tile):
    kv, rows, lons = tile.shape[0] * tile.shape[1], tile.shape[2], tile.shape[3]
    return tile.reshape(kv, rows, lons // LANES, LANES).swapaxes(1, 2).reshape(-1, LANES)


def from_native(flat, shape):
    kv, rows, lons = shape[0] * shape[1], shape[2], shape[3]
    return flat.reshape(kv, lons // LANES, rows, LANES).swapaxes(1, 2).reshape(shape)


def native_rows(ref, base, row, rows, tiles, half):
    parts = [
        ref[pl.ds(base + (half * 8 * tiles + tile) * rows + row, 8, stride=tiles * rows), :]
        for tile in range(tiles)
    ]
    return jnp.concatenate(parts, axis=1)


def lane_low(shape):
    return lax.broadcasted_iota(jnp.int32, shape, 1) < LANES // 2


def lateral_rows(rows, coef, reach):
    for step in range(reach):
        after = []
        for i in range(1, len(rows) - 1):
            at = step + i
            u = rows[i]
            width = u.shape[1]
            after.append(
                coef[0, at : at + 1, :] * u
                + coef[1, at : at + 1, :] * rows[i + 1]
                + coef[2, at : at + 1, :] * rows[i - 1]
                + coef[3, at : at + 1, :] * pltpu.roll(u, width - 1, 1)
                + coef[4, at : at + 1, :] * pltpu.roll(u, 1, 1)
            )
        rows = after
    return rows


def sort_halo(pair_ref, cross_ref, low_ref, high_ref):
    at_y, rows_y = lax.axis_index("gy"), lax.axis_size("gy")
    odd = lax.rem(at_y, 2) == 1

    @pl.when(odd)
    def _():
        low_ref[...] = pair_ref[...]
        high_ref[...] = cross_ref[...]

    @pl.when(jnp.logical_not(odd))
    def _():
        low_ref[...] = cross_ref[...]
        high_ref[...] = pair_ref[...]

    @pl.when(at_y == 0)
    def _():
        low_ref[...] = jnp.zeros_like(low_ref)

    @pl.when(at_y == rows_y - 1)
    def _():
        high_ref[...] = jnp.zeros_like(high_ref)


def halo_kernel(direction_ref, north_ref, east_ref, ocean_ref, own_ref, mask_ref, sems):
    cells, size = direction_ref.shape[0], north_ref.shape[0]
    moves = (
        (ocean_ref, mask_ref),
        (direction_ref, own_ref.at[pl.ds(0, cells)]),
        (north_ref, own_ref.at[pl.ds(cells, size)]),
        (east_ref, own_ref.at[pl.ds(cells + size, size)]),
    )
    copies = [pltpu.make_async_copy(*move, sems.at[at]) for at, move in enumerate(moves)]
    for copy in copies:
        copy.start()
    for copy in copies:
        copy.wait()
    own_ref[cells + 2 * size : cells + 3 * size, :] = mask_ref[...].astype(jnp.float32)


def join_kernel(count, _, __, *refs):
    blocks, (near_ref,) = refs[:count], refs[count:]
    size = blocks[0].shape[0]
    for at, block in enumerate(blocks):
        near_ref[at * size : (at + 1) * size] = block[...]


def first_lateral_kernel(
    kv, rows, tiles, count, own_ref, north_ref, east_ref, ocean_ref, pair_ref, cross_ref, *refs
):
    blocks, (packed_ref, coef_ref, held_ref, ext_ref, low_ref, high_ref) = refs[:count], refs[count:]
    lons = tiles * LANES
    cells = kv * tiles * rows
    for at, block in enumerate(blocks):
        held_ref[at] = block[0]
    sort_halo(pair_ref, cross_ref, low_ref, high_ref)
    ext_ref[...] = jnp.zeros_like(ext_ref)
    for kind, kept in enumerate((north_ref, east_ref, ocean_ref)):
        for tile in range(tiles):
            lanes = slice(tile * LANES, (tile + 1) * LANES)
            start = cells + (kind * tiles + tile) * rows
            ext_ref[kind, 0:rows, lanes] = low_ref[start : start + rows, :]
            ext_ref[kind, rows : 2 * rows, lanes] = kept[tile * rows : (tile + 1) * rows, :].astype(jnp.float32)
            ext_ref[kind, 2 * rows : 3 * rows, lanes] = high_ref[start : start + rows, :]
    total = ext_ref.shape[1]
    north, east, ocean = ext_ref[0], ext_ref[1], ext_ref[2]
    north_face = north * ocean * pltpu.roll(ocean, total - 1, 0)
    east_face = east * ocean * pltpu.roll(ocean, lons - 1, 1)
    south_face = pltpu.roll(north_face, 1, 0)
    west_face = pltpu.roll(east_face, 1, 1)
    coef_ref[0] = ocean - north_face - south_face - east_face - west_face
    coef_ref[1] = north_face
    coef_ref[2] = south_face
    coef_ref[3] = east_face
    coef_ref[4] = west_face
    low = lane_low((8, LANES))
    for half in range(kv // 8):
        grown = [
            native_rows(ref, 0, row, rows, tiles, half)
            for ref in (low_ref, own_ref, high_ref)
            for row in range(rows)
        ]
        done = lateral_rows(grown, coef_ref, rows)
        for pair in range(rows // 2):
            for tile in range(tiles):
                first = done[2 * pair][:, tile * LANES : (tile + 1) * LANES]
                second = done[2 * pair + 1][:, tile * LANES : (tile + 1) * LANES]
                at = pair * kv + half * 8
                packed_ref[2 * tile, at : at + 8, :] = jnp.where(
                    low, first, pltpu.roll(second, LANES // 2, 1)
                )
                packed_ref[2 * tile + 1, at : at + 8, :] = jnp.where(
                    low, pltpu.roll(first, LANES // 2, 1), second
                )


def second_lateral_kernel(
    kv,
    rows,
    tiles,
    own_ref,
    pair_ref,
    cross_ref,
    coef_ref,
    direction_ref,
    residual_ref,
    image_ref,
    sums_ref,
    low_ref,
    high_ref,
):
    sort_halo(pair_ref, cross_ref, low_ref, high_ref)
    low = lane_low((8, LANES))
    totals = [jnp.zeros((8, tiles * LANES), jnp.float32) for _ in range(4)]
    for half in range(kv // 8):
        grown = []
        for ref in (low_ref, own_ref, high_ref):
            for pair in range(rows // 2):
                firsts, seconds = [], []
                at = pair * kv + half * 8
                for tile in range(tiles):
                    even = ref[2 * tile, at : at + 8, :]
                    odd = ref[2 * tile + 1, at : at + 8, :]
                    firsts.append(jnp.where(low, even, pltpu.roll(odd, LANES // 2, 1)))
                    seconds.append(jnp.where(low, pltpu.roll(even, LANES // 2, 1), odd))
                grown.append(jnp.concatenate(firsts, axis=1))
                grown.append(jnp.concatenate(seconds, axis=1))
        done = lateral_rows(grown, coef_ref, rows)
        for row in range(rows):
            direction = native_rows(direction_ref, 0, row, rows, tiles, half)
            residual = native_rows(residual_ref, 0, row, rows, tiles, half)
            image = direction + done[row]
            for tile in range(tiles):
                image_ref[pl.ds((half * 8 * tiles + tile) * rows + row, 8, stride=tiles * rows), :] = image[
                    :, tile * LANES : (tile + 1) * LANES
                ]
            totals[0] = totals[0] + residual * residual
            totals[1] = totals[1] + direction * image
            totals[2] = totals[2] + residual * image
            totals[3] = totals[3] + image * image
    lane = lax.broadcasted_iota(jnp.int32, (1, LANES), 1)
    line = jnp.zeros((1, LANES), jnp.float32)
    for at, total in enumerate(totals):
        line = jnp.where(lane == at, jnp.sum(total), line)
    for device in range(sums_ref.shape[0]):
        sums_ref[device] = line


def update_kernel(sums_ref, direction_ref, solution_ref, residual_ref, image_ref, sol_ref, res_ref, dir_ref):
    line = jnp.sum(sums_ref[...], axis=0)
    lane = lax.broadcasted_iota(jnp.int32, line.shape, 1)

    def pick(at):
        return jnp.sum(jnp.where(lane == at, line, 0.0), axis=1, keepdims=True)

    norm_now, curvature, cross, square = pick(0), pick(1), pick(2), pick(3)
    alpha = norm_now / curvature
    norm_next = norm_now - 2.0 * alpha * cross + alpha * alpha * square
    beta = norm_next / norm_now
    direction = direction_ref[...]
    residual_next = residual_ref[...] - alpha * image_ref[...]
    sol_ref[...] = solution_ref[...] + alpha * direction
    res_ref[...] = residual_next
    dir_ref[...] = residual_next + beta * direction


def split(value):
    high = value.astype(jnp.bfloat16)
    return high, (value - high.astype(jnp.float32)).astype(jnp.bfloat16)


def dot_parts(left, right, contract):
    dims = (contract, ((), ()))
    total = lax.dot_general(left[0], right[0], dims, preferred_element_type=jnp.float32)
    total = total + lax.dot_general(left[0], right[1], dims, preferred_element_type=jnp.float32)
    return total + lax.dot_general(left[1], right[0], dims, preferred_element_type=jnp.float32)


def prepare_kernel(
    devices, capacity, lon_cols, _, owner_ref, row_ref, col_ref, frac_ref, high_ref, low_ref
):
    count = owner_ref.shape[1]
    slots = devices * capacity
    me = lax.axis_index("gy") * lax.axis_size("gx") + lax.axis_index("gx")
    apart = jnp.bitwise_xor(owner_ref[...], me)
    place = jnp.bitwise_and(apart, 1) * (devices // 2) + jnp.right_shift(apart, 1)
    named = lax.broadcasted_iota(jnp.int32, (devices, count), 0) == place
    before = lax.broadcasted_iota(jnp.int32, (count, count), 0) <= lax.broadcasted_iota(
        jnp.int32, (count, count), 1
    )
    running = jnp.dot(
        jnp.where(named, 1.0, 0.0).astype(jnp.bfloat16),
        jnp.where(before, 1.0, 0.0).astype(jnp.bfloat16),
        preferred_element_type=jnp.float32,
    )
    rank = jnp.sum(jnp.where(named, running, 0.0), axis=0, keepdims=True) - 1.0
    slot = place * capacity + rank.astype(jnp.int32)
    chosen = jnp.where(
        lax.broadcasted_iota(jnp.int32, (slots, count), 0) == slot, 1.0, 0.0
    ).astype(jnp.bfloat16)
    lat_frac = frac_ref[0:1, :]
    lon_frac = frac_ref[1:2, :]
    cell = (row_ref[...] * lon_cols + col_ref[...]).astype(jnp.float32)
    values = jnp.concatenate(
        [
            (1.0 - lat_frac) * (1.0 - lon_frac),
            (1.0 - lat_frac) * lon_frac,
            lat_frac * (1.0 - lon_frac),
            lat_frac * lon_frac,
            cell,
            jnp.zeros((3, count), jnp.float32),
        ],
        axis=0,
    )
    high, rest = split(values)
    low, rest = split(values - high.astype(jnp.float32))
    parts = jnp.concatenate([high.astype(jnp.float32), low.astype(jnp.float32), rest.astype(jnp.float32)], axis=0)
    placed = lax.dot_general(
        parts.astype(jnp.bfloat16), chosen, (((1,), (1,)), ((), ())), preferred_element_type=jnp.float32
    )
    placed = placed[0:8] + placed[8:16] + placed[16:24]
    first = jnp.round(placed[4:5, :]).astype(jnp.int32)
    away = lax.broadcasted_iota(jnp.int32, high_ref.shape, 0) - first
    interp = jnp.where(
        away == 0,
        placed[0:1, :],
        jnp.where(
            away == 1,
            placed[1:2, :],
            jnp.where(away == lon_cols, placed[2:3, :], jnp.where(away == lon_cols + 1, placed[3:4, :], 0.0)),
        ),
    )
    high_ref[...], low_ref[...] = split(interp)


def vertical_factors_kernel(vert_ref, factor_ref):
    layers = vert_ref.shape[0]
    top = lax.broadcasted_iota(jnp.int32, (8, LANES), 0) < 4
    coef = [jnp.where(top, vert_ref[layer, 0:1, :], vert_ref[layer, 1:2, :]) for layer in range(layers)]
    ratio = None
    for layer in range(layers):
        diagonal = 1.0 + coef[layer]
        if layer > 0:
            diagonal = diagonal + coef[layer - 1] - coef[layer - 1] * ratio
        inverse = 1.0 / diagonal
        ratio = coef[layer] * inverse
        factor_ref[0, layer] = inverse
        factor_ref[1, layer] = coef[layer - 1] * inverse if layer > 0 else jnp.zeros_like(inverse)
        factor_ref[2, layer] = ratio


def solve_columns(read, write, factor_ref, layers):
    forward = []
    for layer in range(layers):
        value = read(layer) * factor_ref[0, layer]
        if layer > 0:
            value = value + factor_ref[1, layer] * forward[-1]
        forward.append(value)
    value = forward[-1]
    write(layers - 1, value)
    for layer in range(layers - 2, -1, -1):
        value = forward[layer] + factor_ref[2, layer] * value
        write(layer, value)


def packed_at(layer, held):
    return pl.ds((layer // held) * 8 * held + layer % held, 8, stride=held)


def weigh(profile, matrix_ref, capacity):
    kv = matrix_ref.shape[1]
    owners = LANES // capacity
    mine = lax.broadcasted_iota(jnp.int32, (kv, LANES), 1) // capacity
    tiles = []
    for tile in range(matrix_ref.shape[0] // owners):
        values = profile[:, tile * LANES : (tile + 1) * LANES]
        masked = jnp.concatenate([jnp.where(mine == owner, values, 0.0) for owner in range(owners)], axis=0)
        matrices = jnp.concatenate([matrix_ref[tile * owners + owner] for owner in range(owners)], axis=1)
        tiles.append(dot_parts(split(matrices), split(masked), ((1,), (0,))))
    return jnp.concatenate(tiles, axis=1)


def profile_kernel(
    layers,
    held,
    capacity,
    packed_ref,
    vert_ref,
    high_ref,
    low_ref,
    near_ref,
    weighted_ref,
    profile_ref,
    factor_ref,
    column_ref,
):
    kv = profile_ref.shape[0]
    half = profile_ref.shape[1]
    vertical_factors_kernel(vert_ref, factor_ref)

    def read(layer):
        return packed_ref[packed_at(layer, held), :]

    def write(layer, value):
        column_ref[pl.ds(layer, 8, stride=layers), :] = value

    solve_columns(read, write, factor_ref, layers)
    columns = jnp.concatenate([column_ref[0:kv, :], column_ref[kv : 2 * kv, :]], axis=1)
    profile = dot_parts(split(columns), (high_ref[...], low_ref[...]), ((1,), (0,)))
    profile_ref[...] = profile[:, half:]
    weighted_ref[...] = weigh(profile[:, :half], near_ref, capacity)


def spread_kernel(
    layers, held, capacity, near_ref, profile_ref, factor_ref, high_ref, low_ref, far_ref, out_ref, column_ref
):
    kv = near_ref.shape[0]
    weighted = jnp.concatenate([near_ref[...], weigh(profile_ref[...], far_ref, capacity)], axis=1)
    spread = dot_parts(split(weighted), (high_ref[...], low_ref[...]), ((1,), (1,)))
    column_ref[0:kv, :] = spread[:, :LANES]
    column_ref[kv : 2 * kv, :] = spread[:, LANES:]

    def read(layer):
        return column_ref[pl.ds(layer, 8, stride=layers), :]

    def write(layer, value):
        out_ref[packed_at(layer, held), :] = value

    solve_columns(read, write, factor_ref, layers)


def vmem(count):
    return [pl.BlockSpec(memory_space=pltpu.VMEM)] * count


def call(kernel, out_shape, inputs, scratch=(), after=0, hbm=False, flops=1_000_000, mib=8):
    specs = [pl.BlockSpec(memory_space=pl.ANY)] * after + vmem(len(inputs) - after)
    if hbm:
        specs = [pl.BlockSpec(memory_space=pltpu.HBM)] * len(inputs)
    moved = sum(math.prod(x.shape) * 4 for x in inputs)
    return pl.pallas_call(
        kernel,
        out_shape=out_shape,
        in_specs=specs,
        out_specs=tuple(vmem(len(out_shape))) if isinstance(out_shape, tuple) else vmem(1)[0],
        scratch_shapes=list(scratch),
        compiler_params=pltpu.CompilerParams(vmem_limit_bytes=mib * 1024 * 1024),
        cost_estimate=pl.CostEstimate(flops=flops, bytes_accessed=moved, transcendentals=0),
    )(*inputs)


def f32(*shape):
    return jax.ShapeDtypeStruct(shape, jnp.float32)


def from_neighbours(block):
    count = lax.axis_size("gy")
    pair = lax.ppermute(block, "gy", [(i, i ^ 1) for i in range(count)])
    cross = lax.ppermute(block, "gy", [(i, (i + (1 if i % 2 else -1)) % count) for i in range(count)])
    return pair, cross


def apart_by(block, axis, stride):
    return lax.ppermute(block, axis, [(i, i ^ stride) for i in range(lax.axis_size(axis))])


def per_device_gathered(
    direction,
    solution,
    residual,
    north_coef,
    east_coef,
    ocean,
    vert_coef,
    obs_owner,
    obs_row,
    obs_col,
    obs_frac,
    error_inverse,
):
    var_count, held, rows, lons = direction.shape
    kv = var_count * held
    tiles = lons // LANES
    layers, _, lon_cols = vert_coef.shape
    rows_y, cols_x = lax.axis_size("gy"), lax.axis_size("gx")
    device_count = rows_y * cols_x
    obs_count = obs_row.shape[-1]
    capacity = 2 * obs_count // device_count
    wide = error_inverse.shape[-1]
    cells = rows * lon_cols

    direction_n = to_native(direction)
    residual_n = to_native(residual)
    solution_n = to_native(solution)
    faces = [to_native(x[None, None]) for x in (north_coef, east_coef, ocean)]
    own = call(
        halo_kernel,
        f32(direction_n.shape[0] + 3 * faces[0].shape[0], LANES),
        (direction_n, *faces),
        scratch=(pltpu.VMEM(faces[0].shape, jnp.int32), pltpu.SemaphoreType.DMA((4,))),
        hbm=True,
        mib=56,
    )
    pair, cross = from_neighbours(own)

    matrix = error_inverse.reshape(1, wide, wide)
    blocks = [matrix] + [apart_by(matrix, "gx", stride) for stride in range(2, cols_x, 2)]
    extended = 3 * rows + (-3 * rows) % 8
    packed, coef, held_blocks = call(
        functools.partial(first_lateral_kernel, kv, rows, tiles, len(blocks)),
        (f32(cols_x, 2 * kv, LANES), f32(5, extended, lons), f32(len(blocks), wide, wide)),
        (direction_n, *faces, pair, cross, *blocks),
        scratch=(
            pltpu.VMEM((3, extended, lons), jnp.float32),
            pltpu.VMEM(own.shape, jnp.float32),
            pltpu.VMEM(own.shape, jnp.float32),
        ),
        flops=4_000_000,
    )
    halves = jax.ShapeDtypeStruct((cells, device_count * capacity), jnp.bfloat16)
    interp = call(
        functools.partial(prepare_kernel, device_count, capacity, lon_cols),
        (halves, halves),
        (
            packed,
            obs_owner.reshape(1, obs_count),
            obs_row.reshape(1, obs_count),
            obs_col.reshape(1, obs_count),
            obs_frac.reshape(2, obs_count),
        ),
        after=1,
        flops=20_000_000,
        mib=16,
    )
    fetched = [held_blocks] + [apart_by(held_blocks, "gy", stride) for stride in range(1, rows_y)]
    columns = lax.all_to_all(packed, "gx", split_axis=0, concat_axis=0, tiled=True)
    columns = columns.reshape(cols_x * 2 * kv, LANES)
    near = call(
        functools.partial(join_kernel, len(fetched)),
        f32(device_count // 2, wide, wide),
        (columns, interp[0], *fetched),
        after=2,
    )
    far = apart_by(near, "gx", 1)
    half = device_count // 2 * capacity
    weighted, profile, factors = call(
        functools.partial(profile_kernel, layers, held, capacity),
        (f32(wide, half), f32(wide, half), f32(3, layers, 8, LANES)),
        (columns, vert_coef.reshape(layers, cells // LANES, LANES), *interp, near),
        scratch=(pltpu.VMEM((2 * wide, LANES), jnp.float32),),
        flops=400_000_000,
        mib=16,
    )
    spread = call(
        functools.partial(spread_kernel, layers, held, capacity),
        f32(cols_x * 2 * kv, LANES),
        (weighted, profile, factors, *interp, far),
        scratch=(pltpu.VMEM((2 * wide, LANES), jnp.float32),),
        flops=400_000_000,
        mib=16,
    )
    tile = lax.all_to_all(
        spread.reshape(cols_x, 2 * kv, LANES), "gx", split_axis=0, concat_axis=0, tiled=True
    )
    pair, cross = from_neighbours(tile)
    image, sums = call(
        functools.partial(second_lateral_kernel, kv, rows, tiles),
        (f32(*direction_n.shape), f32(device_count, 1, LANES)),
        (tile, pair, cross, coef, direction_n, residual_n),
        scratch=(pltpu.VMEM(tile.shape, jnp.float32), pltpu.VMEM(tile.shape, jnp.float32)),
        flops=4_000_000,
    )
    sums = lax.all_to_all(sums, ("gy", "gx"), split_axis=0, concat_axis=0, tiled=True)
    after = call(
        update_kernel,
        (f32(*direction_n.shape),) * 3,
        (sums, direction_n, solution_n, residual_n, image),
    )
    return tuple(from_native(x, direction.shape) for x in after)


def gathers(mesh, shapes):
    rows_y, cols_x = mesh.shape["gy"], mesh.shape["gx"]
    devices = rows_y * cols_x
    if any(size < 2 or size & (size - 1) for size in (rows_y, cols_x)):
        return False
    direction, vert_coef, obs_row, error_inverse = shapes
    var_count, layers, lat_rows, lons = direction
    rows, held = lat_rows // rows_y, layers // cols_x
    obs_count, wide = obs_row[-1], error_inverse[-1]
    capacity = 2 * obs_count // devices
    return (
        rows == NSTEP == 4
        and var_count == 4
        and (var_count * held) % 8 == 0
        and lons // cols_x * 2 == LANES
        and wide == LANES
        and capacity > 0
        and LANES % capacity == 0
        and devices // 2 % (LANES // capacity) == 0
        and devices * wide * wide * 4 <= 8 * 1024 * 1024
    )


def padded(cells, sides, width):
    for axis, dim in sides:
        count = lax.axis_size(axis)
        ends = count - 1
        head = lax.slice_in_dim(cells, 0, width, axis=dim)
        tail = lax.slice_in_dim(cells, cells.shape[dim] - width, cells.shape[dim], axis=dim)
        cells = jnp.concatenate(
            [
                lax.ppermute(tail, axis, [(i, (i + 1) % count) for i in range(ends)]),
                cells,
                lax.ppermute(head, axis, [((i + 1) % count, i) for i in range(ends)]),
            ],
            axis=dim,
        )
    return cells


def lateral_faces(north_ext, east_ext, ocean_ext):
    ocean_next = jnp.concatenate([ocean_ext[1:], jnp.zeros_like(ocean_ext[:1])], axis=0)
    north_face = north_ext * ocean_ext * ocean_next
    east_face = east_ext * ocean_ext * jnp.roll(ocean_ext, -1, axis=1)
    return (north_face, east_face, ocean_ext)


def diffuse_once(values_grid, north_face, east_face, ocean_ext):
    north_flux = north_face[:-1] * (values_grid[:, :, 1:, :] - values_grid[:, :, :-1, :])
    east_flux = east_face * (jnp.roll(values_grid, -1, axis=3) - values_grid)
    lateral = east_flux - jnp.roll(east_flux, 1, axis=3)
    return (
        ocean_ext[1:-1] * values_grid[:, :, 1:-1, :]
        + north_flux[:, :, 1:, :]
        - north_flux[:, :, :-1, :]
        + lateral[:, :, 1:-1, :]
    )


def lateral_pass(values_tile, faces):
    north_face, east_face, ocean_ext = faces
    grown = padded(values_tile, (("gy", 2),), NSTEP)
    total_rows = grown.shape[2]
    for step_index in range(NSTEP):
        upper = total_rows - step_index
        grown = diffuse_once(
            grown,
            north_face[step_index:upper],
            east_face[step_index:upper],
            ocean_ext[step_index:upper],
        )
    return grown


def vertical_factors(vert_coef):
    inverse_rows = []
    upper_ratio = []
    for layer_index in range(vert_coef.shape[0]):
        diagonal = 1.0 + vert_coef[layer_index]
        if layer_index > 0:
            diagonal = (
                diagonal + vert_coef[layer_index - 1] + vert_coef[layer_index - 1] * upper_ratio[-1]
            )
        inverse = 1.0 / diagonal
        inverse_rows.append(inverse)
        upper_ratio.append(-vert_coef[layer_index] * inverse)
    return (inverse_rows, upper_ratio)


def vertical_solve(values_col, vert_coef, factors):
    inverse_rows, upper_ratio = factors
    layers = values_col.shape[1]
    forward = []
    for layer_index in range(layers):
        source = values_col[:, layer_index]
        if layer_index > 0:
            source = source + vert_coef[layer_index - 1] * forward[-1]
        forward.append(source * inverse_rows[layer_index])
    result = [forward[-1]]
    for layer_index in range(layers - 2, -1, -1):
        result.append(forward[layer_index] - upper_ratio[layer_index] * result[-1])
    return jnp.stack(result[::-1], axis=1)


def observe_weigh_spread(columns, obs_owner, obs_row, obs_col, obs_frac, error_inverse):
    var_count, lev_count, lat_rows, lon_cols = columns.shape
    kv_width = var_count * lev_count
    rows_y = lax.axis_size("gy")
    cols_x = lax.axis_size("gx")
    device_count = rows_y * cols_x
    obs_count = obs_row.shape[-1]
    capacity = 2 * obs_count // device_count
    flat = columns.reshape(kv_width, lat_rows * lon_cols)
    cell = obs_row.reshape(-1) * lon_cols + obs_col.reshape(-1)
    corners = (cell, cell + 1, cell + lon_cols, cell + lon_cols + 1)
    lat_frac = obs_frac[0, 0, 0]
    lon_frac = obs_frac[0, 0, 1]
    weights = (
        (1.0 - lat_frac) * (1.0 - lon_frac),
        (1.0 - lat_frac) * lon_frac,
        lat_frac * (1.0 - lon_frac),
        lat_frac * lon_frac,
    )
    profile = weights[0] * jnp.take(flat, corners[0], axis=1)
    for corner_index in range(1, 4):
        profile = profile + weights[corner_index] * jnp.take(flat, corners[corner_index], axis=1)
    owners = obs_owner.reshape(-1)
    onehot = (owners[:, None] == jnp.arange(device_count, dtype=jnp.int32)[None, :]).astype(
        jnp.int32
    )
    running = jnp.cumsum(onehot, axis=0)
    rank_in = jnp.sum(running * onehot, axis=1) - 1
    slot = owners * capacity + rank_in
    outgoing = jnp.zeros((device_count * capacity, kv_width), jnp.float32).at[slot].set(profile.T)
    outgoing = outgoing.reshape(rows_y, cols_x, capacity, kv_width)
    matrix = error_inverse.reshape(kv_width, kv_width)
    arrived = lax.all_to_all(
        lax.all_to_all(outgoing, "gy", split_axis=0, concat_axis=0, tiled=True),
        "gx",
        split_axis=1,
        concat_axis=1,
        tiled=True,
    )
    weighted = jnp.dot(
        arrived.reshape(-1, kv_width),
        matrix,
        precision=lax.Precision.HIGHEST,
        preferred_element_type=jnp.float32,
    ).reshape(rows_y, cols_x, capacity, kv_width)
    returned = lax.all_to_all(
        lax.all_to_all(weighted, "gy", split_axis=0, concat_axis=0, tiled=True),
        "gx",
        split_axis=1,
        concat_axis=1,
        tiled=True,
    )
    back = returned.reshape(device_count * capacity, kv_width)[slot].T
    spread = jnp.zeros((kv_width, lat_rows * lon_cols), jnp.float32)
    for corner_index in range(4):
        spread = spread.at[:, corners[corner_index]].add(weights[corner_index] * back)
    return spread.reshape(var_count, lev_count, lat_rows, lon_cols)


def per_device(
    direction,
    solution,
    residual,
    north_coef,
    east_coef,
    ocean,
    vert_coef,
    obs_owner,
    obs_row,
    obs_col,
    obs_frac,
    error_inverse,
):
    stacked = jnp.stack([north_coef, east_coef, ocean.astype(jnp.float32)])
    reach = NSTEP
    grown_coef = padded(stacked, (("gy", 1),), reach)
    faces = lateral_faces(grown_coef[0], grown_coef[1], grown_coef[2])
    factors = vertical_factors(vert_coef)
    smoothed = lateral_pass(direction, faces)
    columns = lax.all_to_all(smoothed, "gx", split_axis=3, concat_axis=1, tiled=True)
    columns = vertical_solve(columns, vert_coef, factors)
    spread = observe_weigh_spread(columns, obs_owner, obs_row, obs_col, obs_frac, error_inverse)
    spread = vertical_solve(spread, vert_coef, factors)
    tiles = lax.all_to_all(spread, "gx", split_axis=1, concat_axis=3, tiled=True)
    image = direction + lateral_pass(tiles, faces)
    norm_now, curvature = lax.psum(
        (jnp.sum(residual * residual), jnp.sum(direction * image)), ("gy", "gx")
    )
    alpha = norm_now / curvature
    residual_next = residual - alpha * image
    norm_next = lax.psum(jnp.sum(residual_next * residual_next), ("gy", "gx"))
    solution_next = solution + alpha * direction
    direction_next = residual_next + norm_next / norm_now * direction
    return (solution_next, residual_next, direction_next)


def solution(mesh):
    in_specs = (
        P(None, "gx", "gy", None),
        P(None, "gx", "gy", None),
        P(None, "gx", "gy", None),
        P("gy", None),
        P("gy", None),
        P("gy", None),
        P(None, "gy", "gx"),
        P("gy", "gx", None, None),
        P("gy", "gx", None),
        P("gy", "gx", None),
        P("gy", "gx", None, None),
        P("gy", "gx", None, None),
    )
    out_specs = (P(None, "gx", "gy", None),) * 3

    def step(*arrays):
        shapes = [arrays[at].shape for at in (0, 6, 8, 11)]
        local = per_device_gathered if gathers(mesh, shapes) else per_device
        return jax.shard_map(
            local, mesh=mesh, in_specs=in_specs, out_specs=out_specs, check_vma=False
        )(*arrays)

    return step
```

```python
import functools
import math

import jax
import jax.numpy as jnp
from jax import lax
from jax.experimental import pallas as pl
from jax.experimental.pallas import tpu as pltpu
from jax.sharding import PartitionSpec as P

NSTEP = 4
LANES = 128


def to_native(tile):
    kv, rows, lons = tile.shape[0] * tile.shape[1], tile.shape[2], tile.shape[3]
    return tile.reshape(kv, rows, lons // LANES, LANES).swapaxes(1, 2).reshape(-1, LANES)


def from_native(flat, shape):
    kv, rows, lons = shape[0] * shape[1], shape[2], shape[3]
    return flat.reshape(kv, lons // LANES, rows, LANES).swapaxes(1, 2).reshape(shape)


def native_rows(ref, base, row, rows, tiles, half):
    parts = [
        ref[pl.ds(base + (half * 8 * tiles + tile) * rows + row, 8, stride=tiles * rows), :]
        for tile in range(tiles)
    ]
    return jnp.concatenate(parts, axis=1)


def lane_low(shape):
    return lax.broadcasted_iota(jnp.int32, shape, 1) < LANES // 2


def lateral_rows(rows, coef, reach):
    for step in range(reach):
        after = []
        for i in range(1, len(rows) - 1):
            at = step + i
            u = rows[i]
            width = u.shape[1]
            after.append(
                coef[0, at : at + 1, :] * u
                + coef[1, at : at + 1, :] * rows[i + 1]
                + coef[2, at : at + 1, :] * rows[i - 1]
                + coef[3, at : at + 1, :] * pltpu.roll(u, width - 1, 1)
                + coef[4, at : at + 1, :] * pltpu.roll(u, 1, 1)
            )
        rows = after
    return rows


def sort_halo(pair_ref, cross_ref, low_ref, high_ref):
    at_y, rows_y = lax.axis_index("gy"), lax.axis_size("gy")
    odd = lax.rem(at_y, 2) == 1

    @pl.when(odd)
    def _():
        low_ref[...] = pair_ref[...]
        high_ref[...] = cross_ref[...]

    @pl.when(jnp.logical_not(odd))
    def _():
        low_ref[...] = cross_ref[...]
        high_ref[...] = pair_ref[...]

    @pl.when(at_y == 0)
    def _():
        low_ref[...] = jnp.zeros_like(low_ref)

    @pl.when(at_y == rows_y - 1)
    def _():
        high_ref[...] = jnp.zeros_like(high_ref)


def halo_kernel(direction_ref, north_ref, east_ref, ocean_ref, own_ref, mask_ref, ocean_mask_ref, sems):
    cells, size = direction_ref.shape[0], north_ref.shape[0]
    mask = pltpu.make_async_copy(ocean_ref, mask_ref, sems.at[0])
    moves = (
        (direction_ref, own_ref.at[pl.ds(0, cells)]),
        (north_ref, own_ref.at[pl.ds(cells, size)]),
        (east_ref, own_ref.at[pl.ds(cells + size, size)]),
    )
    copies = [pltpu.make_async_copy(*move, sems.at[1 + at]) for at, move in enumerate(moves)]
    mask.start()
    for copy in copies:
        copy.start()
    mask.wait()
    ocean_mask_ref[...] = mask_ref[...].astype(jnp.float32)
    last = pltpu.make_async_copy(ocean_mask_ref, own_ref.at[pl.ds(cells + 2 * size, size)], sems.at[4])
    last.start()
    for copy in copies:
        copy.wait()
    last.wait()


def join_kernel(after, count, *refs):
    blocks, (near_ref,) = refs[after : after + count], refs[after + count :]
    size = blocks[0].shape[0]
    for at, block in enumerate(blocks):
        near_ref[at * size : (at + 1) * size] = block[...]


def first_lateral_kernel(
    kv,
    rows,
    tiles,
    _,
    own_ref,
    north_ref,
    east_ref,
    ocean_ref,
    pair_ref,
    cross_ref,
    packed_ref,
    coef_ref,
    ext_ref,
    low_ref,
    high_ref,
):
    lons = tiles * LANES
    cells = kv * tiles * rows
    sort_halo(pair_ref, cross_ref, low_ref, high_ref)
    ext_ref[...] = jnp.zeros_like(ext_ref)
    for kind, kept in enumerate((north_ref, east_ref, ocean_ref)):
        for tile in range(tiles):
            lanes = slice(tile * LANES, (tile + 1) * LANES)
            start = cells + (kind * tiles + tile) * rows
            ext_ref[kind, 0:rows, lanes] = low_ref[start : start + rows, :]
            ext_ref[kind, rows : 2 * rows, lanes] = kept[tile * rows : (tile + 1) * rows, :].astype(jnp.float32)
            ext_ref[kind, 2 * rows : 3 * rows, lanes] = high_ref[start : start + rows, :]
    total = ext_ref.shape[1]
    north, east, ocean = ext_ref[0], ext_ref[1], ext_ref[2]
    north_face = north * ocean * pltpu.roll(ocean, total - 1, 0)
    east_face = east * ocean * pltpu.roll(ocean, lons - 1, 1)
    south_face = pltpu.roll(north_face, 1, 0)
    west_face = pltpu.roll(east_face, 1, 1)
    coef_ref[0] = ocean - north_face - south_face - east_face - west_face
    coef_ref[1] = north_face
    coef_ref[2] = south_face
    coef_ref[3] = east_face
    coef_ref[4] = west_face
    low = lane_low((8, LANES))
    for half in range(kv // 8):
        grown = [
            native_rows(ref, 0, row, rows, tiles, half)
            for ref in (low_ref, own_ref, high_ref)
            for row in range(rows)
        ]
        done = lateral_rows(grown, coef_ref, rows)
        for pair in range(rows // 2):
            for tile in range(tiles):
                first = done[2 * pair][:, tile * LANES : (tile + 1) * LANES]
                second = done[2 * pair + 1][:, tile * LANES : (tile + 1) * LANES]
                at = pair * kv + half * 8
                packed_ref[2 * tile, at : at + 8, :] = jnp.where(
                    low, first, pltpu.roll(second, LANES // 2, 1)
                )
                packed_ref[2 * tile + 1, at : at + 8, :] = jnp.where(
                    low, pltpu.roll(first, LANES // 2, 1), second
                )


def second_lateral_kernel(
    kv,
    rows,
    tiles,
    own_ref,
    pair_ref,
    cross_ref,
    coef_ref,
    direction_ref,
    residual_ref,
    image_ref,
    sums_ref,
    low_ref,
    high_ref,
):
    sort_halo(pair_ref, cross_ref, low_ref, high_ref)
    low = lane_low((8, LANES))
    totals = [jnp.zeros((8, tiles * LANES), jnp.float32) for _ in range(4)]
    for half in range(kv // 8):
        grown = []
        for ref in (low_ref, own_ref, high_ref):
            for pair in range(rows // 2):
                firsts, seconds = [], []
                at = pair * kv + half * 8
                for tile in range(tiles):
                    even = ref[2 * tile, at : at + 8, :]
                    odd = ref[2 * tile + 1, at : at + 8, :]
                    firsts.append(jnp.where(low, even, pltpu.roll(odd, LANES // 2, 1)))
                    seconds.append(jnp.where(low, pltpu.roll(even, LANES // 2, 1), odd))
                grown.append(jnp.concatenate(firsts, axis=1))
                grown.append(jnp.concatenate(seconds, axis=1))
        done = lateral_rows(grown, coef_ref, rows)
        for row in range(rows):
            direction = native_rows(direction_ref, 0, row, rows, tiles, half)
            residual = native_rows(residual_ref, 0, row, rows, tiles, half)
            image = direction + done[row]
            for tile in range(tiles):
                image_ref[pl.ds((half * 8 * tiles + tile) * rows + row, 8, stride=tiles * rows), :] = image[
                    :, tile * LANES : (tile + 1) * LANES
                ]
            totals[0] = totals[0] + residual * residual
            totals[1] = totals[1] + direction * image
            totals[2] = totals[2] + residual * image
            totals[3] = totals[3] + image * image
    lane = lax.broadcasted_iota(jnp.int32, (1, LANES), 1)
    line = jnp.zeros((1, LANES), jnp.float32)
    for at, total in enumerate(totals):
        line = jnp.where(lane == at, jnp.sum(total), line)
    for device in range(sums_ref.shape[0]):
        sums_ref[device] = line


def update_kernel(sums_ref, direction_ref, solution_ref, residual_ref, image_ref, sol_ref, res_ref, dir_ref):
    line = jnp.sum(sums_ref[...], axis=0)
    lane = lax.broadcasted_iota(jnp.int32, line.shape, 1)

    def pick(at):
        return jnp.sum(jnp.where(lane == at, line, 0.0), axis=1, keepdims=True)

    norm_now, curvature, cross, square = pick(0), pick(1), pick(2), pick(3)
    alpha = norm_now / curvature
    norm_next = norm_now - 2.0 * alpha * cross + alpha * alpha * square
    beta = norm_next / norm_now
    direction = direction_ref[...]
    residual_next = residual_ref[...] - alpha * image_ref[...]
    sol_ref[...] = solution_ref[...] + alpha * direction
    res_ref[...] = residual_next
    dir_ref[...] = residual_next + beta * direction


def split(value):
    high = value.astype(jnp.bfloat16)
    return high, (value - high.astype(jnp.float32)).astype(jnp.bfloat16)


def dot_parts(left, right, contract):
    dims = (contract, ((), ()))
    total = lax.dot_general(left[0], right[0], dims, preferred_element_type=jnp.float32)
    total = total + lax.dot_general(left[0], right[1], dims, preferred_element_type=jnp.float32)
    return total + lax.dot_general(left[1], right[0], dims, preferred_element_type=jnp.float32)


def prepare_kernel(
    devices,
    capacity,
    lon_cols,
    vert_ref,
    owner_ref,
    row_ref,
    col_ref,
    frac_ref,
    factor_ref,
    high_ref,
    low_ref,
):
    vertical_factors_of(vert_ref, factor_ref)
    count = owner_ref.shape[1]
    slots = devices * capacity
    me = lax.axis_index("gy") * lax.axis_size("gx") + lax.axis_index("gx")
    apart = jnp.bitwise_xor(owner_ref[...], me)
    place = jnp.bitwise_and(apart, 1) * (devices // 2) + jnp.right_shift(apart, 1)
    named = lax.broadcasted_iota(jnp.int32, (devices, count), 0) == place
    before = lax.broadcasted_iota(jnp.int32, (count, count), 0) <= lax.broadcasted_iota(
        jnp.int32, (count, count), 1
    )
    running = jnp.dot(
        jnp.where(named, 1.0, 0.0).astype(jnp.bfloat16),
        jnp.where(before, 1.0, 0.0).astype(jnp.bfloat16),
        preferred_element_type=jnp.float32,
    )
    rank = jnp.sum(jnp.where(named, running, 0.0), axis=0, keepdims=True) - 1.0
    slot = place * capacity + rank.astype(jnp.int32)
    chosen = jnp.where(
        lax.broadcasted_iota(jnp.int32, (slots, count), 0) == slot, 1.0, 0.0
    ).astype(jnp.bfloat16)
    lat_frac = frac_ref[0:1, :]
    lon_frac = frac_ref[1:2, :]
    cell = (row_ref[...] * lon_cols + col_ref[...]).astype(jnp.float32)
    values = jnp.concatenate(
        [
            (1.0 - lat_frac) * (1.0 - lon_frac),
            (1.0 - lat_frac) * lon_frac,
            lat_frac * (1.0 - lon_frac),
            lat_frac * lon_frac,
            cell,
            jnp.zeros((3, count), jnp.float32),
        ],
        axis=0,
    )
    high, rest = split(values)
    low, rest = split(values - high.astype(jnp.float32))
    parts = jnp.concatenate([high.astype(jnp.float32), low.astype(jnp.float32), rest.astype(jnp.float32)], axis=0)
    placed = lax.dot_general(
        parts.astype(jnp.bfloat16), chosen, (((1,), (1,)), ((), ())), preferred_element_type=jnp.float32
    )
    placed = placed[0:8] + placed[8:16] + placed[16:24]
    first = jnp.round(placed[4:5, :]).astype(jnp.int32)
    away = lax.broadcasted_iota(jnp.int32, high_ref.shape, 0) - first
    interp = jnp.where(
        away == 0,
        placed[0:1, :],
        jnp.where(
            away == 1,
            placed[1:2, :],
            jnp.where(away == lon_cols, placed[2:3, :], jnp.where(away == lon_cols + 1, placed[3:4, :], 0.0)),
        ),
    )
    high_ref[...], low_ref[...] = split(interp)


def vertical_factors_of(vert_ref, factor_ref):
    layers = vert_ref.shape[0]
    top = lax.broadcasted_iota(jnp.int32, (8, LANES), 0) < 4
    coef = [jnp.where(top, vert_ref[layer, 0:1, :], vert_ref[layer, 1:2, :]) for layer in range(layers)]
    ratio = None
    for layer in range(layers):
        diagonal = 1.0 + coef[layer]
        if layer > 0:
            diagonal = diagonal + coef[layer - 1] - coef[layer - 1] * ratio
        inverse = 1.0 / diagonal
        ratio = coef[layer] * inverse
        factor_ref[0, layer] = inverse
        factor_ref[1, layer] = coef[layer - 1] * inverse if layer > 0 else jnp.zeros_like(inverse)
        factor_ref[2, layer] = ratio


def solve_columns(read, write, factor_ref, layers):
    forward = []
    for layer in range(layers):
        value = read(layer) * factor_ref[0, layer]
        if layer > 0:
            value = value + factor_ref[1, layer] * forward[-1]
        forward.append(value)
    value = forward[-1]
    write(layers - 1, value)
    for layer in range(layers - 2, -1, -1):
        value = forward[layer] + factor_ref[2, layer] * value
        write(layer, value)


def packed_at(layer, held):
    return pl.ds((layer // held) * 8 * held + layer % held, 8, stride=held)


def weigh(profile, matrix_ref, capacity):
    kv = matrix_ref.shape[1]
    owners = LANES // capacity
    mine = lax.broadcasted_iota(jnp.int32, (kv, LANES), 1) // capacity
    tiles = []
    for tile in range(matrix_ref.shape[0] // owners):
        values = profile[:, tile * LANES : (tile + 1) * LANES]
        masked = jnp.concatenate([jnp.where(mine == owner, values, 0.0) for owner in range(owners)], axis=0)
        matrices = jnp.concatenate([matrix_ref[tile * owners + owner] for owner in range(owners)], axis=1)
        tiles.append(dot_parts(split(matrices), split(masked), ((1,), (0,))))
    return jnp.concatenate(tiles, axis=1)


def profile_kernel(
    layers,
    held,
    capacity,
    packed_ref,
    factor_ref,
    high_ref,
    low_ref,
    near_ref,
    weighted_ref,
    profile_ref,
    column_ref,
):
    kv = profile_ref.shape[0]
    half = profile_ref.shape[1]
    def read(layer):
        return packed_ref[packed_at(layer, held), :]

    def write(layer, value):
        column_ref[pl.ds(layer, 8, stride=layers), :] = value

    solve_columns(read, write, factor_ref, layers)
    columns = jnp.concatenate([column_ref[0:kv, :], column_ref[kv : 2 * kv, :]], axis=1)
    profile = dot_parts(split(columns), (high_ref[...], low_ref[...]), ((1,), (0,)))
    profile_ref[...] = profile[:, half:]
    weighted_ref[...] = weigh(profile[:, :half], near_ref, capacity)


def spread_kernel(
    layers, held, capacity, near_ref, profile_ref, factor_ref, high_ref, low_ref, far_ref, out_ref, column_ref
):
    kv = near_ref.shape[0]
    weighted = jnp.concatenate([near_ref[...], weigh(profile_ref[...], far_ref, capacity)], axis=1)
    spread = dot_parts(split(weighted), (high_ref[...], low_ref[...]), ((1,), (1,)))
    column_ref[0:kv, :] = spread[:, :LANES]
    column_ref[kv : 2 * kv, :] = spread[:, LANES:]

    def read(layer):
        return column_ref[pl.ds(layer, 8, stride=layers), :]

    def write(layer, value):
        out_ref[packed_at(layer, held), :] = value

    solve_columns(read, write, factor_ref, layers)


def vmem(count):
    return [pl.BlockSpec(memory_space=pltpu.VMEM)] * count


def call(kernel, out_shape, inputs, scratch=(), after=0, hbm=False, flops=1_000_000, mib=8):
    specs = [pl.BlockSpec(memory_space=pl.ANY)] * after + vmem(len(inputs) - after)
    outs = vmem(len(out_shape) if isinstance(out_shape, tuple) else 1)
    if hbm:
        specs, outs = ([pl.BlockSpec(memory_space=pltpu.HBM)] * len(x) for x in (specs, outs))
    moved = sum(math.prod(x.shape) * 4 for x in inputs)
    return pl.pallas_call(
        kernel,
        out_shape=out_shape,
        in_specs=specs,
        out_specs=tuple(outs) if isinstance(out_shape, tuple) else outs[0],
        scratch_shapes=list(scratch),
        compiler_params=pltpu.CompilerParams(vmem_limit_bytes=mib * 1024 * 1024),
        cost_estimate=pl.CostEstimate(flops=flops, bytes_accessed=moved, transcendentals=0),
    )(*inputs)


def f32(*shape):
    return jax.ShapeDtypeStruct(shape, jnp.float32)


def from_neighbours(block):
    count = lax.axis_size("gy")
    pair = lax.ppermute(block, "gy", [(i, i ^ 1) for i in range(count)])
    cross = lax.ppermute(block, "gy", [(i, (i + (1 if i % 2 else -1)) % count) for i in range(count)])
    return pair, cross


def apart_by(block, axis, stride):
    return lax.ppermute(block, axis, [(i, i ^ stride) for i in range(lax.axis_size(axis))])


def per_device_gathered(
    direction,
    solution,
    residual,
    north_coef,
    east_coef,
    ocean,
    vert_coef,
    obs_owner,
    obs_row,
    obs_col,
    obs_frac,
    error_inverse,
):
    var_count, held, rows, lons = direction.shape
    kv = var_count * held
    tiles = lons // LANES
    layers, _, lon_cols = vert_coef.shape
    rows_y, cols_x = lax.axis_size("gy"), lax.axis_size("gx")
    device_count = rows_y * cols_x
    obs_count = obs_row.shape[-1]
    capacity = 2 * obs_count // device_count
    wide = error_inverse.shape[-1]
    cells = rows * lon_cols

    direction_n = to_native(direction)
    residual_n = to_native(residual)
    solution_n = to_native(solution)
    faces = [to_native(x[None, None]) for x in (north_coef, east_coef, ocean)]
    own = call(
        halo_kernel,
        f32(direction_n.shape[0] + 3 * faces[0].shape[0], LANES),
        (direction_n, *faces),
        scratch=(
            pltpu.VMEM(faces[0].shape, jnp.int32),
            pltpu.VMEM(faces[0].shape, jnp.float32),
            pltpu.SemaphoreType.DMA((5,)),
        ),
        hbm=True,
        mib=56,
    )
    pair, cross = from_neighbours(own)

    matrix = error_inverse.reshape(1, wide, wide)
    blocks = [matrix] + [apart_by(matrix, "gx", stride) for stride in range(2, cols_x, 2)]
    halves = jax.ShapeDtypeStruct((cells, device_count * capacity), jnp.bfloat16)
    factors, *interp = call(
        functools.partial(prepare_kernel, device_count, capacity, lon_cols),
        (f32(3, layers, 8, LANES), halves, halves),
        (
            vert_coef.reshape(layers, cells // LANES, LANES),
            obs_owner.reshape(1, obs_count),
            obs_row.reshape(1, obs_count),
            obs_col.reshape(1, obs_count),
            obs_frac.reshape(2, obs_count),
        ),
        flops=20_000_000,
        mib=16,
    )
    held_blocks = call(
        functools.partial(join_kernel, 1, len(blocks)),
        f32(len(blocks), wide, wide),
        (interp[0], *blocks),
        after=1,
    )

    extended = 3 * rows + (-3 * rows) % 8
    packed, coef = call(
        functools.partial(first_lateral_kernel, kv, rows, tiles),
        (f32(cols_x, 2 * kv, LANES), f32(5, extended, lons)),
        (held_blocks, direction_n, *faces, pair, cross),
        after=1,
        scratch=(
            pltpu.VMEM((3, extended, lons), jnp.float32),
            pltpu.VMEM(own.shape, jnp.float32),
            pltpu.VMEM(own.shape, jnp.float32),
        ),
        flops=4_000_000,
    )
    fetched = [held_blocks] + [apart_by(held_blocks, "gy", stride) for stride in range(1, rows_y)]
    columns = lax.all_to_all(packed, "gx", split_axis=0, concat_axis=0, tiled=True)
    columns = columns.reshape(cols_x * 2 * kv, LANES)
    near = call(
        functools.partial(join_kernel, 1, len(fetched)),
        f32(device_count // 2, wide, wide),
        (columns, *fetched),
        after=1,
    )
    far = apart_by(near, "gx", 1)
    half = device_count // 2 * capacity
    weighted, profile = call(
        functools.partial(profile_kernel, layers, held, capacity),
        (f32(wide, half), f32(wide, half)),
        (columns, factors, *interp, near),
        scratch=(pltpu.VMEM((2 * wide, LANES), jnp.float32),),
        flops=400_000_000,
        mib=16,
    )
    spread = call(
        functools.partial(spread_kernel, layers, held, capacity),
        f32(cols_x * 2 * kv, LANES),
        (weighted, profile, factors, *interp, far),
        scratch=(pltpu.VMEM((2 * wide, LANES), jnp.float32),),
        flops=400_000_000,
        mib=16,
    )
    tile = lax.all_to_all(
        spread.reshape(cols_x, 2 * kv, LANES), "gx", split_axis=0, concat_axis=0, tiled=True
    )
    pair, cross = from_neighbours(tile)
    image, sums = call(
        functools.partial(second_lateral_kernel, kv, rows, tiles),
        (f32(*direction_n.shape), f32(device_count, 1, LANES)),
        (tile, pair, cross, coef, direction_n, residual_n),
        scratch=(pltpu.VMEM(tile.shape, jnp.float32), pltpu.VMEM(tile.shape, jnp.float32)),
        flops=4_000_000,
    )
    sums = lax.all_to_all(sums, ("gy", "gx"), split_axis=0, concat_axis=0, tiled=True)
    after = call(
        update_kernel,
        (f32(*direction_n.shape),) * 3,
        (sums, direction_n, solution_n, residual_n, image),
    )
    return tuple(from_native(x, direction.shape) for x in after)


def gathers(mesh, shapes):
    rows_y, cols_x = mesh.shape["gy"], mesh.shape["gx"]
    devices = rows_y * cols_x
    if any(size < 2 or size & (size - 1) for size in (rows_y, cols_x)):
        return False
    direction, vert_coef, obs_row, error_inverse = shapes
    var_count, layers, lat_rows, lons = direction
    rows, held = lat_rows // rows_y, layers // cols_x
    obs_count, wide = obs_row[-1], error_inverse[-1]
    capacity = 2 * obs_count // devices
    return (
        rows == NSTEP == 4
        and var_count == 4
        and (var_count * held) % 8 == 0
        and lons // cols_x * 2 == LANES
        and wide == LANES
        and capacity > 0
        and LANES % capacity == 0
        and devices // 2 % (LANES // capacity) == 0
        and devices * wide * wide * 4 <= 8 * 1024 * 1024
    )


def padded(cells, sides, width):
    for axis, dim in sides:
        count = lax.axis_size(axis)
        ends = count - 1
        head = lax.slice_in_dim(cells, 0, width, axis=dim)
        tail = lax.slice_in_dim(cells, cells.shape[dim] - width, cells.shape[dim], axis=dim)
        cells = jnp.concatenate(
            [
                lax.ppermute(tail, axis, [(i, (i + 1) % count) for i in range(ends)]),
                cells,
                lax.ppermute(head, axis, [((i + 1) % count, i) for i in range(ends)]),
            ],
            axis=dim,
        )
    return cells


def lateral_faces(north_ext, east_ext, ocean_ext):
    ocean_next = jnp.concatenate([ocean_ext[1:], jnp.zeros_like(ocean_ext[:1])], axis=0)
    north_face = north_ext * ocean_ext * ocean_next
    east_face = east_ext * ocean_ext * jnp.roll(ocean_ext, -1, axis=1)
    return (north_face, east_face, ocean_ext)


def diffuse_once(values_grid, north_face, east_face, ocean_ext):
    north_flux = north_face[:-1] * (values_grid[:, :, 1:, :] - values_grid[:, :, :-1, :])
    east_flux = east_face * (jnp.roll(values_grid, -1, axis=3) - values_grid)
    lateral = east_flux - jnp.roll(east_flux, 1, axis=3)
    return (
        ocean_ext[1:-1] * values_grid[:, :, 1:-1, :]
        + north_flux[:, :, 1:, :]
        - north_flux[:, :, :-1, :]
        + lateral[:, :, 1:-1, :]
    )


def lateral_pass(values_tile, faces):
    north_face, east_face, ocean_ext = faces
    grown = padded(values_tile, (("gy", 2),), NSTEP)
    total_rows = grown.shape[2]
    for step_index in range(NSTEP):
        upper = total_rows - step_index
        grown = diffuse_once(
            grown,
            north_face[step_index:upper],
            east_face[step_index:upper],
            ocean_ext[step_index:upper],
        )
    return grown


def vertical_factors(vert_coef):
    inverse_rows = []
    upper_ratio = []
    for layer_index in range(vert_coef.shape[0]):
        diagonal = 1.0 + vert_coef[layer_index]
        if layer_index > 0:
            diagonal = (
                diagonal + vert_coef[layer_index - 1] + vert_coef[layer_index - 1] * upper_ratio[-1]
            )
        inverse = 1.0 / diagonal
        inverse_rows.append(inverse)
        upper_ratio.append(-vert_coef[layer_index] * inverse)
    return (inverse_rows, upper_ratio)


def vertical_solve(values_col, vert_coef, factors):
    inverse_rows, upper_ratio = factors
    layers = values_col.shape[1]
    forward = []
    for layer_index in range(layers):
        source = values_col[:, layer_index]
        if layer_index > 0:
            source = source + vert_coef[layer_index - 1] * forward[-1]
        forward.append(source * inverse_rows[layer_index])
    result = [forward[-1]]
    for layer_index in range(layers - 2, -1, -1):
        result.append(forward[layer_index] - upper_ratio[layer_index] * result[-1])
    return jnp.stack(result[::-1], axis=1)


def observe_weigh_spread(columns, obs_owner, obs_row, obs_col, obs_frac, error_inverse):
    var_count, lev_count, lat_rows, lon_cols = columns.shape
    kv_width = var_count * lev_count
    rows_y = lax.axis_size("gy")
    cols_x = lax.axis_size("gx")
    device_count = rows_y * cols_x
    obs_count = obs_row.shape[-1]
    capacity = 2 * obs_count // device_count
    flat = columns.reshape(kv_width, lat_rows * lon_cols)
    cell = obs_row.reshape(-1) * lon_cols + obs_col.reshape(-1)
    corners = (cell, cell + 1, cell + lon_cols, cell + lon_cols + 1)
    lat_frac = obs_frac[0, 0, 0]
    lon_frac = obs_frac[0, 0, 1]
    weights = (
        (1.0 - lat_frac) * (1.0 - lon_frac),
        (1.0 - lat_frac) * lon_frac,
        lat_frac * (1.0 - lon_frac),
        lat_frac * lon_frac,
    )
    profile = weights[0] * jnp.take(flat, corners[0], axis=1)
    for corner_index in range(1, 4):
        profile = profile + weights[corner_index] * jnp.take(flat, corners[corner_index], axis=1)
    owners = obs_owner.reshape(-1)
    onehot = (owners[:, None] == jnp.arange(device_count, dtype=jnp.int32)[None, :]).astype(
        jnp.int32
    )
    running = jnp.cumsum(onehot, axis=0)
    rank_in = jnp.sum(running * onehot, axis=1) - 1
    slot = owners * capacity + rank_in
    outgoing = jnp.zeros((device_count * capacity, kv_width), jnp.float32).at[slot].set(profile.T)
    outgoing = outgoing.reshape(rows_y, cols_x, capacity, kv_width)
    matrix = error_inverse.reshape(kv_width, kv_width)
    arrived = lax.all_to_all(
        lax.all_to_all(outgoing, "gy", split_axis=0, concat_axis=0, tiled=True),
        "gx",
        split_axis=1,
        concat_axis=1,
        tiled=True,
    )
    weighted = jnp.dot(
        arrived.reshape(-1, kv_width),
        matrix,
        precision=lax.Precision.HIGHEST,
        preferred_element_type=jnp.float32,
    ).reshape(rows_y, cols_x, capacity, kv_width)
    returned = lax.all_to_all(
        lax.all_to_all(weighted, "gy", split_axis=0, concat_axis=0, tiled=True),
        "gx",
        split_axis=1,
        concat_axis=1,
        tiled=True,
    )
    back = returned.reshape(device_count * capacity, kv_width)[slot].T
    spread = jnp.zeros((kv_width, lat_rows * lon_cols), jnp.float32)
    for corner_index in range(4):
        spread = spread.at[:, corners[corner_index]].add(weights[corner_index] * back)
    return spread.reshape(var_count, lev_count, lat_rows, lon_cols)


def per_device(
    direction,
    solution,
    residual,
    north_coef,
    east_coef,
    ocean,
    vert_coef,
    obs_owner,
    obs_row,
    obs_col,
    obs_frac,
    error_inverse,
):
    stacked = jnp.stack([north_coef, east_coef, ocean.astype(jnp.float32)])
    reach = NSTEP
    grown_coef = padded(stacked, (("gy", 1),), reach)
    faces = lateral_faces(grown_coef[0], grown_coef[1], grown_coef[2])
    factors = vertical_factors(vert_coef)
    smoothed = lateral_pass(direction, faces)
    columns = lax.all_to_all(smoothed, "gx", split_axis=3, concat_axis=1, tiled=True)
    columns = vertical_solve(columns, vert_coef, factors)
    spread = observe_weigh_spread(columns, obs_owner, obs_row, obs_col, obs_frac, error_inverse)
    spread = vertical_solve(spread, vert_coef, factors)
    tiles = lax.all_to_all(spread, "gx", split_axis=1, concat_axis=3, tiled=True)
    image = direction + lateral_pass(tiles, faces)
    norm_now, curvature = lax.psum(
        (jnp.sum(residual * residual), jnp.sum(direction * image)), ("gy", "gx")
    )
    alpha = norm_now / curvature
    residual_next = residual - alpha * image
    norm_next = lax.psum(jnp.sum(residual_next * residual_next), ("gy", "gx"))
    solution_next = solution + alpha * direction
    direction_next = residual_next + norm_next / norm_now * direction
    return (solution_next, residual_next, direction_next)


def solution(mesh):
    in_specs = (
        P(None, "gx", "gy", None),
        P(None, "gx", "gy", None),
        P(None, "gx", "gy", None),
        P("gy", None),
        P("gy", None),
        P("gy", None),
        P(None, "gy", "gx"),
        P("gy", "gx", None, None),
        P("gy", "gx", None),
        P("gy", "gx", None),
        P("gy", "gx", None, None),
        P("gy", "gx", None, None),
    )
    out_specs = (P(None, "gx", "gy", None),) * 3

    def step(*arrays):
        shapes = [arrays[at].shape for at in (0, 6, 8, 11)]
        local = per_device_gathered if gathers(mesh, shapes) else per_device
        return jax.shard_map(
            local, mesh=mesh, in_specs=in_specs, out_specs=out_specs, check_vma=False
        )(*arrays)

    return step
```

```python
import functools
import math

import jax
import jax.numpy as jnp
from jax import lax
from jax.experimental import pallas as pl
from jax.experimental.pallas import tpu as pltpu
from jax.sharding import PartitionSpec as P

NSTEP = 4
LANES = 128


def to_native(tile):
    kv, rows, lons = tile.shape[0] * tile.shape[1], tile.shape[2], tile.shape[3]
    return tile.reshape(kv, rows, lons // LANES, LANES).swapaxes(1, 2).reshape(-1, LANES)


def from_native(flat, shape):
    kv, rows, lons = shape[0] * shape[1], shape[2], shape[3]
    return flat.reshape(kv, lons // LANES, rows, LANES).swapaxes(1, 2).reshape(shape)


def native_rows(ref, base, row, rows, tiles, half):
    parts = [
        ref[pl.ds(base + (half * 8 * tiles + tile) * rows + row, 8, stride=tiles * rows), :]
        for tile in range(tiles)
    ]
    return jnp.concatenate(parts, axis=1)


def lane_low(shape):
    return lax.broadcasted_iota(jnp.int32, shape, 1) < LANES // 2


def lateral_rows(rows, coef, reach):
    for step in range(reach):
        after = []
        for i in range(1, len(rows) - 1):
            at = step + i
            u = rows[i]
            width = u.shape[1]
            after.append(
                coef[0, at : at + 1, :] * u
                + coef[1, at : at + 1, :] * rows[i + 1]
                + coef[2, at : at + 1, :] * rows[i - 1]
                + coef[3, at : at + 1, :] * pltpu.roll(u, width - 1, 1)
                + coef[4, at : at + 1, :] * pltpu.roll(u, 1, 1)
            )
        rows = after
    return rows


def sort_halo(pair_ref, cross_ref, low_ref, high_ref):
    at_y, rows_y = lax.axis_index("gy"), lax.axis_size("gy")
    odd = lax.rem(at_y, 2) == 1

    @pl.when(odd)
    def _():
        low_ref[...] = pair_ref[...]
        high_ref[...] = cross_ref[...]

    @pl.when(jnp.logical_not(odd))
    def _():
        low_ref[...] = cross_ref[...]
        high_ref[...] = pair_ref[...]

    @pl.when(at_y == 0)
    def _():
        low_ref[...] = jnp.zeros_like(low_ref)

    @pl.when(at_y == rows_y - 1)
    def _():
        high_ref[...] = jnp.zeros_like(high_ref)


def halo_kernel(chunks, direction_ref, north_ref, east_ref, ocean_ref, own_ref, stage_ref, mask_ref, sems):
    cells, size = direction_ref.shape[0], north_ref.shape[0]
    rows = cells // chunks
    spans = [(direction_ref.at[pl.ds(at * rows, rows)], at * rows, rows) for at in range(chunks)]
    spans += [(north_ref, cells, size), (east_ref, cells + size, size)]
    arrive = [
        pltpu.make_async_copy(source, stage_ref.at[pl.ds(start, count)], sems.at[0, at])
        for at, (source, start, count) in enumerate(spans)
    ]
    arrive.append(pltpu.make_async_copy(ocean_ref, mask_ref, sems.at[0, len(spans)]))
    spans.append((ocean_ref, cells + 2 * size, size))
    leave = [
        pltpu.make_async_copy(
            stage_ref.at[pl.ds(start, count)], own_ref.at[pl.ds(start, count)], sems.at[1, at]
        )
        for at, (_, start, count) in enumerate(spans)
    ]
    for copy in arrive:
        copy.start()
    for at, copy in enumerate(arrive):
        copy.wait()
        if at == len(arrive) - 1:
            stage_ref[cells + 2 * size : cells + 3 * size, :] = mask_ref[...].astype(jnp.float32)
        leave[at].start()
    for copy in leave:
        copy.wait()


def join_kernel(after, count, *refs):
    blocks, (near_ref,) = refs[after : after + count], refs[after + count :]
    size = blocks[0].shape[0]
    for at, block in enumerate(blocks):
        near_ref[at * size : (at + 1) * size] = block[...]


def first_lateral_kernel(
    kv,
    rows,
    tiles,
    _,
    own_ref,
    north_ref,
    east_ref,
    ocean_ref,
    pair_ref,
    cross_ref,
    packed_ref,
    coef_ref,
    ext_ref,
    low_ref,
    high_ref,
):
    lons = tiles * LANES
    cells = kv * tiles * rows
    sort_halo(pair_ref, cross_ref, low_ref, high_ref)
    ext_ref[...] = jnp.zeros_like(ext_ref)
    for kind, kept in enumerate((north_ref, east_ref, ocean_ref)):
        for tile in range(tiles):
            lanes = slice(tile * LANES, (tile + 1) * LANES)
            start = cells + (kind * tiles + tile) * rows
            ext_ref[kind, 0:rows, lanes] = low_ref[start : start + rows, :]
            ext_ref[kind, rows : 2 * rows, lanes] = kept[tile * rows : (tile + 1) * rows, :].astype(jnp.float32)
            ext_ref[kind, 2 * rows : 3 * rows, lanes] = high_ref[start : start + rows, :]
    total = ext_ref.shape[1]
    north, east, ocean = ext_ref[0], ext_ref[1], ext_ref[2]
    north_face = north * ocean * pltpu.roll(ocean, total - 1, 0)
    east_face = east * ocean * pltpu.roll(ocean, lons - 1, 1)
    south_face = pltpu.roll(north_face, 1, 0)
    west_face = pltpu.roll(east_face, 1, 1)
    coef_ref[0] = ocean - north_face - south_face - east_face - west_face
    coef_ref[1] = north_face
    coef_ref[2] = south_face
    coef_ref[3] = east_face
    coef_ref[4] = west_face
    low = lane_low((8, LANES))
    for half in range(kv // 8):
        grown = [
            native_rows(ref, 0, row, rows, tiles, half)
            for ref in (low_ref, own_ref, high_ref)
            for row in range(rows)
        ]
        done = lateral_rows(grown, coef_ref, rows)
        for pair in range(rows // 2):
            for tile in range(tiles):
                first = done[2 * pair][:, tile * LANES : (tile + 1) * LANES]
                second = done[2 * pair + 1][:, tile * LANES : (tile + 1) * LANES]
                at = pair * kv + half * 8
                packed_ref[2 * tile, at : at + 8, :] = jnp.where(
                    low, first, pltpu.roll(second, LANES // 2, 1)
                )
                packed_ref[2 * tile + 1, at : at + 8, :] = jnp.where(
                    low, pltpu.roll(first, LANES // 2, 1), second
                )


def second_lateral_kernel(
    kv,
    rows,
    tiles,
    own_ref,
    pair_ref,
    cross_ref,
    coef_ref,
    direction_ref,
    residual_ref,
    image_ref,
    sums_ref,
    low_ref,
    high_ref,
):
    sort_halo(pair_ref, cross_ref, low_ref, high_ref)
    low = lane_low((8, LANES))
    totals = [jnp.zeros((8, tiles * LANES), jnp.float32) for _ in range(4)]
    for half in range(kv // 8):
        grown = []
        for ref in (low_ref, own_ref, high_ref):
            for pair in range(rows // 2):
                firsts, seconds = [], []
                at = pair * kv + half * 8
                for tile in range(tiles):
                    even = ref[2 * tile, at : at + 8, :]
                    odd = ref[2 * tile + 1, at : at + 8, :]
                    firsts.append(jnp.where(low, even, pltpu.roll(odd, LANES // 2, 1)))
                    seconds.append(jnp.where(low, pltpu.roll(even, LANES // 2, 1), odd))
                grown.append(jnp.concatenate(firsts, axis=1))
                grown.append(jnp.concatenate(seconds, axis=1))
        done = lateral_rows(grown, coef_ref, rows)
        for row in range(rows):
            direction = native_rows(direction_ref, 0, row, rows, tiles, half)
            residual = native_rows(residual_ref, 0, row, rows, tiles, half)
            image = direction + done[row]
            for tile in range(tiles):
                image_ref[pl.ds((half * 8 * tiles + tile) * rows + row, 8, stride=tiles * rows), :] = image[
                    :, tile * LANES : (tile + 1) * LANES
                ]
            totals[0] = totals[0] + residual * residual
            totals[1] = totals[1] + direction * image
            totals[2] = totals[2] + residual * image
            totals[3] = totals[3] + image * image
    lane = lax.broadcasted_iota(jnp.int32, (1, LANES), 1)
    line = jnp.zeros((1, LANES), jnp.float32)
    for at, total in enumerate(totals):
        line = jnp.where(lane == at, jnp.sum(total), line)
    for device in range(sums_ref.shape[0]):
        sums_ref[device] = line


def update_kernel(sums_ref, direction_ref, solution_ref, residual_ref, image_ref, sol_ref, res_ref, dir_ref):
    line = jnp.sum(sums_ref[...], axis=0)
    lane = lax.broadcasted_iota(jnp.int32, line.shape, 1)

    def pick(at):
        return jnp.sum(jnp.where(lane == at, line, 0.0), axis=1, keepdims=True)

    norm_now, curvature, cross, square = pick(0), pick(1), pick(2), pick(3)
    alpha = norm_now / curvature
    norm_next = norm_now - 2.0 * alpha * cross + alpha * alpha * square
    beta = norm_next / norm_now
    direction = direction_ref[...]
    residual_next = residual_ref[...] - alpha * image_ref[...]
    sol_ref[...] = solution_ref[...] + alpha * direction
    res_ref[...] = residual_next
    dir_ref[...] = residual_next + beta * direction


def split(value):
    high = value.astype(jnp.bfloat16)
    return high, (value - high.astype(jnp.float32)).astype(jnp.bfloat16)


def dot_parts(left, right, contract):
    dims = (contract, ((), ()))
    total = lax.dot_general(left[0], right[0], dims, preferred_element_type=jnp.float32)
    total = total + lax.dot_general(left[0], right[1], dims, preferred_element_type=jnp.float32)
    return total + lax.dot_general(left[1], right[0], dims, preferred_element_type=jnp.float32)


def prepare_kernel(
    devices,
    capacity,
    lon_cols,
    vert_ref,
    owner_ref,
    row_ref,
    col_ref,
    frac_ref,
    factor_ref,
    high_ref,
    low_ref,
):
    vertical_factors_of(vert_ref, factor_ref)
    count = owner_ref.shape[1]
    slots = devices * capacity
    me = lax.axis_index("gy") * lax.axis_size("gx") + lax.axis_index("gx")
    apart = jnp.bitwise_xor(owner_ref[...], me)
    place = jnp.bitwise_and(apart, 1) * (devices // 2) + jnp.right_shift(apart, 1)
    named = lax.broadcasted_iota(jnp.int32, (devices, count), 0) == place
    before = lax.broadcasted_iota(jnp.int32, (count, count), 0) <= lax.broadcasted_iota(
        jnp.int32, (count, count), 1
    )
    running = jnp.dot(
        jnp.where(named, 1.0, 0.0).astype(jnp.bfloat16),
        jnp.where(before, 1.0, 0.0).astype(jnp.bfloat16),
        preferred_element_type=jnp.float32,
    )
    rank = jnp.sum(jnp.where(named, running, 0.0), axis=0, keepdims=True) - 1.0
    slot = place * capacity + rank.astype(jnp.int32)
    chosen = jnp.where(
        lax.broadcasted_iota(jnp.int32, (slots, count), 0) == slot, 1.0, 0.0
    ).astype(jnp.bfloat16)
    lat_frac = frac_ref[0:1, :]
    lon_frac = frac_ref[1:2, :]
    cell = (row_ref[...] * lon_cols + col_ref[...]).astype(jnp.float32)
    values = jnp.concatenate(
        [
            (1.0 - lat_frac) * (1.0 - lon_frac),
            (1.0 - lat_frac) * lon_frac,
            lat_frac * (1.0 - lon_frac),
            lat_frac * lon_frac,
            cell,
            jnp.zeros((3, count), jnp.float32),
        ],
        axis=0,
    )
    high, rest = split(values)
    low, rest = split(values - high.astype(jnp.float32))
    parts = jnp.concatenate([high.astype(jnp.float32), low.astype(jnp.float32), rest.astype(jnp.float32)], axis=0)
    placed = lax.dot_general(
        parts.astype(jnp.bfloat16), chosen, (((1,), (1,)), ((), ())), preferred_element_type=jnp.float32
    )
    placed = placed[0:8] + placed[8:16] + placed[16:24]
    first = jnp.round(placed[4:5, :]).astype(jnp.int32)
    away = lax.broadcasted_iota(jnp.int32, high_ref.shape, 0) - first
    interp = jnp.where(
        away == 0,
        placed[0:1, :],
        jnp.where(
            away == 1,
            placed[1:2, :],
            jnp.where(away == lon_cols, placed[2:3, :], jnp.where(away == lon_cols + 1, placed[3:4, :], 0.0)),
        ),
    )
    high_ref[...], low_ref[...] = split(interp)


def vertical_factors_of(vert_ref, factor_ref):
    layers = vert_ref.shape[0]
    top = lax.broadcasted_iota(jnp.int32, (8, LANES), 0) < 4
    coef = [jnp.where(top, vert_ref[layer, 0:1, :], vert_ref[layer, 1:2, :]) for layer in range(layers)]
    ratio = None
    for layer in range(layers):
        diagonal = 1.0 + coef[layer]
        if layer > 0:
            diagonal = diagonal + coef[layer - 1] - coef[layer - 1] * ratio
        inverse = 1.0 / diagonal
        ratio = coef[layer] * inverse
        factor_ref[0, layer] = inverse
        factor_ref[1, layer] = coef[layer - 1] * inverse if layer > 0 else jnp.zeros_like(inverse)
        factor_ref[2, layer] = ratio


def solve_columns(read, write, factor_ref, layers):
    forward = []
    for layer in range(layers):
        value = read(layer) * factor_ref[0, layer]
        if layer > 0:
            value = value + factor_ref[1, layer] * forward[-1]
        forward.append(value)
    value = forward[-1]
    write(layers - 1, value)
    for layer in range(layers - 2, -1, -1):
        value = forward[layer] + factor_ref[2, layer] * value
        write(layer, value)


def packed_at(layer, held):
    return pl.ds((layer // held) * 8 * held + layer % held, 8, stride=held)


def weigh(profile, matrix_ref, capacity):
    kv = matrix_ref.shape[1]
    owners = LANES // capacity
    mine = lax.broadcasted_iota(jnp.int32, (kv, LANES), 1) // capacity
    tiles = []
    for tile in range(matrix_ref.shape[0] // owners):
        values = profile[:, tile * LANES : (tile + 1) * LANES]
        masked = jnp.concatenate([jnp.where(mine == owner, values, 0.0) for owner in range(owners)], axis=0)
        matrices = jnp.concatenate([matrix_ref[tile * owners + owner] for owner in range(owners)], axis=1)
        tiles.append(dot_parts(split(matrices), split(masked), ((1,), (0,))))
    return jnp.concatenate(tiles, axis=1)


def smooth_kernel(layers, held, packed_ref, factor_ref, column_ref):
    def read(layer):
        return packed_ref[packed_at(layer, held), :]

    def write(layer, value):
        column_ref[pl.ds(layer, 8, stride=layers), :] = value

    solve_columns(read, write, factor_ref, layers)


def profile_kernel(capacity, column_ref, high_ref, low_ref, near_ref, weighted_ref, profile_ref):
    kv = profile_ref.shape[0]
    half = profile_ref.shape[1]
    columns = jnp.concatenate([column_ref[0:kv, :], column_ref[kv : 2 * kv, :]], axis=1)
    profile = dot_parts(split(columns), (high_ref[...], low_ref[...]), ((1,), (0,)))
    profile_ref[...] = profile[:, half:]
    weighted_ref[...] = weigh(profile[:, :half], near_ref, capacity)


def spread_kernel(
    layers, held, capacity, near_ref, profile_ref, factor_ref, high_ref, low_ref, far_ref, out_ref, column_ref
):
    kv = near_ref.shape[0]
    weighted = jnp.concatenate([near_ref[...], weigh(profile_ref[...], far_ref, capacity)], axis=1)
    spread = dot_parts(split(weighted), (high_ref[...], low_ref[...]), ((1,), (1,)))
    column_ref[0:kv, :] = spread[:, :LANES]
    column_ref[kv : 2 * kv, :] = spread[:, LANES:]

    def read(layer):
        return column_ref[pl.ds(layer, 8, stride=layers), :]

    def write(layer, value):
        out_ref[packed_at(layer, held), :] = value

    solve_columns(read, write, factor_ref, layers)


def vmem(count):
    return [pl.BlockSpec(memory_space=pltpu.VMEM)] * count


def call(kernel, out_shape, inputs, scratch=(), after=0, hbm=False, flops=1_000_000, mib=8):
    specs = [pl.BlockSpec(memory_space=pl.ANY)] * after + vmem(len(inputs) - after)
    outs = vmem(len(out_shape) if isinstance(out_shape, tuple) else 1)
    if hbm:
        specs, outs = ([pl.BlockSpec(memory_space=pltpu.HBM)] * len(x) for x in (specs, outs))
    moved = sum(math.prod(x.shape) * 4 for x in inputs)
    return pl.pallas_call(
        kernel,
        out_shape=out_shape,
        in_specs=specs,
        out_specs=tuple(outs) if isinstance(out_shape, tuple) else outs[0],
        scratch_shapes=list(scratch),
        compiler_params=pltpu.CompilerParams(vmem_limit_bytes=mib * 1024 * 1024),
        cost_estimate=pl.CostEstimate(flops=flops, bytes_accessed=moved, transcendentals=0),
    )(*inputs)


def f32(*shape):
    return jax.ShapeDtypeStruct(shape, jnp.float32)


def from_neighbours(block):
    count = lax.axis_size("gy")
    pair = lax.ppermute(block, "gy", [(i, i ^ 1) for i in range(count)])
    cross = lax.ppermute(block, "gy", [(i, (i + (1 if i % 2 else -1)) % count) for i in range(count)])
    return pair, cross


def apart_by(block, axis, stride):
    return lax.ppermute(block, axis, [(i, i ^ stride) for i in range(lax.axis_size(axis))])


def per_device_gathered(
    direction,
    solution,
    residual,
    north_coef,
    east_coef,
    ocean,
    vert_coef,
    obs_owner,
    obs_row,
    obs_col,
    obs_frac,
    error_inverse,
):
    var_count, held, rows, lons = direction.shape
    kv = var_count * held
    tiles = lons // LANES
    layers, _, lon_cols = vert_coef.shape
    rows_y, cols_x = lax.axis_size("gy"), lax.axis_size("gx")
    device_count = rows_y * cols_x
    obs_count = obs_row.shape[-1]
    capacity = 2 * obs_count // device_count
    wide = error_inverse.shape[-1]
    cells = rows * lon_cols

    direction_n = to_native(direction)
    residual_n = to_native(residual)
    solution_n = to_native(solution)
    faces = [to_native(x[None, None]) for x in (north_coef, east_coef, ocean)]
    own = call(
        functools.partial(halo_kernel, 4),
        f32(direction_n.shape[0] + 3 * faces[0].shape[0], LANES),
        (direction_n, *faces),
        scratch=(
            pltpu.VMEM((direction_n.shape[0] + 3 * faces[0].shape[0], LANES), jnp.float32),
            pltpu.VMEM(faces[0].shape, jnp.int32),
            pltpu.SemaphoreType.DMA((2, 7)),
        ),
        hbm=True,
        mib=56,
    )
    pair, cross = from_neighbours(own)

    matrix = error_inverse.reshape(1, wide, wide)
    blocks = [matrix] + [apart_by(matrix, "gx", stride) for stride in range(2, cols_x, 2)]
    halves = jax.ShapeDtypeStruct((cells, device_count * capacity), jnp.bfloat16)
    factors, *interp = call(
        functools.partial(prepare_kernel, device_count, capacity, lon_cols),
        (f32(3, layers, 8, LANES), halves, halves),
        (
            vert_coef.reshape(layers, cells // LANES, LANES),
            obs_owner.reshape(1, obs_count),
            obs_row.reshape(1, obs_count),
            obs_col.reshape(1, obs_count),
            obs_frac.reshape(2, obs_count),
        ),
        flops=20_000_000,
        mib=16,
    )
    held_blocks = call(
        functools.partial(join_kernel, 1, len(blocks)),
        f32(len(blocks), wide, wide),
        (interp[0], *blocks),
        after=1,
    )

    extended = 3 * rows + (-3 * rows) % 8
    packed, coef = call(
        functools.partial(first_lateral_kernel, kv, rows, tiles),
        (f32(cols_x, 2 * kv, LANES), f32(5, extended, lons)),
        (held_blocks, direction_n, *faces, pair, cross),
        after=1,
        scratch=(
            pltpu.VMEM((3, extended, lons), jnp.float32),
            pltpu.VMEM(own.shape, jnp.float32),
            pltpu.VMEM(own.shape, jnp.float32),
        ),
        flops=4_000_000,
    )
    fetched = [held_blocks] + [apart_by(held_blocks, "gy", stride) for stride in range(1, rows_y)]
    columns = lax.all_to_all(packed, "gx", split_axis=0, concat_axis=0, tiled=True)
    smoothed = call(
        functools.partial(smooth_kernel, layers, held),
        f32(2 * wide, LANES),
        (columns.reshape(cols_x * 2 * kv, LANES), factors),
        flops=400_000_000,
    )
    near = call(
        functools.partial(join_kernel, 1, len(fetched)),
        f32(device_count // 2, wide, wide),
        (smoothed, *fetched),
        after=1,
    )
    far = apart_by(near, "gx", 1)
    half = device_count // 2 * capacity
    weighted, profile = call(
        functools.partial(profile_kernel, capacity),
        (f32(wide, half), f32(wide, half)),
        (smoothed, *interp, near),
        flops=400_000_000,
        mib=16,
    )
    spread = call(
        functools.partial(spread_kernel, layers, held, capacity),
        f32(cols_x * 2 * kv, LANES),
        (weighted, profile, factors, *interp, far),
        scratch=(pltpu.VMEM((2 * wide, LANES), jnp.float32),),
        flops=400_000_000,
        mib=16,
    )
    tile = lax.all_to_all(
        spread.reshape(cols_x, 2 * kv, LANES), "gx", split_axis=0, concat_axis=0, tiled=True
    )
    pair, cross = from_neighbours(tile)
    image, sums = call(
        functools.partial(second_lateral_kernel, kv, rows, tiles),
        (f32(*direction_n.shape), f32(device_count, 1, LANES)),
        (tile, pair, cross, coef, direction_n, residual_n),
        scratch=(pltpu.VMEM(tile.shape, jnp.float32), pltpu.VMEM(tile.shape, jnp.float32)),
        flops=4_000_000,
    )
    sums = lax.all_to_all(sums, ("gy", "gx"), split_axis=0, concat_axis=0, tiled=True)
    after = call(
        update_kernel,
        (f32(*direction_n.shape),) * 3,
        (sums, direction_n, solution_n, residual_n, image),
    )
    return tuple(from_native(x, direction.shape) for x in after)


def gathers(mesh, shapes):
    rows_y, cols_x = mesh.shape["gy"], mesh.shape["gx"]
    devices = rows_y * cols_x
    if any(size < 2 or size & (size - 1) for size in (rows_y, cols_x)):
        return False
    direction, vert_coef, obs_row, error_inverse = shapes
    var_count, layers, lat_rows, lons = direction
    rows, held = lat_rows // rows_y, layers // cols_x
    obs_count, wide = obs_row[-1], error_inverse[-1]
    capacity = 2 * obs_count // devices
    return (
        rows == NSTEP == 4
        and var_count == 4
        and (var_count * held) % 8 == 0
        and lons // cols_x * 2 == LANES
        and wide == LANES
        and capacity > 0
        and LANES % capacity == 0
        and devices // 2 % (LANES // capacity) == 0
        and devices * wide * wide * 4 <= 8 * 1024 * 1024
    )


def padded(cells, sides, width):
    for axis, dim in sides:
        count = lax.axis_size(axis)
        ends = count - 1
        head = lax.slice_in_dim(cells, 0, width, axis=dim)
        tail = lax.slice_in_dim(cells, cells.shape[dim] - width, cells.shape[dim], axis=dim)
        cells = jnp.concatenate(
            [
                lax.ppermute(tail, axis, [(i, (i + 1) % count) for i in range(ends)]),
                cells,
                lax.ppermute(head, axis, [((i + 1) % count, i) for i in range(ends)]),
            ],
            axis=dim,
        )
    return cells


def lateral_faces(north_ext, east_ext, ocean_ext):
    ocean_next = jnp.concatenate([ocean_ext[1:], jnp.zeros_like(ocean_ext[:1])], axis=0)
    north_face = north_ext * ocean_ext * ocean_next
    east_face = east_ext * ocean_ext * jnp.roll(ocean_ext, -1, axis=1)
    return (north_face, east_face, ocean_ext)


def diffuse_once(values_grid, north_face, east_face, ocean_ext):
    north_flux = north_face[:-1] * (values_grid[:, :, 1:, :] - values_grid[:, :, :-1, :])
    east_flux = east_face * (jnp.roll(values_grid, -1, axis=3) - values_grid)
    lateral = east_flux - jnp.roll(east_flux, 1, axis=3)
    return (
        ocean_ext[1:-1] * values_grid[:, :, 1:-1, :]
        + north_flux[:, :, 1:, :]
        - north_flux[:, :, :-1, :]
        + lateral[:, :, 1:-1, :]
    )


def lateral_pass(values_tile, faces):
    north_face, east_face, ocean_ext = faces
    grown = padded(values_tile, (("gy", 2),), NSTEP)
    total_rows = grown.shape[2]
    for step_index in range(NSTEP):
        upper = total_rows - step_index
        grown = diffuse_once(
            grown,
            north_face[step_index:upper],
            east_face[step_index:upper],
            ocean_ext[step_index:upper],
        )
    return grown


def vertical_factors(vert_coef):
    inverse_rows = []
    upper_ratio = []
    for layer_index in range(vert_coef.shape[0]):
        diagonal = 1.0 + vert_coef[layer_index]
        if layer_index > 0:
            diagonal = (
                diagonal + vert_coef[layer_index - 1] + vert_coef[layer_index - 1] * upper_ratio[-1]
            )
        inverse = 1.0 / diagonal
        inverse_rows.append(inverse)
        upper_ratio.append(-vert_coef[layer_index] * inverse)
    return (inverse_rows, upper_ratio)


def vertical_solve(values_col, vert_coef, factors):
    inverse_rows, upper_ratio = factors
    layers = values_col.shape[1]
    forward = []
    for layer_index in range(layers):
        source = values_col[:, layer_index]
        if layer_index > 0:
            source = source + vert_coef[layer_index - 1] * forward[-1]
        forward.append(source * inverse_rows[layer_index])
    result = [forward[-1]]
    for layer_index in range(layers - 2, -1, -1):
        result.append(forward[layer_index] - upper_ratio[layer_index] * result[-1])
    return jnp.stack(result[::-1], axis=1)


def observe_weigh_spread(columns, obs_owner, obs_row, obs_col, obs_frac, error_inverse):
    var_count, lev_count, lat_rows, lon_cols = columns.shape
    kv_width = var_count * lev_count
    rows_y = lax.axis_size("gy")
    cols_x = lax.axis_size("gx")
    device_count = rows_y * cols_x
    obs_count = obs_row.shape[-1]
    capacity = 2 * obs_count // device_count
    flat = columns.reshape(kv_width, lat_rows * lon_cols)
    cell = obs_row.reshape(-1) * lon_cols + obs_col.reshape(-1)
    corners = (cell, cell + 1, cell + lon_cols, cell + lon_cols + 1)
    lat_frac = obs_frac[0, 0, 0]
    lon_frac = obs_frac[0, 0, 1]
    weights = (
        (1.0 - lat_frac) * (1.0 - lon_frac),
        (1.0 - lat_frac) * lon_frac,
        lat_frac * (1.0 - lon_frac),
        lat_frac * lon_frac,
    )
    profile = weights[0] * jnp.take(flat, corners[0], axis=1)
    for corner_index in range(1, 4):
        profile = profile + weights[corner_index] * jnp.take(flat, corners[corner_index], axis=1)
    owners = obs_owner.reshape(-1)
    onehot = (owners[:, None] == jnp.arange(device_count, dtype=jnp.int32)[None, :]).astype(
        jnp.int32
    )
    running = jnp.cumsum(onehot, axis=0)
    rank_in = jnp.sum(running * onehot, axis=1) - 1
    slot = owners * capacity + rank_in
    outgoing = jnp.zeros((device_count * capacity, kv_width), jnp.float32).at[slot].set(profile.T)
    outgoing = outgoing.reshape(rows_y, cols_x, capacity, kv_width)
    matrix = error_inverse.reshape(kv_width, kv_width)
    arrived = lax.all_to_all(
        lax.all_to_all(outgoing, "gy", split_axis=0, concat_axis=0, tiled=True),
        "gx",
        split_axis=1,
        concat_axis=1,
        tiled=True,
    )
    weighted = jnp.dot(
        arrived.reshape(-1, kv_width),
        matrix,
        precision=lax.Precision.HIGHEST,
        preferred_element_type=jnp.float32,
    ).reshape(rows_y, cols_x, capacity, kv_width)
    returned = lax.all_to_all(
        lax.all_to_all(weighted, "gy", split_axis=0, concat_axis=0, tiled=True),
        "gx",
        split_axis=1,
        concat_axis=1,
        tiled=True,
    )
    back = returned.reshape(device_count * capacity, kv_width)[slot].T
    spread = jnp.zeros((kv_width, lat_rows * lon_cols), jnp.float32)
    for corner_index in range(4):
        spread = spread.at[:, corners[corner_index]].add(weights[corner_index] * back)
    return spread.reshape(var_count, lev_count, lat_rows, lon_cols)


def per_device(
    direction,
    solution,
    residual,
    north_coef,
    east_coef,
    ocean,
    vert_coef,
    obs_owner,
    obs_row,
    obs_col,
    obs_frac,
    error_inverse,
):
    stacked = jnp.stack([north_coef, east_coef, ocean.astype(jnp.float32)])
    reach = NSTEP
    grown_coef = padded(stacked, (("gy", 1),), reach)
    faces = lateral_faces(grown_coef[0], grown_coef[1], grown_coef[2])
    factors = vertical_factors(vert_coef)
    smoothed = lateral_pass(direction, faces)
    columns = lax.all_to_all(smoothed, "gx", split_axis=3, concat_axis=1, tiled=True)
    columns = vertical_solve(columns, vert_coef, factors)
    spread = observe_weigh_spread(columns, obs_owner, obs_row, obs_col, obs_frac, error_inverse)
    spread = vertical_solve(spread, vert_coef, factors)
    tiles = lax.all_to_all(spread, "gx", split_axis=1, concat_axis=3, tiled=True)
    image = direction + lateral_pass(tiles, faces)
    norm_now, curvature = lax.psum(
        (jnp.sum(residual * residual), jnp.sum(direction * image)), ("gy", "gx")
    )
    alpha = norm_now / curvature
    residual_next = residual - alpha * image
    norm_next = lax.psum(jnp.sum(residual_next * residual_next), ("gy", "gx"))
    solution_next = solution + alpha * direction
    direction_next = residual_next + norm_next / norm_now * direction
    return (solution_next, residual_next, direction_next)


def solution(mesh):
    in_specs = (
        P(None, "gx", "gy", None),
        P(None, "gx", "gy", None),
        P(None, "gx", "gy", None),
        P("gy", None),
        P("gy", None),
        P("gy", None),
        P(None, "gy", "gx"),
        P("gy", "gx", None, None),
        P("gy", "gx", None),
        P("gy", "gx", None),
        P("gy", "gx", None, None),
        P("gy", "gx", None, None),
    )
    out_specs = (P(None, "gx", "gy", None),) * 3

    def step(*arrays):
        shapes = [arrays[at].shape for at in (0, 6, 8, 11)]
        local = per_device_gathered if gathers(mesh, shapes) else per_device
        return jax.shard_map(
            local, mesh=mesh, in_specs=in_specs, out_specs=out_specs, check_vma=False
        )(*arrays)

    return step
```

```python
import functools
import math

import jax
import jax.numpy as jnp
from jax import lax
from jax.experimental import pallas as pl
from jax.experimental.pallas import tpu as pltpu
from jax.sharding import PartitionSpec as P

NSTEP = 4
LANES = 128


def to_native(tile):
    kv, rows, lons = tile.shape[0] * tile.shape[1], tile.shape[2], tile.shape[3]
    return tile.reshape(kv, rows, lons // LANES, LANES).swapaxes(1, 2).reshape(-1, LANES)


def from_native(flat, shape):
    kv, rows, lons = shape[0] * shape[1], shape[2], shape[3]
    return flat.reshape(kv, lons // LANES, rows, LANES).swapaxes(1, 2).reshape(shape)


def native_rows(ref, base, row, rows, tiles, half):
    parts = [
        ref[pl.ds(base + (half * 8 * tiles + tile) * rows + row, 8, stride=tiles * rows), :]
        for tile in range(tiles)
    ]
    return jnp.concatenate(parts, axis=1)


def lane_low(shape):
    return lax.broadcasted_iota(jnp.int32, shape, 1) < LANES // 2


def lateral_rows(rows, coef, reach):
    for step in range(reach):
        after = []
        for i in range(1, len(rows) - 1):
            at = step + i
            u = rows[i]
            width = u.shape[1]
            after.append(
                coef[0, at : at + 1, :] * u
                + coef[1, at : at + 1, :] * rows[i + 1]
                + coef[2, at : at + 1, :] * rows[i - 1]
                + coef[3, at : at + 1, :] * pltpu.roll(u, width - 1, 1)
                + coef[4, at : at + 1, :] * pltpu.roll(u, 1, 1)
            )
        rows = after
    return rows


def sort_halo(pair_ref, cross_ref, low_ref, high_ref):
    at_y, rows_y = lax.axis_index("gy"), lax.axis_size("gy")
    odd = lax.rem(at_y, 2) == 1

    @pl.when(odd)
    def _():
        low_ref[...] = pair_ref[...]
        high_ref[...] = cross_ref[...]

    @pl.when(jnp.logical_not(odd))
    def _():
        low_ref[...] = cross_ref[...]
        high_ref[...] = pair_ref[...]

    @pl.when(at_y == 0)
    def _():
        low_ref[...] = jnp.zeros_like(low_ref)

    @pl.when(at_y == rows_y - 1)
    def _():
        high_ref[...] = jnp.zeros_like(high_ref)


def halo_kernel(chunks, direction_ref, north_ref, east_ref, ocean_ref, own_ref, stage_ref, mask_ref, sems):
    cells, size = direction_ref.shape[0], north_ref.shape[0]
    rows = cells // chunks
    spans = [(direction_ref.at[pl.ds(at * rows, rows)], at * rows, rows) for at in range(chunks)]
    spans += [(north_ref, cells, size), (east_ref, cells + size, size)]
    arrive = [
        pltpu.make_async_copy(source, stage_ref.at[pl.ds(start, count)], sems.at[0, at])
        for at, (source, start, count) in enumerate(spans)
    ]
    arrive.append(pltpu.make_async_copy(ocean_ref, mask_ref, sems.at[0, len(spans)]))
    spans.append((ocean_ref, cells + 2 * size, size))
    leave = [
        pltpu.make_async_copy(
            stage_ref.at[pl.ds(start, count)], own_ref.at[pl.ds(start, count)], sems.at[1, at]
        )
        for at, (_, start, count) in enumerate(spans)
    ]
    for copy in arrive:
        copy.start()
    for at, copy in enumerate(arrive):
        copy.wait()
        if at == len(arrive) - 1:
            stage_ref[cells + 2 * size : cells + 3 * size, :] = mask_ref[...].astype(jnp.float32)
        leave[at].start()
    for copy in leave:
        copy.wait()


def join_kernel(after, count, *refs):
    blocks, (near_ref,) = refs[after : after + count], refs[after + count :]
    size = blocks[0].shape[0]
    for at, block in enumerate(blocks):
        near_ref[at * size : (at + 1) * size] = block[...]


def first_lateral_kernel(
    kv,
    rows,
    tiles,
    _,
    own_ref,
    north_ref,
    east_ref,
    ocean_ref,
    pair_ref,
    cross_ref,
    packed_ref,
    coef_ref,
    ext_ref,
    low_ref,
    high_ref,
):
    lons = tiles * LANES
    cells = kv * tiles * rows
    sort_halo(pair_ref, cross_ref, low_ref, high_ref)
    ext_ref[...] = jnp.zeros_like(ext_ref)
    for kind, kept in enumerate((north_ref, east_ref, ocean_ref)):
        for tile in range(tiles):
            lanes = slice(tile * LANES, (tile + 1) * LANES)
            start = cells + (kind * tiles + tile) * rows
            ext_ref[kind, 0:rows, lanes] = low_ref[start : start + rows, :]
            ext_ref[kind, rows : 2 * rows, lanes] = kept[tile * rows : (tile + 1) * rows, :].astype(jnp.float32)
            ext_ref[kind, 2 * rows : 3 * rows, lanes] = high_ref[start : start + rows, :]
    total = ext_ref.shape[1]
    north, east, ocean = ext_ref[0], ext_ref[1], ext_ref[2]
    north_face = north * ocean * pltpu.roll(ocean, total - 1, 0)
    east_face = east * ocean * pltpu.roll(ocean, lons - 1, 1)
    south_face = pltpu.roll(north_face, 1, 0)
    west_face = pltpu.roll(east_face, 1, 1)
    coef_ref[0] = ocean - north_face - south_face - east_face - west_face
    coef_ref[1] = north_face
    coef_ref[2] = south_face
    coef_ref[3] = east_face
    coef_ref[4] = west_face
    low = lane_low((8, LANES))
    for half in range(kv // 8):
        grown = [
            native_rows(ref, 0, row, rows, tiles, half)
            for ref in (low_ref, own_ref, high_ref)
            for row in range(rows)
        ]
        done = lateral_rows(grown, coef_ref, rows)
        for pair in range(rows // 2):
            for tile in range(tiles):
                first = done[2 * pair][:, tile * LANES : (tile + 1) * LANES]
                second = done[2 * pair + 1][:, tile * LANES : (tile + 1) * LANES]
                at = pair * kv + half * 8
                packed_ref[2 * tile, at : at + 8, :] = jnp.where(
                    low, first, pltpu.roll(second, LANES // 2, 1)
                )
                packed_ref[2 * tile + 1, at : at + 8, :] = jnp.where(
                    low, pltpu.roll(first, LANES // 2, 1), second
                )


def second_lateral_kernel(
    kv,
    rows,
    tiles,
    own_ref,
    pair_ref,
    cross_ref,
    coef_ref,
    direction_ref,
    residual_ref,
    image_ref,
    sums_ref,
    low_ref,
    high_ref,
):
    sort_halo(pair_ref, cross_ref, low_ref, high_ref)
    low = lane_low((8, LANES))
    totals = [jnp.zeros((8, tiles * LANES), jnp.float32) for _ in range(4)]
    for half in range(kv // 8):
        grown = []
        for ref in (low_ref, own_ref, high_ref):
            for pair in range(rows // 2):
                firsts, seconds = [], []
                at = pair * kv + half * 8
                for tile in range(tiles):
                    even = ref[2 * tile, at : at + 8, :]
                    odd = ref[2 * tile + 1, at : at + 8, :]
                    firsts.append(jnp.where(low, even, pltpu.roll(odd, LANES // 2, 1)))
                    seconds.append(jnp.where(low, pltpu.roll(even, LANES // 2, 1), odd))
                grown.append(jnp.concatenate(firsts, axis=1))
                grown.append(jnp.concatenate(seconds, axis=1))
        done = lateral_rows(grown, coef_ref, rows)
        for row in range(rows):
            direction = native_rows(direction_ref, 0, row, rows, tiles, half)
            residual = native_rows(residual_ref, 0, row, rows, tiles, half)
            image = direction + done[row]
            for tile in range(tiles):
                image_ref[pl.ds((half * 8 * tiles + tile) * rows + row, 8, stride=tiles * rows), :] = image[
                    :, tile * LANES : (tile + 1) * LANES
                ]
            totals[0] = totals[0] + residual * residual
            totals[1] = totals[1] + direction * image
            totals[2] = totals[2] + residual * image
            totals[3] = totals[3] + image * image
    lane = lax.broadcasted_iota(jnp.int32, (1, LANES), 1)
    line = jnp.zeros((1, LANES), jnp.float32)
    for at, total in enumerate(totals):
        line = jnp.where(lane == at, jnp.sum(total), line)
    for device in range(sums_ref.shape[0]):
        sums_ref[device] = line


def update_kernel(sums_ref, direction_ref, solution_ref, residual_ref, image_ref, sol_ref, res_ref, dir_ref):
    line = jnp.sum(sums_ref[...], axis=0)
    lane = lax.broadcasted_iota(jnp.int32, line.shape, 1)

    def pick(at):
        return jnp.sum(jnp.where(lane == at, line, 0.0), axis=1, keepdims=True)

    norm_now, curvature, cross, square = pick(0), pick(1), pick(2), pick(3)
    alpha = norm_now / curvature
    norm_next = norm_now - 2.0 * alpha * cross + alpha * alpha * square
    beta = norm_next / norm_now
    direction = direction_ref[...]
    residual_next = residual_ref[...] - alpha * image_ref[...]
    sol_ref[...] = solution_ref[...] + alpha * direction
    res_ref[...] = residual_next
    dir_ref[...] = residual_next + beta * direction


def split(value):
    high = value.astype(jnp.bfloat16)
    return high, (value - high.astype(jnp.float32)).astype(jnp.bfloat16)


def dot_parts(left, right, contract):
    dims = (contract, ((), ()))
    total = lax.dot_general(left[0], right[0], dims, preferred_element_type=jnp.float32)
    total = total + lax.dot_general(left[0], right[1], dims, preferred_element_type=jnp.float32)
    return total + lax.dot_general(left[1], right[0], dims, preferred_element_type=jnp.float32)


def prepare_kernel(
    devices,
    capacity,
    lon_cols,
    vert_ref,
    owner_ref,
    row_ref,
    col_ref,
    frac_ref,
    factor_ref,
    high_ref,
    low_ref,
):
    vertical_factors_of(vert_ref, factor_ref)
    count = owner_ref.shape[1]
    slots = devices * capacity
    me = lax.axis_index("gy") * lax.axis_size("gx") + lax.axis_index("gx")
    apart = jnp.bitwise_xor(owner_ref[...], me)
    place = jnp.bitwise_and(apart, 1) * (devices // 2) + jnp.right_shift(apart, 1)
    named = lax.broadcasted_iota(jnp.int32, (devices, count), 0) == place
    before = lax.broadcasted_iota(jnp.int32, (count, count), 0) <= lax.broadcasted_iota(
        jnp.int32, (count, count), 1
    )
    running = jnp.dot(
        jnp.where(named, 1.0, 0.0).astype(jnp.bfloat16),
        jnp.where(before, 1.0, 0.0).astype(jnp.bfloat16),
        preferred_element_type=jnp.float32,
    )
    rank = jnp.sum(jnp.where(named, running, 0.0), axis=0, keepdims=True) - 1.0
    slot = place * capacity + rank.astype(jnp.int32)
    chosen = jnp.where(
        lax.broadcasted_iota(jnp.int32, (slots, count), 0) == slot, 1.0, 0.0
    ).astype(jnp.bfloat16)
    lat_frac = frac_ref[0:1, :]
    lon_frac = frac_ref[1:2, :]
    cell = (row_ref[...] * lon_cols + col_ref[...]).astype(jnp.float32)
    values = jnp.concatenate(
        [
            (1.0 - lat_frac) * (1.0 - lon_frac),
            (1.0 - lat_frac) * lon_frac,
            lat_frac * (1.0 - lon_frac),
            lat_frac * lon_frac,
            cell,
            jnp.zeros((3, count), jnp.float32),
        ],
        axis=0,
    )
    high, rest = split(values)
    low, rest = split(values - high.astype(jnp.float32))
    parts = jnp.concatenate([high.astype(jnp.float32), low.astype(jnp.float32), rest.astype(jnp.float32)], axis=0)
    placed = lax.dot_general(
        parts.astype(jnp.bfloat16), chosen, (((1,), (1,)), ((), ())), preferred_element_type=jnp.float32
    )
    placed = placed[0:8] + placed[8:16] + placed[16:24]
    first = jnp.round(placed[4:5, :]).astype(jnp.int32)
    away = lax.broadcasted_iota(jnp.int32, high_ref.shape, 0) - first
    interp = jnp.where(
        away == 0,
        placed[0:1, :],
        jnp.where(
            away == 1,
            placed[1:2, :],
            jnp.where(away == lon_cols, placed[2:3, :], jnp.where(away == lon_cols + 1, placed[3:4, :], 0.0)),
        ),
    )
    high_ref[...], low_ref[...] = split(interp)


def vertical_factors_of(vert_ref, factor_ref):
    layers = vert_ref.shape[0]
    top = lax.broadcasted_iota(jnp.int32, (8, LANES), 0) < 4
    coef = [jnp.where(top, vert_ref[layer, 0:1, :], vert_ref[layer, 1:2, :]) for layer in range(layers)]
    ratio = None
    for layer in range(layers):
        diagonal = 1.0 + coef[layer]
        if layer > 0:
            diagonal = diagonal + coef[layer - 1] - coef[layer - 1] * ratio
        inverse = 1.0 / diagonal
        ratio = coef[layer] * inverse
        factor_ref[0, layer] = inverse
        factor_ref[1, layer] = coef[layer - 1] * inverse if layer > 0 else jnp.zeros_like(inverse)
        factor_ref[2, layer] = ratio


def solve_columns(read, write, factor_ref, layers):
    forward = []
    for layer in range(layers):
        value = read(layer) * factor_ref[0, layer]
        if layer > 0:
            value = value + factor_ref[1, layer] * forward[-1]
        forward.append(value)
    value = forward[-1]
    write(layers - 1, value)
    for layer in range(layers - 2, -1, -1):
        value = forward[layer] + factor_ref[2, layer] * value
        write(layer, value)


def packed_at(layer, held):
    return pl.ds((layer // held) * 8 * held + layer % held, 8, stride=held)


def weigh(profile, matrix_ref, capacity):
    kv = matrix_ref.shape[1]
    owners = LANES // capacity
    mine = lax.broadcasted_iota(jnp.int32, (kv, LANES), 1) // capacity
    tiles = []
    for tile in range(matrix_ref.shape[0] // owners):
        values = profile[:, tile * LANES : (tile + 1) * LANES]
        masked = jnp.concatenate([jnp.where(mine == owner, values, 0.0) for owner in range(owners)], axis=0)
        matrices = jnp.concatenate([matrix_ref[tile * owners + owner] for owner in range(owners)], axis=1)
        tiles.append(dot_parts(split(matrices), split(masked), ((1,), (0,))))
    return jnp.concatenate(tiles, axis=1)


def smooth_kernel(layers, held, packed_ref, factor_ref, column_ref):
    def read(layer):
        return packed_ref[packed_at(layer, held), :]

    def write(layer, value):
        column_ref[pl.ds(layer, 8, stride=layers), :] = value

    solve_columns(read, write, factor_ref, layers)


def profile_kernel(capacity, column_ref, high_ref, low_ref, near_ref, weighted_ref, profile_ref):
    kv = profile_ref.shape[0]
    half = profile_ref.shape[1]
    columns = jnp.concatenate([column_ref[0:kv, :], column_ref[kv : 2 * kv, :]], axis=1)
    profile = dot_parts(split(columns), (high_ref[...], low_ref[...]), ((1,), (0,)))
    profile_ref[...] = profile[:, half:]
    weighted_ref[...] = weigh(profile[:, :half], near_ref, capacity)


def spread_kernel(
    layers, held, capacity, near_ref, profile_ref, factor_ref, high_ref, low_ref, far_ref, out_ref, column_ref
):
    kv = near_ref.shape[0]
    weighted = jnp.concatenate([near_ref[...], weigh(profile_ref[...], far_ref, capacity)], axis=1)
    spread = dot_parts(split(weighted), (high_ref[...], low_ref[...]), ((1,), (1,)))
    column_ref[0:kv, :] = spread[:, :LANES]
    column_ref[kv : 2 * kv, :] = spread[:, LANES:]

    def read(layer):
        return column_ref[pl.ds(layer, 8, stride=layers), :]

    def write(layer, value):
        out_ref[packed_at(layer, held), :] = value

    solve_columns(read, write, factor_ref, layers)


def vmem(count):
    return [pl.BlockSpec(memory_space=pltpu.VMEM)] * count


def call(kernel, out_shape, inputs, scratch=(), after=0, hbm=False, flops=1_000_000, mib=8):
    specs = [pl.BlockSpec(memory_space=pl.ANY)] * after + vmem(len(inputs) - after)
    outs = vmem(len(out_shape) if isinstance(out_shape, tuple) else 1)
    if hbm:
        specs, outs = ([pl.BlockSpec(memory_space=pltpu.HBM)] * len(x) for x in (specs, outs))
    moved = sum(math.prod(x.shape) * 4 for x in inputs)
    return pl.pallas_call(
        kernel,
        out_shape=out_shape,
        in_specs=specs,
        out_specs=tuple(outs) if isinstance(out_shape, tuple) else outs[0],
        scratch_shapes=list(scratch),
        compiler_params=pltpu.CompilerParams(vmem_limit_bytes=mib * 1024 * 1024),
        cost_estimate=pl.CostEstimate(flops=flops, bytes_accessed=moved, transcendentals=0),
    )(*inputs)


def f32(*shape):
    return jax.ShapeDtypeStruct(shape, jnp.float32)


def from_neighbours(block):
    count = lax.axis_size("gy")
    pair = lax.ppermute(block, "gy", [(i, i ^ 1) for i in range(count)])
    cross = lax.ppermute(block, "gy", [(i, (i + (1 if i % 2 else -1)) % count) for i in range(count)])
    return pair, cross


def apart_by(block, axis, stride):
    return lax.ppermute(block, axis, [(i, i ^ stride) for i in range(lax.axis_size(axis))])


def per_device_gathered(
    direction,
    solution,
    residual,
    north_coef,
    east_coef,
    ocean,
    vert_coef,
    obs_owner,
    obs_row,
    obs_col,
    obs_frac,
    error_inverse,
):
    var_count, held, rows, lons = direction.shape
    kv = var_count * held
    tiles = lons // LANES
    layers, _, lon_cols = vert_coef.shape
    rows_y, cols_x = lax.axis_size("gy"), lax.axis_size("gx")
    device_count = rows_y * cols_x
    obs_count = obs_row.shape[-1]
    capacity = 2 * obs_count // device_count
    wide = error_inverse.shape[-1]
    cells = rows * lon_cols

    direction_n = to_native(direction)
    residual_n = to_native(residual)
    solution_n = to_native(solution)
    faces = [to_native(x[None, None]) for x in (north_coef, east_coef, ocean)]
    own = call(
        functools.partial(halo_kernel, 4),
        f32(direction_n.shape[0] + 3 * faces[0].shape[0], LANES),
        (direction_n, *faces),
        scratch=(
            pltpu.VMEM((direction_n.shape[0] + 3 * faces[0].shape[0], LANES), jnp.float32),
            pltpu.VMEM(faces[0].shape, jnp.int32),
            pltpu.SemaphoreType.DMA((2, 7)),
        ),
        hbm=True,
        mib=56,
    )
    pair, cross = from_neighbours(own)

    matrix = error_inverse.reshape(1, wide, wide)
    blocks = [matrix] + [apart_by(matrix, "gx", stride) for stride in range(2, cols_x, 2)]
    halves = jax.ShapeDtypeStruct((cells, device_count * capacity), jnp.bfloat16)
    factors, *interp = call(
        functools.partial(prepare_kernel, device_count, capacity, lon_cols),
        (f32(3, layers, 8, LANES), halves, halves),
        (
            vert_coef.reshape(layers, cells // LANES, LANES),
            obs_owner.reshape(1, obs_count),
            obs_row.reshape(1, obs_count),
            obs_col.reshape(1, obs_count),
            obs_frac.reshape(2, obs_count),
        ),
        flops=20_000_000,
        mib=16,
    )
    held_blocks = call(
        functools.partial(join_kernel, 1, len(blocks)),
        f32(len(blocks), wide, wide),
        (interp[0], *blocks),
        after=1,
    )

    extended = 3 * rows + (-3 * rows) % 8
    packed, coef = call(
        functools.partial(first_lateral_kernel, kv, rows, tiles),
        (f32(cols_x, 2 * kv, LANES), f32(5, extended, lons)),
        (held_blocks, direction_n, *faces, pair, cross),
        after=1,
        scratch=(
            pltpu.VMEM((3, extended, lons), jnp.float32),
            pltpu.VMEM(own.shape, jnp.float32),
            pltpu.VMEM(own.shape, jnp.float32),
        ),
        flops=4_000_000,
    )
    fetched = [held_blocks] + [apart_by(held_blocks, "gy", stride) for stride in range(1, rows_y)]
    columns = lax.all_to_all(packed, "gx", split_axis=0, concat_axis=0, tiled=True)
    smoothed = call(
        functools.partial(smooth_kernel, layers, held),
        f32(2 * wide, LANES),
        (columns.reshape(cols_x * 2 * kv, LANES), factors),
        flops=1000,
    )
    near = call(
        functools.partial(join_kernel, 1, len(fetched)),
        f32(device_count // 2, wide, wide),
        (smoothed, *fetched),
        after=1,
    )
    far = apart_by(near, "gx", 1)
    half = device_count // 2 * capacity
    weighted, profile = call(
        functools.partial(profile_kernel, capacity),
        (f32(wide, half), f32(wide, half)),
        (smoothed, *interp, near),
        flops=400_000_000,
        mib=16,
    )
    spread = call(
        functools.partial(spread_kernel, layers, held, capacity),
        f32(cols_x * 2 * kv, LANES),
        (weighted, profile, factors, *interp, far),
        scratch=(pltpu.VMEM((2 * wide, LANES), jnp.float32),),
        flops=400_000_000,
        mib=16,
    )
    tile = lax.all_to_all(
        spread.reshape(cols_x, 2 * kv, LANES), "gx", split_axis=0, concat_axis=0, tiled=True
    )
    pair, cross = from_neighbours(tile)
    image, sums = call(
        functools.partial(second_lateral_kernel, kv, rows, tiles),
        (f32(*direction_n.shape), f32(device_count, 1, LANES)),
        (tile, pair, cross, coef, direction_n, residual_n),
        scratch=(pltpu.VMEM(tile.shape, jnp.float32), pltpu.VMEM(tile.shape, jnp.float32)),
        flops=4_000_000,
    )
    sums = lax.all_to_all(sums, ("gy", "gx"), split_axis=0, concat_axis=0, tiled=True)
    after = call(
        update_kernel,
        (f32(*direction_n.shape),) * 3,
        (sums, direction_n, solution_n, residual_n, image),
    )
    return tuple(from_native(x, direction.shape) for x in after)


def gathers(mesh, shapes):
    rows_y, cols_x = mesh.shape["gy"], mesh.shape["gx"]
    devices = rows_y * cols_x
    if any(size < 2 or size & (size - 1) for size in (rows_y, cols_x)):
        return False
    direction, vert_coef, obs_row, error_inverse = shapes
    var_count, layers, lat_rows, lons = direction
    rows, held = lat_rows // rows_y, layers // cols_x
    obs_count, wide = obs_row[-1], error_inverse[-1]
    capacity = 2 * obs_count // devices
    return (
        rows == NSTEP == 4
        and var_count == 4
        and (var_count * held) % 8 == 0
        and lons // cols_x * 2 == LANES
        and wide == LANES
        and capacity > 0
        and LANES % capacity == 0
        and devices // 2 % (LANES // capacity) == 0
        and devices * wide * wide * 4 <= 8 * 1024 * 1024
    )


def padded(cells, sides, width):
    for axis, dim in sides:
        count = lax.axis_size(axis)
        ends = count - 1
        head = lax.slice_in_dim(cells, 0, width, axis=dim)
        tail = lax.slice_in_dim(cells, cells.shape[dim] - width, cells.shape[dim], axis=dim)
        cells = jnp.concatenate(
            [
                lax.ppermute(tail, axis, [(i, (i + 1) % count) for i in range(ends)]),
                cells,
                lax.ppermute(head, axis, [((i + 1) % count, i) for i in range(ends)]),
            ],
            axis=dim,
        )
    return cells


def lateral_faces(north_ext, east_ext, ocean_ext):
    ocean_next = jnp.concatenate([ocean_ext[1:], jnp.zeros_like(ocean_ext[:1])], axis=0)
    north_face = north_ext * ocean_ext * ocean_next
    east_face = east_ext * ocean_ext * jnp.roll(ocean_ext, -1, axis=1)
    return (north_face, east_face, ocean_ext)


def diffuse_once(values_grid, north_face, east_face, ocean_ext):
    north_flux = north_face[:-1] * (values_grid[:, :, 1:, :] - values_grid[:, :, :-1, :])
    east_flux = east_face * (jnp.roll(values_grid, -1, axis=3) - values_grid)
    lateral = east_flux - jnp.roll(east_flux, 1, axis=3)
    return (
        ocean_ext[1:-1] * values_grid[:, :, 1:-1, :]
        + north_flux[:, :, 1:, :]
        - north_flux[:, :, :-1, :]
        + lateral[:, :, 1:-1, :]
    )


def lateral_pass(values_tile, faces):
    north_face, east_face, ocean_ext = faces
    grown = padded(values_tile, (("gy", 2),), NSTEP)
    total_rows = grown.shape[2]
    for step_index in range(NSTEP):
        upper = total_rows - step_index
        grown = diffuse_once(
            grown,
            north_face[step_index:upper],
            east_face[step_index:upper],
            ocean_ext[step_index:upper],
        )
    return grown


def vertical_factors(vert_coef):
    inverse_rows = []
    upper_ratio = []
    for layer_index in range(vert_coef.shape[0]):
        diagonal = 1.0 + vert_coef[layer_index]
        if layer_index > 0:
            diagonal = (
                diagonal + vert_coef[layer_index - 1] + vert_coef[layer_index - 1] * upper_ratio[-1]
            )
        inverse = 1.0 / diagonal
        inverse_rows.append(inverse)
        upper_ratio.append(-vert_coef[layer_index] * inverse)
    return (inverse_rows, upper_ratio)


def vertical_solve(values_col, vert_coef, factors):
    inverse_rows, upper_ratio = factors
    layers = values_col.shape[1]
    forward = []
    for layer_index in range(layers):
        source = values_col[:, layer_index]
        if layer_index > 0:
            source = source + vert_coef[layer_index - 1] * forward[-1]
        forward.append(source * inverse_rows[layer_index])
    result = [forward[-1]]
    for layer_index in range(layers - 2, -1, -1):
        result.append(forward[layer_index] - upper_ratio[layer_index] * result[-1])
    return jnp.stack(result[::-1], axis=1)


def observe_weigh_spread(columns, obs_owner, obs_row, obs_col, obs_frac, error_inverse):
    var_count, lev_count, lat_rows, lon_cols = columns.shape
    kv_width = var_count * lev_count
    rows_y = lax.axis_size("gy")
    cols_x = lax.axis_size("gx")
    device_count = rows_y * cols_x
    obs_count = obs_row.shape[-1]
    capacity = 2 * obs_count // device_count
    flat = columns.reshape(kv_width, lat_rows * lon_cols)
    cell = obs_row.reshape(-1) * lon_cols + obs_col.reshape(-1)
    corners = (cell, cell + 1, cell + lon_cols, cell + lon_cols + 1)
    lat_frac = obs_frac[0, 0, 0]
    lon_frac = obs_frac[0, 0, 1]
    weights = (
        (1.0 - lat_frac) * (1.0 - lon_frac),
        (1.0 - lat_frac) * lon_frac,
        lat_frac * (1.0 - lon_frac),
        lat_frac * lon_frac,
    )
    profile = weights[0] * jnp.take(flat, corners[0], axis=1)
    for corner_index in range(1, 4):
        profile = profile + weights[corner_index] * jnp.take(flat, corners[corner_index], axis=1)
    owners = obs_owner.reshape(-1)
    onehot = (owners[:, None] == jnp.arange(device_count, dtype=jnp.int32)[None, :]).astype(
        jnp.int32
    )
    running = jnp.cumsum(onehot, axis=0)
    rank_in = jnp.sum(running * onehot, axis=1) - 1
    slot = owners * capacity + rank_in
    outgoing = jnp.zeros((device_count * capacity, kv_width), jnp.float32).at[slot].set(profile.T)
    outgoing = outgoing.reshape(rows_y, cols_x, capacity, kv_width)
    matrix = error_inverse.reshape(kv_width, kv_width)
    arrived = lax.all_to_all(
        lax.all_to_all(outgoing, "gy", split_axis=0, concat_axis=0, tiled=True),
        "gx",
        split_axis=1,
        concat_axis=1,
        tiled=True,
    )
    weighted = jnp.dot(
        arrived.reshape(-1, kv_width),
        matrix,
        precision=lax.Precision.HIGHEST,
        preferred_element_type=jnp.float32,
    ).reshape(rows_y, cols_x, capacity, kv_width)
    returned = lax.all_to_all(
        lax.all_to_all(weighted, "gy", split_axis=0, concat_axis=0, tiled=True),
        "gx",
        split_axis=1,
        concat_axis=1,
        tiled=True,
    )
    back = returned.reshape(device_count * capacity, kv_width)[slot].T
    spread = jnp.zeros((kv_width, lat_rows * lon_cols), jnp.float32)
    for corner_index in range(4):
        spread = spread.at[:, corners[corner_index]].add(weights[corner_index] * back)
    return spread.reshape(var_count, lev_count, lat_rows, lon_cols)


def per_device(
    direction,
    solution,
    residual,
    north_coef,
    east_coef,
    ocean,
    vert_coef,
    obs_owner,
    obs_row,
    obs_col,
    obs_frac,
    error_inverse,
):
    stacked = jnp.stack([north_coef, east_coef, ocean.astype(jnp.float32)])
    reach = NSTEP
    grown_coef = padded(stacked, (("gy", 1),), reach)
    faces = lateral_faces(grown_coef[0], grown_coef[1], grown_coef[2])
    factors = vertical_factors(vert_coef)
    smoothed = lateral_pass(direction, faces)
    columns = lax.all_to_all(smoothed, "gx", split_axis=3, concat_axis=1, tiled=True)
    columns = vertical_solve(columns, vert_coef, factors)
    spread = observe_weigh_spread(columns, obs_owner, obs_row, obs_col, obs_frac, error_inverse)
    spread = vertical_solve(spread, vert_coef, factors)
    tiles = lax.all_to_all(spread, "gx", split_axis=1, concat_axis=3, tiled=True)
    image = direction + lateral_pass(tiles, faces)
    norm_now, curvature = lax.psum(
        (jnp.sum(residual * residual), jnp.sum(direction * image)), ("gy", "gx")
    )
    alpha = norm_now / curvature
    residual_next = residual - alpha * image
    norm_next = lax.psum(jnp.sum(residual_next * residual_next), ("gy", "gx"))
    solution_next = solution + alpha * direction
    direction_next = residual_next + norm_next / norm_now * direction
    return (solution_next, residual_next, direction_next)


def solution(mesh):
    in_specs = (
        P(None, "gx", "gy", None),
        P(None, "gx", "gy", None),
        P(None, "gx", "gy", None),
        P("gy", None),
        P("gy", None),
        P("gy", None),
        P(None, "gy", "gx"),
        P("gy", "gx", None, None),
        P("gy", "gx", None),
        P("gy", "gx", None),
        P("gy", "gx", None, None),
        P("gy", "gx", None, None),
    )
    out_specs = (P(None, "gx", "gy", None),) * 3

    def step(*arrays):
        shapes = [arrays[at].shape for at in (0, 6, 8, 11)]
        local = per_device_gathered if gathers(mesh, shapes) else per_device
        return jax.shard_map(
            local, mesh=mesh, in_specs=in_specs, out_specs=out_specs, check_vma=False
        )(*arrays)

    return step
```

```python
import functools
import math

import jax
import jax.numpy as jnp
from jax import lax
from jax.experimental import pallas as pl
from jax.experimental.pallas import tpu as pltpu
from jax.sharding import PartitionSpec as P

NSTEP = 4
LANES = 128


def to_native(tile):
    kv, rows, lons = tile.shape[0] * tile.shape[1], tile.shape[2], tile.shape[3]
    return tile.reshape(kv, rows, lons // LANES, LANES).swapaxes(1, 2).reshape(-1, LANES)


def from_native(flat, shape):
    kv, rows, lons = shape[0] * shape[1], shape[2], shape[3]
    return flat.reshape(kv, lons // LANES, rows, LANES).swapaxes(1, 2).reshape(shape)


def native_rows(ref, base, row, rows, tiles, half):
    parts = [
        ref[pl.ds(base + (half * 8 * tiles + tile) * rows + row, 8, stride=tiles * rows), :]
        for tile in range(tiles)
    ]
    return jnp.concatenate(parts, axis=1)


def lane_low(shape):
    return lax.broadcasted_iota(jnp.int32, shape, 1) < LANES // 2


def lateral_rows(rows, coef, reach):
    for step in range(reach):
        after = []
        for i in range(1, len(rows) - 1):
            at = step + i
            u = rows[i]
            width = u.shape[1]
            after.append(
                coef[0, at : at + 1, :] * u
                + coef[1, at : at + 1, :] * rows[i + 1]
                + coef[2, at : at + 1, :] * rows[i - 1]
                + coef[3, at : at + 1, :] * pltpu.roll(u, width - 1, 1)
                + coef[4, at : at + 1, :] * pltpu.roll(u, 1, 1)
            )
        rows = after
    return rows


def sort_halo(pair_ref, cross_ref, low_ref, high_ref):
    at_y, rows_y = lax.axis_index("gy"), lax.axis_size("gy")
    odd = lax.rem(at_y, 2) == 1

    @pl.when(odd)
    def _():
        low_ref[...] = pair_ref[...]
        high_ref[...] = cross_ref[...]

    @pl.when(jnp.logical_not(odd))
    def _():
        low_ref[...] = cross_ref[...]
        high_ref[...] = pair_ref[...]

    @pl.when(at_y == 0)
    def _():
        low_ref[...] = jnp.zeros_like(low_ref)

    @pl.when(at_y == rows_y - 1)
    def _():
        high_ref[...] = jnp.zeros_like(high_ref)


def triangle_masks():
    shape = (LANES // 2, LANES)
    lane = lax.broadcasted_iota(jnp.int32, shape, 1)
    return lane, lane - lax.broadcasted_iota(jnp.int32, shape, 0)


def pack_symmetric(matrix, packed_ref):
    half = LANES // 2
    lane, away = triangle_masks()
    top, bottom = matrix[:half], matrix[half:]
    corner = jnp.where(away <= 0, top, pltpu.roll(bottom, half, 1))
    packed_ref[0:half, :] = jnp.where(lane < half, corner, top)
    diagonal = jnp.sum(jnp.where(away == half, bottom, 0.0), axis=0, keepdims=True)
    packed_ref[half:, :] = jnp.broadcast_to(diagonal, (packed_ref.shape[0] - half, LANES))


def unpack_symmetric(packed):
    half = LANES // 2
    lane, away = triangle_masks()
    rows, diagonal = packed[:half], packed[half : half + 1]
    turned = jnp.concatenate([rows, rows], axis=0).T
    top = jnp.where((lane < half) & (away > 0), turned[:half], rows)
    corner = jnp.where(
        away > half, pltpu.roll(rows, half, 1), jnp.where(away == half, diagonal, turned[:half])
    )
    return jnp.concatenate([top, jnp.where(lane < half, turned[half:], corner)], axis=0)


def halo_kernel(chunks, direction_ref, north_ref, east_ref, ocean_ref, own_ref, stage_ref, mask_ref, sems):
    cells, size = direction_ref.shape[0], north_ref.shape[0]
    rows = cells // chunks
    spans = [(direction_ref.at[pl.ds(at * rows, rows)], at * rows, rows) for at in range(chunks)]
    spans += [(north_ref, cells, size), (east_ref, cells + size, size)]
    arrive = [
        pltpu.make_async_copy(source, stage_ref.at[pl.ds(start, count)], sems.at[0, at])
        for at, (source, start, count) in enumerate(spans)
    ]
    arrive.append(pltpu.make_async_copy(ocean_ref, mask_ref, sems.at[0, len(spans)]))
    spans.append((ocean_ref, cells + 2 * size, size))
    leave = [
        pltpu.make_async_copy(
            stage_ref.at[pl.ds(start, count)], own_ref.at[pl.ds(start, count)], sems.at[1, at]
        )
        for at, (_, start, count) in enumerate(spans)
    ]
    for copy in arrive:
        copy.start()
    for at, copy in enumerate(arrive):
        copy.wait()
        if at == len(arrive) - 1:
            stage_ref[cells + 2 * size : cells + 3 * size, :] = mask_ref[...].astype(jnp.float32)
        leave[at].start()
    for copy in leave:
        copy.wait()


def join_kernel(after, count, *refs):
    blocks, (near_ref,) = refs[after : after + count], refs[after + count :]
    size = blocks[0].shape[0]
    for at, block in enumerate(blocks):
        near_ref[at * size : (at + 1) * size] = block[...]


def pack_kernel(_, *refs):
    blocks, (packed_ref,) = refs[:-1], refs[-1:]
    size = blocks[0].shape[0]
    for at, block in enumerate(blocks):
        for inner in range(size):
            pack_symmetric(block[inner], packed_ref.at[at * size + inner])


def first_lateral_kernel(
    kv,
    rows,
    tiles,
    _,
    own_ref,
    north_ref,
    east_ref,
    ocean_ref,
    pair_ref,
    cross_ref,
    packed_ref,
    coef_ref,
    ext_ref,
    low_ref,
    high_ref,
):
    lons = tiles * LANES
    cells = kv * tiles * rows
    sort_halo(pair_ref, cross_ref, low_ref, high_ref)
    ext_ref[...] = jnp.zeros_like(ext_ref)
    for kind, kept in enumerate((north_ref, east_ref, ocean_ref)):
        for tile in range(tiles):
            lanes = slice(tile * LANES, (tile + 1) * LANES)
            start = cells + (kind * tiles + tile) * rows
            ext_ref[kind, 0:rows, lanes] = low_ref[start : start + rows, :]
            ext_ref[kind, rows : 2 * rows, lanes] = kept[tile * rows : (tile + 1) * rows, :].astype(jnp.float32)
            ext_ref[kind, 2 * rows : 3 * rows, lanes] = high_ref[start : start + rows, :]
    total = ext_ref.shape[1]
    north, east, ocean = ext_ref[0], ext_ref[1], ext_ref[2]
    north_face = north * ocean * pltpu.roll(ocean, total - 1, 0)
    east_face = east * ocean * pltpu.roll(ocean, lons - 1, 1)
    south_face = pltpu.roll(north_face, 1, 0)
    west_face = pltpu.roll(east_face, 1, 1)
    coef_ref[0] = ocean - north_face - south_face - east_face - west_face
    coef_ref[1] = north_face
    coef_ref[2] = south_face
    coef_ref[3] = east_face
    coef_ref[4] = west_face
    low = lane_low((8, LANES))
    for half in range(kv // 8):
        grown = [
            native_rows(ref, 0, row, rows, tiles, half)
            for ref in (low_ref, own_ref, high_ref)
            for row in range(rows)
        ]
        done = lateral_rows(grown, coef_ref, rows)
        for pair in range(rows // 2):
            for tile in range(tiles):
                first = done[2 * pair][:, tile * LANES : (tile + 1) * LANES]
                second = done[2 * pair + 1][:, tile * LANES : (tile + 1) * LANES]
                at = pair * kv + half * 8
                packed_ref[2 * tile, at : at + 8, :] = jnp.where(
                    low, first, pltpu.roll(second, LANES // 2, 1)
                )
                packed_ref[2 * tile + 1, at : at + 8, :] = jnp.where(
                    low, pltpu.roll(first, LANES // 2, 1), second
                )


def second_lateral_kernel(
    kv,
    rows,
    tiles,
    own_ref,
    pair_ref,
    cross_ref,
    coef_ref,
    direction_ref,
    residual_ref,
    image_ref,
    sums_ref,
    low_ref,
    high_ref,
):
    sort_halo(pair_ref, cross_ref, low_ref, high_ref)
    low = lane_low((8, LANES))
    totals = [jnp.zeros((8, tiles * LANES), jnp.float32) for _ in range(4)]
    for half in range(kv // 8):
        grown = []
        for ref in (low_ref, own_ref, high_ref):
            for pair in range(rows // 2):
                firsts, seconds = [], []
                at = pair * kv + half * 8
                for tile in range(tiles):
                    even = ref[2 * tile, at : at + 8, :]
                    odd = ref[2 * tile + 1, at : at + 8, :]
                    firsts.append(jnp.where(low, even, pltpu.roll(odd, LANES // 2, 1)))
                    seconds.append(jnp.where(low, pltpu.roll(even, LANES // 2, 1), odd))
                grown.append(jnp.concatenate(firsts, axis=1))
                grown.append(jnp.concatenate(seconds, axis=1))
        done = lateral_rows(grown, coef_ref, rows)
        for row in range(rows):
            direction = native_rows(direction_ref, 0, row, rows, tiles, half)
            residual = native_rows(residual_ref, 0, row, rows, tiles, half)
            image = direction + done[row]
            for tile in range(tiles):
                image_ref[pl.ds((half * 8 * tiles + tile) * rows + row, 8, stride=tiles * rows), :] = image[
                    :, tile * LANES : (tile + 1) * LANES
                ]
            totals[0] = totals[0] + residual * residual
            totals[1] = totals[1] + direction * image
            totals[2] = totals[2] + residual * image
            totals[3] = totals[3] + image * image
    lane = lax.broadcasted_iota(jnp.int32, (1, LANES), 1)
    line = jnp.zeros((1, LANES), jnp.float32)
    for at, total in enumerate(totals):
        line = jnp.where(lane == at, jnp.sum(total), line)
    for device in range(sums_ref.shape[0]):
        sums_ref[device] = line


def update_kernel(sums_ref, direction_ref, solution_ref, residual_ref, image_ref, sol_ref, res_ref, dir_ref):
    line = jnp.sum(sums_ref[...], axis=0)
    lane = lax.broadcasted_iota(jnp.int32, line.shape, 1)

    def pick(at):
        return jnp.sum(jnp.where(lane == at, line, 0.0), axis=1, keepdims=True)

    norm_now, curvature, cross, square = pick(0), pick(1), pick(2), pick(3)
    alpha = norm_now / curvature
    norm_next = norm_now - 2.0 * alpha * cross + alpha * alpha * square
    beta = norm_next / norm_now
    direction = direction_ref[...]
    residual_next = residual_ref[...] - alpha * image_ref[...]
    sol_ref[...] = solution_ref[...] + alpha * direction
    res_ref[...] = residual_next
    dir_ref[...] = residual_next + beta * direction


def split(value):
    high = value.astype(jnp.bfloat16)
    return high, (value - high.astype(jnp.float32)).astype(jnp.bfloat16)


def dot_parts(left, right, contract):
    dims = (contract, ((), ()))
    total = lax.dot_general(left[0], right[0], dims, preferred_element_type=jnp.float32)
    total = total + lax.dot_general(left[0], right[1], dims, preferred_element_type=jnp.float32)
    return total + lax.dot_general(left[1], right[0], dims, preferred_element_type=jnp.float32)


def prepare_kernel(
    devices,
    capacity,
    lon_cols,
    vert_ref,
    owner_ref,
    row_ref,
    col_ref,
    frac_ref,
    factor_ref,
    high_ref,
    low_ref,
):
    vertical_factors_of(vert_ref, factor_ref)
    count = owner_ref.shape[1]
    slots = devices * capacity
    me = lax.axis_index("gy") * lax.axis_size("gx") + lax.axis_index("gx")
    apart = jnp.bitwise_xor(owner_ref[...], me)
    place = jnp.bitwise_and(apart, 1) * (devices // 2) + jnp.right_shift(apart, 1)
    named = lax.broadcasted_iota(jnp.int32, (devices, count), 0) == place
    before = lax.broadcasted_iota(jnp.int32, (count, count), 0) <= lax.broadcasted_iota(
        jnp.int32, (count, count), 1
    )
    running = jnp.dot(
        jnp.where(named, 1.0, 0.0).astype(jnp.bfloat16),
        jnp.where(before, 1.0, 0.0).astype(jnp.bfloat16),
        preferred_element_type=jnp.float32,
    )
    rank = jnp.sum(jnp.where(named, running, 0.0), axis=0, keepdims=True) - 1.0
    slot = place * capacity + rank.astype(jnp.int32)
    chosen = jnp.where(
        lax.broadcasted_iota(jnp.int32, (slots, count), 0) == slot, 1.0, 0.0
    ).astype(jnp.bfloat16)
    lat_frac = frac_ref[0:1, :]
    lon_frac = frac_ref[1:2, :]
    cell = (row_ref[...] * lon_cols + col_ref[...]).astype(jnp.float32)
    values = jnp.concatenate(
        [
            (1.0 - lat_frac) * (1.0 - lon_frac),
            (1.0 - lat_frac) * lon_frac,
            lat_frac * (1.0 - lon_frac),
            lat_frac * lon_frac,
            cell,
            jnp.zeros((3, count), jnp.float32),
        ],
        axis=0,
    )
    high, rest = split(values)
    low, rest = split(values - high.astype(jnp.float32))
    parts = jnp.concatenate([high.astype(jnp.float32), low.astype(jnp.float32), rest.astype(jnp.float32)], axis=0)
    placed = lax.dot_general(
        parts.astype(jnp.bfloat16), chosen, (((1,), (1,)), ((), ())), preferred_element_type=jnp.float32
    )
    placed = placed[0:8] + placed[8:16] + placed[16:24]
    first = jnp.round(placed[4:5, :]).astype(jnp.int32)
    away = lax.broadcasted_iota(jnp.int32, high_ref.shape, 0) - first
    interp = jnp.where(
        away == 0,
        placed[0:1, :],
        jnp.where(
            away == 1,
            placed[1:2, :],
            jnp.where(away == lon_cols, placed[2:3, :], jnp.where(away == lon_cols + 1, placed[3:4, :], 0.0)),
        ),
    )
    high_ref[...], low_ref[...] = split(interp)


def vertical_factors_of(vert_ref, factor_ref):
    layers = vert_ref.shape[0]
    top = lax.broadcasted_iota(jnp.int32, (8, LANES), 0) < 4
    coef = [jnp.where(top, vert_ref[layer, 0:1, :], vert_ref[layer, 1:2, :]) for layer in range(layers)]
    ratio = None
    for layer in range(layers):
        diagonal = 1.0 + coef[layer]
        if layer > 0:
            diagonal = diagonal + coef[layer - 1] - coef[layer - 1] * ratio
        inverse = 1.0 / diagonal
        ratio = coef[layer] * inverse
        factor_ref[0, layer] = inverse
        factor_ref[1, layer] = coef[layer - 1] * inverse if layer > 0 else jnp.zeros_like(inverse)
        factor_ref[2, layer] = ratio


def solve_columns(read, write, factor_ref, layers):
    forward = []
    for layer in range(layers):
        value = read(layer) * factor_ref[0, layer]
        if layer > 0:
            value = value + factor_ref[1, layer] * forward[-1]
        forward.append(value)
    value = forward[-1]
    write(layers - 1, value)
    for layer in range(layers - 2, -1, -1):
        value = forward[layer] + factor_ref[2, layer] * value
        write(layer, value)


def packed_at(layer, held):
    return pl.ds((layer // held) * 8 * held + layer % held, 8, stride=held)


def weigh(profile, matrices, capacity):
    kv = profile.shape[0]
    owners = LANES // capacity
    mine = lax.broadcasted_iota(jnp.int32, (kv, LANES), 1) // capacity
    tiles = []
    for tile in range(profile.shape[1] // LANES):
        values = profile[:, tile * LANES : (tile + 1) * LANES]
        masked = jnp.concatenate([jnp.where(mine == owner, values, 0.0) for owner in range(owners)], axis=0)
        beside = jnp.concatenate([matrices(tile * owners + owner) for owner in range(owners)], axis=1)
        tiles.append(dot_parts(split(beside), split(masked), ((1,), (0,))))
    return jnp.concatenate(tiles, axis=1)


def smooth_kernel(layers, held, packed_ref, factor_ref, column_ref):
    def read(layer):
        return packed_ref[packed_at(layer, held), :]

    def write(layer, value):
        column_ref[pl.ds(layer, 8, stride=layers), :] = value

    solve_columns(read, write, factor_ref, layers)


def profile_kernel(capacity, column_ref, high_ref, low_ref, *refs):
    near_refs, (weighted_ref, profile_ref) = refs[:-2], refs[-2:]
    kv, half = profile_ref.shape
    size = near_refs[0].shape[0]
    columns = jnp.concatenate([column_ref[0:kv, :], column_ref[kv : 2 * kv, :]], axis=1)
    profile = dot_parts(split(columns), (high_ref[...], low_ref[...]), ((1,), (0,)))
    profile_ref[...] = profile[:, half:]
    weighted_ref[...] = weigh(profile[:, :half], lambda at: near_refs[at // size][at % size], capacity)


def spread_kernel(
    layers, held, capacity, near_ref, profile_ref, factor_ref, high_ref, low_ref, far_ref, out_ref, column_ref
):
    kv = near_ref.shape[0]
    weighted = jnp.concatenate([near_ref[...], weigh(profile_ref[...], lambda at: unpack_symmetric(far_ref[at]), capacity)], axis=1)
    spread = dot_parts(split(weighted), (high_ref[...], low_ref[...]), ((1,), (1,)))
    column_ref[0:kv, :] = spread[:, :LANES]
    column_ref[kv : 2 * kv, :] = spread[:, LANES:]

    def read(layer):
        return column_ref[pl.ds(layer, 8, stride=layers), :]

    def write(layer, value):
        out_ref[packed_at(layer, held), :] = value

    solve_columns(read, write, factor_ref, layers)


def vmem(count):
    return [pl.BlockSpec(memory_space=pltpu.VMEM)] * count


def call(kernel, out_shape, inputs, scratch=(), after=0, hbm=False, flops=1_000_000, mib=8):
    specs = [pl.BlockSpec(memory_space=pl.ANY)] * after + vmem(len(inputs) - after)
    outs = vmem(len(out_shape) if isinstance(out_shape, tuple) else 1)
    if hbm:
        specs, outs = ([pl.BlockSpec(memory_space=pltpu.HBM)] * len(x) for x in (specs, outs))
    moved = sum(math.prod(x.shape) * 4 for x in inputs)
    return pl.pallas_call(
        kernel,
        out_shape=out_shape,
        in_specs=specs,
        out_specs=tuple(outs) if isinstance(out_shape, tuple) else outs[0],
        scratch_shapes=list(scratch),
        compiler_params=pltpu.CompilerParams(vmem_limit_bytes=mib * 1024 * 1024),
        cost_estimate=pl.CostEstimate(flops=flops, bytes_accessed=moved, transcendentals=0),
    )(*inputs)


def f32(*shape):
    return jax.ShapeDtypeStruct(shape, jnp.float32)


def from_neighbours(block):
    count = lax.axis_size("gy")
    pair = lax.ppermute(block, "gy", [(i, i ^ 1) for i in range(count)])
    cross = lax.ppermute(block, "gy", [(i, (i + (1 if i % 2 else -1)) % count) for i in range(count)])
    return pair, cross


def apart_by(block, axis, stride):
    return lax.ppermute(block, axis, [(i, i ^ stride) for i in range(lax.axis_size(axis))])


def per_device_gathered(
    direction,
    solution,
    residual,
    north_coef,
    east_coef,
    ocean,
    vert_coef,
    obs_owner,
    obs_row,
    obs_col,
    obs_frac,
    error_inverse,
):
    var_count, held, rows, lons = direction.shape
    kv = var_count * held
    tiles = lons // LANES
    layers, _, lon_cols = vert_coef.shape
    rows_y, cols_x = lax.axis_size("gy"), lax.axis_size("gx")
    device_count = rows_y * cols_x
    obs_count = obs_row.shape[-1]
    capacity = 2 * obs_count // device_count
    wide = error_inverse.shape[-1]
    cells = rows * lon_cols

    direction_n = to_native(direction)
    residual_n = to_native(residual)
    solution_n = to_native(solution)
    faces = [to_native(x[None, None]) for x in (north_coef, east_coef, ocean)]
    own = call(
        functools.partial(halo_kernel, 4),
        f32(direction_n.shape[0] + 3 * faces[0].shape[0], LANES),
        (direction_n, *faces),
        scratch=(
            pltpu.VMEM((direction_n.shape[0] + 3 * faces[0].shape[0], LANES), jnp.float32),
            pltpu.VMEM(faces[0].shape, jnp.int32),
            pltpu.SemaphoreType.DMA((2, 7)),
        ),
        hbm=True,
        mib=56,
    )
    pair, cross = from_neighbours(own)

    matrix = error_inverse.reshape(1, wide, wide)
    blocks = [matrix] + [apart_by(matrix, "gx", stride) for stride in range(2, cols_x, 2)]
    halves = jax.ShapeDtypeStruct((cells, device_count * capacity), jnp.bfloat16)
    factors, *interp = call(
        functools.partial(prepare_kernel, device_count, capacity, lon_cols),
        (f32(3, layers, 8, LANES), halves, halves),
        (
            vert_coef.reshape(layers, cells // LANES, LANES),
            obs_owner.reshape(1, obs_count),
            obs_row.reshape(1, obs_count),
            obs_col.reshape(1, obs_count),
            obs_frac.reshape(2, obs_count),
        ),
        flops=20_000_000,
        mib=16,
    )
    extended = 3 * rows + (-3 * rows) % 8
    packed, coef = call(
        functools.partial(first_lateral_kernel, kv, rows, tiles),
        (f32(cols_x, 2 * kv, LANES), f32(5, extended, lons)),
        (interp[0], direction_n, *faces, pair, cross),
        after=1,
        scratch=(
            pltpu.VMEM((3, extended, lons), jnp.float32),
            pltpu.VMEM(own.shape, jnp.float32),
            pltpu.VMEM(own.shape, jnp.float32),
        ),
        flops=4_000_000,
    )
    held_blocks = call(
        functools.partial(join_kernel, 1, len(blocks)),
        f32(len(blocks), wide, wide),
        (packed, *blocks),
        after=1,
    )

    fetched = [held_blocks] + [apart_by(held_blocks, "gy", stride) for stride in range(1, rows_y)]
    columns = lax.all_to_all(packed, "gx", split_axis=0, concat_axis=0, tiled=True)
    smoothed = call(
        functools.partial(smooth_kernel, layers, held),
        f32(2 * wide, LANES),
        (columns.reshape(cols_x * 2 * kv, LANES), factors),
        flops=1000,
    )
    far = apart_by(
        call(
            pack_kernel, f32(device_count // 2, wide // 2 + 8, wide), (smoothed, *fetched), after=1
        ),
        "gx",
        1,
    )
    half = device_count // 2 * capacity
    weighted, profile = call(
        functools.partial(profile_kernel, capacity),
        (f32(wide, half), f32(wide, half)),
        (smoothed, *interp, *fetched),
        flops=400_000_000,
        mib=16,
    )
    spread = call(
        functools.partial(spread_kernel, layers, held, capacity),
        f32(cols_x * 2 * kv, LANES),
        (weighted, profile, factors, *interp, far),
        scratch=(pltpu.VMEM((2 * wide, LANES), jnp.float32),),
        flops=400_000_000,
        mib=16,
    )
    tile = lax.all_to_all(
        spread.reshape(cols_x, 2 * kv, LANES), "gx", split_axis=0, concat_axis=0, tiled=True
    )
    pair, cross = from_neighbours(tile)
    image, sums = call(
        functools.partial(second_lateral_kernel, kv, rows, tiles),
        (f32(*direction_n.shape), f32(device_count, 1, LANES)),
        (tile, pair, cross, coef, direction_n, residual_n),
        scratch=(pltpu.VMEM(tile.shape, jnp.float32), pltpu.VMEM(tile.shape, jnp.float32)),
        flops=4_000_000,
    )
    sums = lax.all_to_all(sums, ("gy", "gx"), split_axis=0, concat_axis=0, tiled=True)
    after = call(
        update_kernel,
        (f32(*direction_n.shape),) * 3,
        (sums, direction_n, solution_n, residual_n, image),
    )
    return tuple(from_native(x, direction.shape) for x in after)


def gathers(mesh, shapes):
    rows_y, cols_x = mesh.shape["gy"], mesh.shape["gx"]
    devices = rows_y * cols_x
    if any(size < 2 or size & (size - 1) for size in (rows_y, cols_x)):
        return False
    direction, vert_coef, obs_row, error_inverse = shapes
    var_count, layers, lat_rows, lons = direction
    rows, held = lat_rows // rows_y, layers // cols_x
    obs_count, wide = obs_row[-1], error_inverse[-1]
    capacity = 2 * obs_count // devices
    return (
        rows == NSTEP == 4
        and var_count == 4
        and (var_count * held) % 8 == 0
        and lons // cols_x * 2 == LANES
        and wide == LANES
        and capacity > 0
        and LANES % capacity == 0
        and devices // 2 % (LANES // capacity) == 0
        and devices * wide * wide * 4 <= 8 * 1024 * 1024
    )


def padded(cells, sides, width):
    for axis, dim in sides:
        count = lax.axis_size(axis)
        ends = count - 1
        head = lax.slice_in_dim(cells, 0, width, axis=dim)
        tail = lax.slice_in_dim(cells, cells.shape[dim] - width, cells.shape[dim], axis=dim)
        cells = jnp.concatenate(
            [
                lax.ppermute(tail, axis, [(i, (i + 1) % count) for i in range(ends)]),
                cells,
                lax.ppermute(head, axis, [((i + 1) % count, i) for i in range(ends)]),
            ],
            axis=dim,
        )
    return cells


def lateral_faces(north_ext, east_ext, ocean_ext):
    ocean_next = jnp.concatenate([ocean_ext[1:], jnp.zeros_like(ocean_ext[:1])], axis=0)
    north_face = north_ext * ocean_ext * ocean_next
    east_face = east_ext * ocean_ext * jnp.roll(ocean_ext, -1, axis=1)
    return (north_face, east_face, ocean_ext)


def diffuse_once(values_grid, north_face, east_face, ocean_ext):
    north_flux = north_face[:-1] * (values_grid[:, :, 1:, :] - values_grid[:, :, :-1, :])
    east_flux = east_face * (jnp.roll(values_grid, -1, axis=3) - values_grid)
    lateral = east_flux - jnp.roll(east_flux, 1, axis=3)
    return (
        ocean_ext[1:-1] * values_grid[:, :, 1:-1, :]
        + north_flux[:, :, 1:, :]
        - north_flux[:, :, :-1, :]
        + lateral[:, :, 1:-1, :]
    )


def lateral_pass(values_tile, faces):
    north_face, east_face, ocean_ext = faces
    grown = padded(values_tile, (("gy", 2),), NSTEP)
    total_rows = grown.shape[2]
    for step_index in range(NSTEP):
        upper = total_rows - step_index
        grown = diffuse_once(
            grown,
            north_face[step_index:upper],
            east_face[step_index:upper],
            ocean_ext[step_index:upper],
        )
    return grown


def vertical_factors(vert_coef):
    inverse_rows = []
    upper_ratio = []
    for layer_index in range(vert_coef.shape[0]):
        diagonal = 1.0 + vert_coef[layer_index]
        if layer_index > 0:
            diagonal = (
                diagonal + vert_coef[layer_index - 1] + vert_coef[layer_index - 1] * upper_ratio[-1]
            )
        inverse = 1.0 / diagonal
        inverse_rows.append(inverse)
        upper_ratio.append(-vert_coef[layer_index] * inverse)
    return (inverse_rows, upper_ratio)


def vertical_solve(values_col, vert_coef, factors):
    inverse_rows, upper_ratio = factors
    layers = values_col.shape[1]
    forward = []
    for layer_index in range(layers):
        source = values_col[:, layer_index]
        if layer_index > 0:
            source = source + vert_coef[layer_index - 1] * forward[-1]
        forward.append(source * inverse_rows[layer_index])
    result = [forward[-1]]
    for layer_index in range(layers - 2, -1, -1):
        result.append(forward[layer_index] - upper_ratio[layer_index] * result[-1])
    return jnp.stack(result[::-1], axis=1)


def observe_weigh_spread(columns, obs_owner, obs_row, obs_col, obs_frac, error_inverse):
    var_count, lev_count, lat_rows, lon_cols = columns.shape
    kv_width = var_count * lev_count
    rows_y = lax.axis_size("gy")
    cols_x = lax.axis_size("gx")
    device_count = rows_y * cols_x
    obs_count = obs_row.shape[-1]
    capacity = 2 * obs_count // device_count
    flat = columns.reshape(kv_width, lat_rows * lon_cols)
    cell = obs_row.reshape(-1) * lon_cols + obs_col.reshape(-1)
    corners = (cell, cell + 1, cell + lon_cols, cell + lon_cols + 1)
    lat_frac = obs_frac[0, 0, 0]
    lon_frac = obs_frac[0, 0, 1]
    weights = (
        (1.0 - lat_frac) * (1.0 - lon_frac),
        (1.0 - lat_frac) * lon_frac,
        lat_frac * (1.0 - lon_frac),
        lat_frac * lon_frac,
    )
    profile = weights[0] * jnp.take(flat, corners[0], axis=1)
    for corner_index in range(1, 4):
        profile = profile + weights[corner_index] * jnp.take(flat, corners[corner_index], axis=1)
    owners = obs_owner.reshape(-1)
    onehot = (owners[:, None] == jnp.arange(device_count, dtype=jnp.int32)[None, :]).astype(
        jnp.int32
    )
    running = jnp.cumsum(onehot, axis=0)
    rank_in = jnp.sum(running * onehot, axis=1) - 1
    slot = owners * capacity + rank_in
    outgoing = jnp.zeros((device_count * capacity, kv_width), jnp.float32).at[slot].set(profile.T)
    outgoing = outgoing.reshape(rows_y, cols_x, capacity, kv_width)
    matrix = error_inverse.reshape(kv_width, kv_width)
    arrived = lax.all_to_all(
        lax.all_to_all(outgoing, "gy", split_axis=0, concat_axis=0, tiled=True),
        "gx",
        split_axis=1,
        concat_axis=1,
        tiled=True,
    )
    weighted = jnp.dot(
        arrived.reshape(-1, kv_width),
        matrix,
        precision=lax.Precision.HIGHEST,
        preferred_element_type=jnp.float32,
    ).reshape(rows_y, cols_x, capacity, kv_width)
    returned = lax.all_to_all(
        lax.all_to_all(weighted, "gy", split_axis=0, concat_axis=0, tiled=True),
        "gx",
        split_axis=1,
        concat_axis=1,
        tiled=True,
    )
    back = returned.reshape(device_count * capacity, kv_width)[slot].T
    spread = jnp.zeros((kv_width, lat_rows * lon_cols), jnp.float32)
    for corner_index in range(4):
        spread = spread.at[:, corners[corner_index]].add(weights[corner_index] * back)
    return spread.reshape(var_count, lev_count, lat_rows, lon_cols)


def per_device(
    direction,
    solution,
    residual,
    north_coef,
    east_coef,
    ocean,
    vert_coef,
    obs_owner,
    obs_row,
    obs_col,
    obs_frac,
    error_inverse,
):
    stacked = jnp.stack([north_coef, east_coef, ocean.astype(jnp.float32)])
    reach = NSTEP
    grown_coef = padded(stacked, (("gy", 1),), reach)
    faces = lateral_faces(grown_coef[0], grown_coef[1], grown_coef[2])
    factors = vertical_factors(vert_coef)
    smoothed = lateral_pass(direction, faces)
    columns = lax.all_to_all(smoothed, "gx", split_axis=3, concat_axis=1, tiled=True)
    columns = vertical_solve(columns, vert_coef, factors)
    spread = observe_weigh_spread(columns, obs_owner, obs_row, obs_col, obs_frac, error_inverse)
    spread = vertical_solve(spread, vert_coef, factors)
    tiles = lax.all_to_all(spread, "gx", split_axis=1, concat_axis=3, tiled=True)
    image = direction + lateral_pass(tiles, faces)
    norm_now, curvature = lax.psum(
        (jnp.sum(residual * residual), jnp.sum(direction * image)), ("gy", "gx")
    )
    alpha = norm_now / curvature
    residual_next = residual - alpha * image
    norm_next = lax.psum(jnp.sum(residual_next * residual_next), ("gy", "gx"))
    solution_next = solution + alpha * direction
    direction_next = residual_next + norm_next / norm_now * direction
    return (solution_next, residual_next, direction_next)


def solution(mesh):
    in_specs = (
        P(None, "gx", "gy", None),
        P(None, "gx", "gy", None),
        P(None, "gx", "gy", None),
        P("gy", None),
        P("gy", None),
        P("gy", None),
        P(None, "gy", "gx"),
        P("gy", "gx", None, None),
        P("gy", "gx", None),
        P("gy", "gx", None),
        P("gy", "gx", None, None),
        P("gy", "gx", None, None),
    )
    out_specs = (P(None, "gx", "gy", None),) * 3

    def step(*arrays):
        shapes = [arrays[at].shape for at in (0, 6, 8, 11)]
        local = per_device_gathered if gathers(mesh, shapes) else per_device
        return jax.shard_map(
            local, mesh=mesh, in_specs=in_specs, out_specs=out_specs, check_vma=False
        )(*arrays)

    return step
```

```python
import functools
import math

import jax
import jax.numpy as jnp
from jax import lax
from jax.experimental import pallas as pl
from jax.experimental.pallas import tpu as pltpu
from jax.sharding import PartitionSpec as P

NSTEP = 4
LANES = 128


def to_native(tile):
    kv, rows, lons = tile.shape[0] * tile.shape[1], tile.shape[2], tile.shape[3]
    return tile.reshape(kv, rows, lons // LANES, LANES).swapaxes(1, 2).reshape(-1, LANES)


def from_native(flat, shape):
    kv, rows, lons = shape[0] * shape[1], shape[2], shape[3]
    return flat.reshape(kv, lons // LANES, rows, LANES).swapaxes(1, 2).reshape(shape)


def native_rows(ref, row, rows, tiles, half):
    parts = [
        ref[pl.ds((half * 8 * tiles + tile) * rows + row, 8, stride=tiles * rows), :]
        for tile in range(tiles)
    ]
    return jnp.concatenate(parts, axis=1)


def lane_low(shape):
    return lax.broadcasted_iota(jnp.int32, shape, 1) < LANES // 2


def lateral_rows(rows, coef, reach):
    for step in range(reach):
        after = []
        for i in range(1, len(rows) - 1):
            at = step + i
            u = rows[i]
            width = u.shape[1]
            after.append(
                coef[0, at : at + 1, :] * u
                + coef[1, at : at + 1, :] * rows[i + 1]
                + coef[2, at : at + 1, :] * rows[i - 1]
                + coef[3, at : at + 1, :] * pltpu.roll(u, width - 1, 1)
                + coef[4, at : at + 1, :] * pltpu.roll(u, 1, 1)
            )
        rows = after
    return rows


def sort_halo(pair_ref, cross_ref, low_ref, high_ref):
    odd = lax.rem(lax.axis_index("gy"), 2) == 1

    @pl.when(odd)
    def _():
        low_ref[...] = pair_ref[...]
        high_ref[...] = cross_ref[...]

    @pl.when(jnp.logical_not(odd))
    def _():
        low_ref[...] = cross_ref[...]
        high_ref[...] = pair_ref[...]


def triangle_masks():
    shape = (LANES // 2, LANES)
    lane = lax.broadcasted_iota(jnp.int32, shape, 1)
    return lane, lane - lax.broadcasted_iota(jnp.int32, shape, 0)


def pack_symmetric(matrix, packed_ref):
    half = LANES // 2
    lane, away = triangle_masks()
    top, bottom = matrix[:half], matrix[half:]
    corner = jnp.where(away <= 0, top, pltpu.roll(bottom, half, 1))
    packed_ref[0:half, :] = jnp.where(lane < half, corner, top)
    diagonal = jnp.sum(jnp.where(away == half, bottom, 0.0), axis=0, keepdims=True)
    packed_ref[half:, :] = jnp.broadcast_to(diagonal, (packed_ref.shape[0] - half, LANES))


def unpack_symmetric(packed):
    half = LANES // 2
    lane, away = triangle_masks()
    rows, diagonal = packed[:half], packed[half : half + 1]
    turned = jnp.concatenate([rows, rows], axis=0).T
    top = jnp.where((lane < half) & (away > 0), turned[:half], rows)
    corner = jnp.where(
        away > half, pltpu.roll(rows, half, 1), jnp.where(away == half, diagonal, turned[:half])
    )
    return jnp.concatenate([top, jnp.where(lane < half, turned[half:], corner)], axis=0)


def halo_kernel(
    chunks, direction_ref, north_ref, east_ref, ocean_ref, own_ref, stage_ref, mask_ref, sems
):
    cells, size = direction_ref.shape[0], north_ref.shape[0]
    rows = cells // chunks
    spans = [(at * rows, rows) for at in range(chunks)] + [(cells, 2 * size)]
    faces = [
        pltpu.make_async_copy(ref, to, sems.at[0, at])
        for at, (ref, to) in enumerate(
            (
                (ocean_ref, mask_ref),
                (north_ref, stage_ref.at[pl.ds(cells, size)]),
                (east_ref, stage_ref.at[pl.ds(cells + size, size)]),
            )
        )
    ]
    arrive = [
        pltpu.make_async_copy(
            direction_ref.at[pl.ds(start, count)], stage_ref.at[pl.ds(start, count)], sems.at[0, 3 + at]
        )
        for at, (start, count) in enumerate(spans[:-1])
    ]
    leave = [
        pltpu.make_async_copy(
            stage_ref.at[pl.ds(start, count)], own_ref.at[pl.ds(start, count)], sems.at[1, at]
        )
        for at, (start, count) in enumerate(spans)
    ]
    for copy in arrive + faces:
        copy.start()
    for at, copy in enumerate(arrive):
        copy.wait()
        leave[at].start()
    for copy in faces:
        copy.wait()
    mask = mask_ref[...].astype(jnp.float32)
    for kind in range(2):
        here = slice(cells + kind * size, cells + (kind + 1) * size)
        stage_ref[here, :] = stage_ref[here, :] * mask
    leave[-1].start()
    for copy in leave:
        copy.wait()


def join_kernel(after, count, *refs):
    blocks, (near_ref,) = refs[after : after + count], refs[after + count :]
    size = blocks[0].shape[0]
    for at, block in enumerate(blocks):
        near_ref[at * size : (at + 1) * size] = block[...]


def pack_kernel(_, *refs):
    blocks, (packed_ref,) = refs[:-1], refs[-1:]
    size = blocks[0].shape[0]
    for at, block in enumerate(blocks):
        for inner in range(size):
            pack_symmetric(block[inner], packed_ref.at[at * size + inner])


def first_lateral_kernel(
    kv,
    rows,
    tiles,
    _,
    own_ref,
    north_ref,
    east_ref,
    ocean_ref,
    pair_ref,
    cross_ref,
    packed_ref,
    coef_ref,
    ext_ref,
    low_ref,
    high_ref,
):
    lons = tiles * LANES
    cells = kv * tiles * rows
    sort_halo(pair_ref, cross_ref, low_ref, high_ref)
    at_y, rows_y = lax.axis_index("gy"), lax.axis_size("gy")
    inside = (
        jnp.where(at_y > 0, 1.0, 0.0).astype(jnp.float32),
        jnp.where(at_y < rows_y - 1, 1.0, 0.0).astype(jnp.float32),
    )
    ext_ref[...] = jnp.zeros_like(ext_ref)
    for tile in range(tiles):
        lanes = slice(tile * LANES, (tile + 1) * LANES)
        here = slice(tile * rows, (tile + 1) * rows)
        mask = ocean_ref[here, :].astype(jnp.float32)
        ext_ref[0, rows : 2 * rows, lanes] = north_ref[here, :] * mask
        ext_ref[1, rows : 2 * rows, lanes] = east_ref[here, :] * mask
        ext_ref[2, rows : 2 * rows, lanes] = mask
        for block, ref in ((0, low_ref), (2, high_ref)):
            across = slice(block * rows, (block + 1) * rows)
            for kind in range(2):
                start = cells + (kind * tiles + tile) * rows
                ext_ref[kind, across, lanes] = ref[start : start + rows, :] * inside[block // 2]
            ext_ref[2, across, lanes] = jnp.where(ext_ref[0, across, lanes] > 0.0, 1.0, 0.0)
    total = ext_ref.shape[1]
    ocean = ext_ref[2]
    north_face = ext_ref[0] * pltpu.roll(ocean, total - 1, 0)
    east_face = ext_ref[1] * pltpu.roll(ocean, lons - 1, 1)
    south_face = pltpu.roll(north_face, 1, 0)
    west_face = pltpu.roll(east_face, 1, 1)
    coef_ref[0] = ocean - north_face - south_face - east_face - west_face
    coef_ref[1] = north_face
    coef_ref[2] = south_face
    coef_ref[3] = east_face
    coef_ref[4] = west_face
    low = lane_low((8, LANES))
    for half in range(kv // 8):
        grown = [
            native_rows(ref, row, rows, tiles, half)
            for ref in (low_ref, own_ref, high_ref)
            for row in range(rows)
        ]
        done = lateral_rows(grown, coef_ref, rows)
        for pair in range(rows // 2):
            at = pair * kv + half * 8
            for tile in range(tiles):
                first = done[2 * pair][:, tile * LANES : (tile + 1) * LANES]
                second = done[2 * pair + 1][:, tile * LANES : (tile + 1) * LANES]
                packed_ref[2 * tile, at : at + 8, :] = jnp.where(
                    low, first, pltpu.roll(second, LANES // 2, 1)
                )
                packed_ref[2 * tile + 1, at : at + 8, :] = jnp.where(
                    low, pltpu.roll(first, LANES // 2, 1), second
                )


def second_lateral_kernel(
    kv,
    rows,
    tiles,
    own_ref,
    pair_ref,
    cross_ref,
    coef_ref,
    direction_ref,
    residual_ref,
    image_ref,
    sums_ref,
    low_ref,
    high_ref,
):
    sort_halo(pair_ref, cross_ref, low_ref, high_ref)
    low = lane_low((8, LANES))
    totals = [jnp.zeros((8, tiles * LANES), jnp.float32) for _ in range(4)]
    for half in range(kv // 8):
        grown = []
        for ref in (low_ref, own_ref, high_ref):
            for pair in range(rows // 2):
                firsts, seconds = [], []
                at = pair * kv + half * 8
                for tile in range(tiles):
                    even = ref[2 * tile, at : at + 8, :]
                    odd = ref[2 * tile + 1, at : at + 8, :]
                    firsts.append(jnp.where(low, even, pltpu.roll(odd, LANES // 2, 1)))
                    seconds.append(jnp.where(low, pltpu.roll(even, LANES // 2, 1), odd))
                grown.append(jnp.concatenate(firsts, axis=1))
                grown.append(jnp.concatenate(seconds, axis=1))
        done = lateral_rows(grown, coef_ref, rows)
        for row in range(rows):
            direction = native_rows(direction_ref, row, rows, tiles, half)
            residual = native_rows(residual_ref, row, rows, tiles, half)
            image = direction + done[row]
            for tile in range(tiles):
                image_ref[pl.ds((half * 8 * tiles + tile) * rows + row, 8, stride=tiles * rows), :] = image[
                    :, tile * LANES : (tile + 1) * LANES
                ]
            totals[0] = totals[0] + residual * residual
            totals[1] = totals[1] + direction * image
            totals[2] = totals[2] + residual * image
            totals[3] = totals[3] + image * image
    lane = lax.broadcasted_iota(jnp.int32, (1, LANES), 1)
    line = jnp.zeros((1, LANES), jnp.float32)
    for at, total in enumerate(totals):
        line = jnp.where(lane == at, jnp.sum(total), line)
    for device in range(sums_ref.shape[0]):
        sums_ref[device] = line


def update_kernel(sums_ref, direction_ref, solution_ref, residual_ref, image_ref, sol_ref, res_ref, dir_ref):
    line = jnp.sum(sums_ref[...], axis=0)
    lane = lax.broadcasted_iota(jnp.int32, line.shape, 1)

    def pick(at):
        return jnp.sum(jnp.where(lane == at, line, 0.0), axis=1, keepdims=True)

    norm_now, curvature, cross, square = pick(0), pick(1), pick(2), pick(3)
    alpha = norm_now / curvature
    norm_next = norm_now - 2.0 * alpha * cross + alpha * alpha * square
    beta = norm_next / norm_now
    direction = direction_ref[...]
    residual_next = residual_ref[...] - alpha * image_ref[...]
    sol_ref[...] = solution_ref[...] + alpha * direction
    res_ref[...] = residual_next
    dir_ref[...] = residual_next + beta * direction


def split(value):
    high = value.astype(jnp.bfloat16)
    return high, (value - high.astype(jnp.float32)).astype(jnp.bfloat16)


def dot_parts(left, right, contract):
    dims = (contract, ((), ()))
    total = lax.dot_general(left[0], right[0], dims, preferred_element_type=jnp.float32)
    total = total + lax.dot_general(left[0], right[1], dims, preferred_element_type=jnp.float32)
    return total + lax.dot_general(left[1], right[0], dims, preferred_element_type=jnp.float32)


def prepare_kernel(
    devices,
    capacity,
    lon_cols,
    vert_ref,
    owner_ref,
    row_ref,
    col_ref,
    frac_ref,
    factor_ref,
    high_ref,
    low_ref,
):
    vertical_factors_of(vert_ref, factor_ref)
    count = owner_ref.shape[1]
    slots = devices * capacity
    me = lax.axis_index("gy") * lax.axis_size("gx") + lax.axis_index("gx")
    apart = jnp.bitwise_xor(owner_ref[...], me)
    place = jnp.bitwise_and(apart, 1) * (devices // 2) + jnp.right_shift(apart, 1)
    named = lax.broadcasted_iota(jnp.int32, (devices, count), 0) == place
    before = lax.broadcasted_iota(jnp.int32, (count, count), 0) <= lax.broadcasted_iota(
        jnp.int32, (count, count), 1
    )
    running = jnp.dot(
        jnp.where(named, 1.0, 0.0).astype(jnp.bfloat16),
        jnp.where(before, 1.0, 0.0).astype(jnp.bfloat16),
        preferred_element_type=jnp.float32,
    )
    rank = jnp.sum(jnp.where(named, running, 0.0), axis=0, keepdims=True) - 1.0
    slot = place * capacity + rank.astype(jnp.int32)
    chosen = jnp.where(
        lax.broadcasted_iota(jnp.int32, (slots, count), 0) == slot, 1.0, 0.0
    ).astype(jnp.bfloat16)
    lat_frac = frac_ref[0:1, :]
    lon_frac = frac_ref[1:2, :]
    cell = (row_ref[...] * lon_cols + col_ref[...]).astype(jnp.float32)
    values = jnp.concatenate(
        [
            (1.0 - lat_frac) * (1.0 - lon_frac),
            (1.0 - lat_frac) * lon_frac,
            lat_frac * (1.0 - lon_frac),
            lat_frac * lon_frac,
            cell,
            jnp.zeros((3, count), jnp.float32),
        ],
        axis=0,
    )
    high, rest = split(values)
    low, rest = split(values - high.astype(jnp.float32))
    parts = jnp.concatenate([high.astype(jnp.float32), low.astype(jnp.float32), rest.astype(jnp.float32)], axis=0)
    placed = lax.dot_general(
        parts.astype(jnp.bfloat16), chosen, (((1,), (1,)), ((), ())), preferred_element_type=jnp.float32
    )
    placed = placed[0:8] + placed[8:16] + placed[16:24]
    first = jnp.round(placed[4:5, :]).astype(jnp.int32)
    away = lax.broadcasted_iota(jnp.int32, high_ref.shape, 0) - first
    interp = jnp.where(
        away == 0,
        placed[0:1, :],
        jnp.where(
            away == 1,
            placed[1:2, :],
            jnp.where(away == lon_cols, placed[2:3, :], jnp.where(away == lon_cols + 1, placed[3:4, :], 0.0)),
        ),
    )
    high_ref[...], low_ref[...] = split(interp)


def vertical_factors_of(vert_ref, factor_ref):
    layers = vert_ref.shape[0]
    top = lax.broadcasted_iota(jnp.int32, (8, LANES), 0) < 4
    coef = [jnp.where(top, vert_ref[layer, 0:1, :], vert_ref[layer, 1:2, :]) for layer in range(layers)]
    ratio = None
    for layer in range(layers):
        diagonal = 1.0 + coef[layer]
        if layer > 0:
            diagonal = diagonal + coef[layer - 1] - coef[layer - 1] * ratio
        inverse = 1.0 / diagonal
        ratio = coef[layer] * inverse
        factor_ref[0, layer] = inverse
        factor_ref[1, layer] = coef[layer - 1] * inverse if layer > 0 else jnp.zeros_like(inverse)
        factor_ref[2, layer] = ratio


def solve_columns(read, write, factor_ref, layers):
    forward = []
    for layer in range(layers):
        value = read(layer) * factor_ref[0, layer]
        if layer > 0:
            value = value + factor_ref[1, layer] * forward[-1]
        forward.append(value)
    value = forward[-1]
    write(layers - 1, value)
    for layer in range(layers - 2, -1, -1):
        value = forward[layer] + factor_ref[2, layer] * value
        write(layer, value)


def packed_at(layer, held):
    return pl.ds((layer // held) * 8 * held + layer % held, 8, stride=held)


def weigh(profile, matrices, capacity):
    kv = profile.shape[0]
    owners = LANES // capacity
    mine = lax.broadcasted_iota(jnp.int32, (kv, LANES), 1) // capacity
    tiles = []
    for tile in range(profile.shape[1] // LANES):
        values = profile[:, tile * LANES : (tile + 1) * LANES]
        masked = jnp.concatenate([jnp.where(mine == owner, values, 0.0) for owner in range(owners)], axis=0)
        beside = jnp.concatenate([matrices(tile * owners + owner) for owner in range(owners)], axis=1)
        tiles.append(dot_parts(split(beside), split(masked), ((1,), (0,))))
    return jnp.concatenate(tiles, axis=1)


def smooth_kernel(layers, held, packed_ref, factor_ref, column_ref):
    def read(layer):
        return packed_ref[packed_at(layer, held), :]

    def write(layer, value):
        column_ref[pl.ds(layer, 8, stride=layers), :] = value

    solve_columns(read, write, factor_ref, layers)


def profile_kernel(capacity, column_ref, high_ref, low_ref, *refs):
    near_refs, (weighted_ref, profile_ref) = refs[:-2], refs[-2:]
    kv, half = profile_ref.shape
    size = near_refs[0].shape[0]
    columns = jnp.concatenate([column_ref[0:kv, :], column_ref[kv : 2 * kv, :]], axis=1)
    profile = dot_parts(split(columns), (high_ref[...], low_ref[...]), ((1,), (0,)))
    profile_ref[...] = profile[:, half:]
    weighted_ref[...] = weigh(profile[:, :half], lambda at: near_refs[at // size][at % size], capacity)


def spread_kernel(
    layers, held, capacity, near_ref, profile_ref, factor_ref, high_ref, low_ref, far_ref, out_ref, column_ref
):
    kv = near_ref.shape[0]
    weighted = jnp.concatenate([near_ref[...], weigh(profile_ref[...], lambda at: unpack_symmetric(far_ref[at]), capacity)], axis=1)
    spread = dot_parts(split(weighted), (high_ref[...], low_ref[...]), ((1,), (1,)))
    column_ref[0:kv, :] = spread[:, :LANES]
    column_ref[kv : 2 * kv, :] = spread[:, LANES:]

    def read(layer):
        return column_ref[pl.ds(layer, 8, stride=layers), :]

    def write(layer, value):
        out_ref[packed_at(layer, held), :] = value

    solve_columns(read, write, factor_ref, layers)


def vmem(count):
    return [pl.BlockSpec(memory_space=pltpu.VMEM)] * count


def call(kernel, out_shape, inputs, scratch=(), after=0, hbm=False, flops=1_000_000, mib=8):
    specs = [pl.BlockSpec(memory_space=pl.ANY)] * after + vmem(len(inputs) - after)
    outs = vmem(len(out_shape) if isinstance(out_shape, tuple) else 1)
    if hbm:
        specs, outs = ([pl.BlockSpec(memory_space=pltpu.HBM)] * len(x) for x in (specs, outs))
    moved = sum(math.prod(x.shape) * 4 for x in inputs)
    return pl.pallas_call(
        kernel,
        out_shape=out_shape,
        in_specs=specs,
        out_specs=tuple(outs) if isinstance(out_shape, tuple) else outs[0],
        scratch_shapes=list(scratch),
        compiler_params=pltpu.CompilerParams(vmem_limit_bytes=mib * 1024 * 1024),
        cost_estimate=pl.CostEstimate(flops=flops, bytes_accessed=moved, transcendentals=0),
    )(*inputs)


def f32(*shape):
    return jax.ShapeDtypeStruct(shape, jnp.float32)


def from_neighbours(block):
    count = lax.axis_size("gy")
    pair = lax.ppermute(block, "gy", [(i, i ^ 1) for i in range(count)])
    cross = lax.ppermute(block, "gy", [(i, (i + (1 if i % 2 else -1)) % count) for i in range(count)])
    return pair, cross


def apart_by(block, axis, stride):
    return lax.ppermute(block, axis, [(i, i ^ stride) for i in range(lax.axis_size(axis))])


def per_device_gathered(
    direction,
    solution,
    residual,
    north_coef,
    east_coef,
    ocean,
    vert_coef,
    obs_owner,
    obs_row,
    obs_col,
    obs_frac,
    error_inverse,
):
    var_count, held, rows, lons = direction.shape
    kv = var_count * held
    tiles = lons // LANES
    layers, _, lon_cols = vert_coef.shape
    rows_y, cols_x = lax.axis_size("gy"), lax.axis_size("gx")
    device_count = rows_y * cols_x
    obs_count = obs_row.shape[-1]
    capacity = 2 * obs_count // device_count
    wide = error_inverse.shape[-1]
    cells = rows * lon_cols

    direction_n = to_native(direction)
    residual_n = to_native(residual)
    solution_n = to_native(solution)
    faces = [to_native(x[None, None]) for x in (north_coef, east_coef, ocean)]
    own = call(
        functools.partial(halo_kernel, 4),
        f32(direction_n.shape[0] + 2 * faces[0].shape[0], LANES),
        (direction_n, *faces),
        scratch=(
            pltpu.VMEM((direction_n.shape[0] + 2 * faces[0].shape[0], LANES), jnp.float32),
            pltpu.VMEM(faces[0].shape, jnp.int32),
            pltpu.SemaphoreType.DMA((2, 7)),
        ),
        hbm=True,
        mib=56,
    )
    pair, cross = from_neighbours(own)

    matrix = error_inverse.reshape(1, wide, wide)
    blocks = [matrix] + [apart_by(matrix, "gx", stride) for stride in range(2, cols_x, 2)]
    halves = jax.ShapeDtypeStruct((cells, device_count * capacity), jnp.bfloat16)
    factors, *interp = call(
        functools.partial(prepare_kernel, device_count, capacity, lon_cols),
        (f32(3, layers, 8, LANES), halves, halves),
        (
            vert_coef.reshape(layers, cells // LANES, LANES),
            obs_owner.reshape(1, obs_count),
            obs_row.reshape(1, obs_count),
            obs_col.reshape(1, obs_count),
            obs_frac.reshape(2, obs_count),
        ),
        flops=20_000_000,
        mib=16,
    )
    extended = 3 * rows + (-3 * rows) % 8
    packed, coef = call(
        functools.partial(first_lateral_kernel, kv, rows, tiles),
        (f32(cols_x, 2 * kv, LANES), f32(5, extended, lons)),
        (interp[0], direction_n, *faces, pair, cross),
        after=1,
        scratch=(
            pltpu.VMEM((3, extended, lons), jnp.float32),
            pltpu.VMEM(own.shape, jnp.float32),
            pltpu.VMEM(own.shape, jnp.float32),
        ),
        flops=4_000_000,
    )
    held_blocks = call(
        functools.partial(join_kernel, 1, len(blocks)),
        f32(len(blocks), wide, wide),
        (packed, *blocks),
        after=1,
    )

    fetched = [held_blocks] + [apart_by(held_blocks, "gy", stride) for stride in range(1, rows_y)]
    columns = lax.all_to_all(packed, "gx", split_axis=0, concat_axis=0, tiled=True)
    smoothed = call(
        functools.partial(smooth_kernel, layers, held),
        f32(2 * wide, LANES),
        (columns.reshape(cols_x * 2 * kv, LANES), factors),
        flops=1000,
    )
    far = apart_by(
        call(
            pack_kernel, f32(device_count // 2, wide // 2 + 8, wide), (smoothed, *fetched), after=1
        ),
        "gx",
        1,
    )
    half = device_count // 2 * capacity
    weighted, profile = call(
        functools.partial(profile_kernel, capacity),
        (f32(wide, half), f32(wide, half)),
        (smoothed, *interp, *fetched),
        flops=400_000_000,
        mib=16,
    )
    spread = call(
        functools.partial(spread_kernel, layers, held, capacity),
        f32(cols_x * 2 * kv, LANES),
        (weighted, profile, factors, *interp, far),
        scratch=(pltpu.VMEM((2 * wide, LANES), jnp.float32),),
        flops=400_000_000,
        mib=16,
    )
    tile = lax.all_to_all(
        spread.reshape(cols_x, 2 * kv, LANES), "gx", split_axis=0, concat_axis=0, tiled=True
    )
    pair, cross = from_neighbours(tile)
    image, sums = call(
        functools.partial(second_lateral_kernel, kv, rows, tiles),
        (f32(*direction_n.shape), f32(device_count, 1, LANES)),
        (tile, pair, cross, coef, direction_n, residual_n),
        scratch=(pltpu.VMEM(tile.shape, jnp.float32), pltpu.VMEM(tile.shape, jnp.float32)),
        flops=4_000_000,
    )
    sums = lax.all_to_all(sums, ("gy", "gx"), split_axis=0, concat_axis=0, tiled=True)
    after = call(
        update_kernel,
        (f32(*direction_n.shape),) * 3,
        (sums, direction_n, solution_n, residual_n, image),
    )
    return tuple(from_native(x, direction.shape) for x in after)


def gathers(mesh, shapes):
    rows_y, cols_x = mesh.shape["gy"], mesh.shape["gx"]
    devices = rows_y * cols_x
    if any(size < 2 or size & (size - 1) for size in (rows_y, cols_x)):
        return False
    direction, vert_coef, obs_row, error_inverse = shapes
    var_count, layers, lat_rows, lons = direction
    rows, held = lat_rows // rows_y, layers // cols_x
    obs_count, wide = obs_row[-1], error_inverse[-1]
    capacity = 2 * obs_count // devices
    return (
        rows == NSTEP == 4
        and var_count == 4
        and (var_count * held) % 8 == 0
        and lons // cols_x * 2 == LANES
        and wide == LANES
        and capacity > 0
        and LANES % capacity == 0
        and devices // 2 % (LANES // capacity) == 0
        and devices * wide * wide * 4 <= 8 * 1024 * 1024
    )


def padded(cells, sides, width):
    for axis, dim in sides:
        count = lax.axis_size(axis)
        ends = count - 1
        head = lax.slice_in_dim(cells, 0, width, axis=dim)
        tail = lax.slice_in_dim(cells, cells.shape[dim] - width, cells.shape[dim], axis=dim)
        cells = jnp.concatenate(
            [
                lax.ppermute(tail, axis, [(i, (i + 1) % count) for i in range(ends)]),
                cells,
                lax.ppermute(head, axis, [((i + 1) % count, i) for i in range(ends)]),
            ],
            axis=dim,
        )
    return cells


def lateral_faces(north_ext, east_ext, ocean_ext):
    ocean_next = jnp.concatenate([ocean_ext[1:], jnp.zeros_like(ocean_ext[:1])], axis=0)
    north_face = north_ext * ocean_ext * ocean_next
    east_face = east_ext * ocean_ext * jnp.roll(ocean_ext, -1, axis=1)
    return (north_face, east_face, ocean_ext)


def diffuse_once(values_grid, north_face, east_face, ocean_ext):
    north_flux = north_face[:-1] * (values_grid[:, :, 1:, :] - values_grid[:, :, :-1, :])
    east_flux = east_face * (jnp.roll(values_grid, -1, axis=3) - values_grid)
    lateral = east_flux - jnp.roll(east_flux, 1, axis=3)
    return (
        ocean_ext[1:-1] * values_grid[:, :, 1:-1, :]
        + north_flux[:, :, 1:, :]
        - north_flux[:, :, :-1, :]
        + lateral[:, :, 1:-1, :]
    )


def lateral_pass(values_tile, faces):
    north_face, east_face, ocean_ext = faces
    grown = padded(values_tile, (("gy", 2),), NSTEP)
    total_rows = grown.shape[2]
    for step_index in range(NSTEP):
        upper = total_rows - step_index
        grown = diffuse_once(
            grown,
            north_face[step_index:upper],
            east_face[step_index:upper],
            ocean_ext[step_index:upper],
        )
    return grown


def vertical_factors(vert_coef):
    inverse_rows = []
    upper_ratio = []
    for layer_index in range(vert_coef.shape[0]):
        diagonal = 1.0 + vert_coef[layer_index]
        if layer_index > 0:
            diagonal = (
                diagonal + vert_coef[layer_index - 1] + vert_coef[layer_index - 1] * upper_ratio[-1]
            )
        inverse = 1.0 / diagonal
        inverse_rows.append(inverse)
        upper_ratio.append(-vert_coef[layer_index] * inverse)
    return (inverse_rows, upper_ratio)


def vertical_solve(values_col, vert_coef, factors):
    inverse_rows, upper_ratio = factors
    layers = values_col.shape[1]
    forward = []
    for layer_index in range(layers):
        source = values_col[:, layer_index]
        if layer_index > 0:
            source = source + vert_coef[layer_index - 1] * forward[-1]
        forward.append(source * inverse_rows[layer_index])
    result = [forward[-1]]
    for layer_index in range(layers - 2, -1, -1):
        result.append(forward[layer_index] - upper_ratio[layer_index] * result[-1])
    return jnp.stack(result[::-1], axis=1)


def observe_weigh_spread(columns, obs_owner, obs_row, obs_col, obs_frac, error_inverse):
    var_count, lev_count, lat_rows, lon_cols = columns.shape
    kv_width = var_count * lev_count
    rows_y = lax.axis_size("gy")
    cols_x = lax.axis_size("gx")
    device_count = rows_y * cols_x
    obs_count = obs_row.shape[-1]
    capacity = 2 * obs_count // device_count
    flat = columns.reshape(kv_width, lat_rows * lon_cols)
    cell = obs_row.reshape(-1) * lon_cols + obs_col.reshape(-1)
    corners = (cell, cell + 1, cell + lon_cols, cell + lon_cols + 1)
    lat_frac = obs_frac[0, 0, 0]
    lon_frac = obs_frac[0, 0, 1]
    weights = (
        (1.0 - lat_frac) * (1.0 - lon_frac),
        (1.0 - lat_frac) * lon_frac,
        lat_frac * (1.0 - lon_frac),
        lat_frac * lon_frac,
    )
    profile = weights[0] * jnp.take(flat, corners[0], axis=1)
    for corner_index in range(1, 4):
        profile = profile + weights[corner_index] * jnp.take(flat, corners[corner_index], axis=1)
    owners = obs_owner.reshape(-1)
    onehot = (owners[:, None] == jnp.arange(device_count, dtype=jnp.int32)[None, :]).astype(
        jnp.int32
    )
    running = jnp.cumsum(onehot, axis=0)
    rank_in = jnp.sum(running * onehot, axis=1) - 1
    slot = owners * capacity + rank_in
    outgoing = jnp.zeros((device_count * capacity, kv_width), jnp.float32).at[slot].set(profile.T)
    outgoing = outgoing.reshape(rows_y, cols_x, capacity, kv_width)
    matrix = error_inverse.reshape(kv_width, kv_width)
    arrived = lax.all_to_all(
        lax.all_to_all(outgoing, "gy", split_axis=0, concat_axis=0, tiled=True),
        "gx",
        split_axis=1,
        concat_axis=1,
        tiled=True,
    )
    weighted = jnp.dot(
        arrived.reshape(-1, kv_width),
        matrix,
        precision=lax.Precision.HIGHEST,
        preferred_element_type=jnp.float32,
    ).reshape(rows_y, cols_x, capacity, kv_width)
    returned = lax.all_to_all(
        lax.all_to_all(weighted, "gy", split_axis=0, concat_axis=0, tiled=True),
        "gx",
        split_axis=1,
        concat_axis=1,
        tiled=True,
    )
    back = returned.reshape(device_count * capacity, kv_width)[slot].T
    spread = jnp.zeros((kv_width, lat_rows * lon_cols), jnp.float32)
    for corner_index in range(4):
        spread = spread.at[:, corners[corner_index]].add(weights[corner_index] * back)
    return spread.reshape(var_count, lev_count, lat_rows, lon_cols)


def per_device(
    direction,
    solution,
    residual,
    north_coef,
    east_coef,
    ocean,
    vert_coef,
    obs_owner,
    obs_row,
    obs_col,
    obs_frac,
    error_inverse,
):
    stacked = jnp.stack([north_coef, east_coef, ocean.astype(jnp.float32)])
    reach = NSTEP
    grown_coef = padded(stacked, (("gy", 1),), reach)
    faces = lateral_faces(grown_coef[0], grown_coef[1], grown_coef[2])
    factors = vertical_factors(vert_coef)
    smoothed = lateral_pass(direction, faces)
    columns = lax.all_to_all(smoothed, "gx", split_axis=3, concat_axis=1, tiled=True)
    columns = vertical_solve(columns, vert_coef, factors)
    spread = observe_weigh_spread(columns, obs_owner, obs_row, obs_col, obs_frac, error_inverse)
    spread = vertical_solve(spread, vert_coef, factors)
    tiles = lax.all_to_all(spread, "gx", split_axis=1, concat_axis=3, tiled=True)
    image = direction + lateral_pass(tiles, faces)
    norm_now, curvature = lax.psum(
        (jnp.sum(residual * residual), jnp.sum(direction * image)), ("gy", "gx")
    )
    alpha = norm_now / curvature
    residual_next = residual - alpha * image
    norm_next = lax.psum(jnp.sum(residual_next * residual_next), ("gy", "gx"))
    solution_next = solution + alpha * direction
    direction_next = residual_next + norm_next / norm_now * direction
    return (solution_next, residual_next, direction_next)


def solution(mesh):
    in_specs = (
        P(None, "gx", "gy", None),
        P(None, "gx", "gy", None),
        P(None, "gx", "gy", None),
        P("gy", None),
        P("gy", None),
        P("gy", None),
        P(None, "gy", "gx"),
        P("gy", "gx", None, None),
        P("gy", "gx", None),
        P("gy", "gx", None),
        P("gy", "gx", None, None),
        P("gy", "gx", None, None),
    )
    out_specs = (P(None, "gx", "gy", None),) * 3

    def step(*arrays):
        shapes = [arrays[at].shape for at in (0, 6, 8, 11)]
        local = per_device_gathered if gathers(mesh, shapes) else per_device
        return jax.shard_map(
            local, mesh=mesh, in_specs=in_specs, out_specs=out_specs, check_vma=False
        )(*arrays)

    return step
```

```python
import functools
import math

import jax
import jax.numpy as jnp
from jax import lax
from jax.experimental import pallas as pl
from jax.experimental.pallas import tpu as pltpu
from jax.sharding import PartitionSpec as P

NSTEP = 4
LANES = 128


def to_native(tile):
    kv, rows, lons = tile.shape[0] * tile.shape[1], tile.shape[2], tile.shape[3]
    return tile.reshape(kv, rows, lons // LANES, LANES).swapaxes(1, 2).reshape(-1, LANES)


def from_native(flat, shape):
    kv, rows, lons = shape[0] * shape[1], shape[2], shape[3]
    return flat.reshape(kv, lons // LANES, rows, LANES).swapaxes(1, 2).reshape(shape)


def native_rows(ref, row, rows, tiles, half):
    parts = [
        ref[pl.ds((half * 8 * tiles + tile) * rows + row, 8, stride=tiles * rows), :]
        for tile in range(tiles)
    ]
    return jnp.concatenate(parts, axis=1)


def lane_low(shape):
    return lax.broadcasted_iota(jnp.int32, shape, 1) < LANES // 2


def lateral_rows(rows, coef, reach):
    for step in range(reach):
        after = []
        for i in range(1, len(rows) - 1):
            at = step + i
            u = rows[i]
            width = u.shape[1]
            after.append(
                coef[0, at : at + 1, :] * u
                + coef[1, at : at + 1, :] * rows[i + 1]
                + coef[2, at : at + 1, :] * rows[i - 1]
                + coef[3, at : at + 1, :] * pltpu.roll(u, width - 1, 1)
                + coef[4, at : at + 1, :] * pltpu.roll(u, 1, 1)
            )
        rows = after
    return rows


def sort_halo(pair_ref, cross_ref, low_ref, high_ref):
    odd = lax.rem(lax.axis_index("gy"), 2) == 1

    @pl.when(odd)
    def _():
        low_ref[...] = pair_ref[...]
        high_ref[...] = cross_ref[...]

    @pl.when(jnp.logical_not(odd))
    def _():
        low_ref[...] = cross_ref[...]
        high_ref[...] = pair_ref[...]


def triangle_masks():
    shape = (LANES // 2, LANES)
    lane = lax.broadcasted_iota(jnp.int32, shape, 1)
    return lane, lane - lax.broadcasted_iota(jnp.int32, shape, 0)


def pack_symmetric(matrix, packed_ref):
    half = LANES // 2
    lane, away = triangle_masks()
    top, bottom = matrix[:half], matrix[half:]
    corner = jnp.where(away <= 0, top, pltpu.roll(bottom, half, 1))
    packed_ref[0:half, :] = jnp.where(lane < half, corner, top)
    diagonal = jnp.sum(jnp.where(away == half, bottom, 0.0), axis=0, keepdims=True)
    packed_ref[half:, :] = jnp.broadcast_to(diagonal, (packed_ref.shape[0] - half, LANES))


def unpack_symmetric(packed):
    half = LANES // 2
    lane, away = triangle_masks()
    rows, diagonal = packed[:half], packed[half : half + 1]
    turned = jnp.concatenate([rows, rows], axis=0).T
    top = jnp.where((lane < half) & (away > 0), turned[:half], rows)
    corner = jnp.where(
        away > half, pltpu.roll(rows, half, 1), jnp.where(away == half, diagonal, turned[:half])
    )
    return jnp.concatenate([top, jnp.where(lane < half, turned[half:], corner)], axis=0)


def halo_kernel(
    chunks, direction_ref, north_ref, east_ref, ocean_ref, own_ref, stage_ref, mask_ref, sems
):
    cells, size = direction_ref.shape[0], north_ref.shape[0]
    rows = cells // chunks
    spans = [(at * rows, rows) for at in range(chunks)] + [(cells, 2 * size)]
    faces = [
        pltpu.make_async_copy(ref, to, sems.at[0, at])
        for at, (ref, to) in enumerate(
            (
                (ocean_ref, mask_ref),
                (north_ref, stage_ref.at[pl.ds(cells, size)]),
                (east_ref, stage_ref.at[pl.ds(cells + size, size)]),
            )
        )
    ]
    arrive = [
        pltpu.make_async_copy(
            direction_ref.at[pl.ds(start, count)], stage_ref.at[pl.ds(start, count)], sems.at[0, 3 + at]
        )
        for at, (start, count) in enumerate(spans[:-1])
    ]
    leave = [
        pltpu.make_async_copy(
            stage_ref.at[pl.ds(start, count)], own_ref.at[pl.ds(start, count)], sems.at[1, at]
        )
        for at, (start, count) in enumerate(spans)
    ]
    for copy in arrive + faces:
        copy.start()
    for at, copy in enumerate(arrive):
        copy.wait()
        leave[at].start()
    for copy in faces:
        copy.wait()
    mask = mask_ref[...].astype(jnp.float32)
    for kind in range(2):
        here = slice(cells + kind * size, cells + (kind + 1) * size)
        stage_ref[here, :] = stage_ref[here, :] * mask
    leave[-1].start()
    for copy in leave:
        copy.wait()


def join_kernel(_, *refs):
    blocks, (out_ref,) = refs[:-1], refs[-1:]
    size = blocks[0].shape[0]
    for at, block in enumerate(blocks):
        out_ref[at * size : (at + 1) * size] = block[:, : out_ref.shape[1], :]


def hold_kernel(_, *refs):
    blocks, (packed_ref,) = refs[:-1], refs[-1:]
    for at, block in enumerate(blocks):
        pack_symmetric(block[0], packed_ref.at[at])


def first_lateral_kernel(
    kv,
    rows,
    tiles,
    _,
    own_ref,
    north_ref,
    east_ref,
    ocean_ref,
    pair_ref,
    cross_ref,
    packed_ref,
    coef_ref,
    ext_ref,
    low_ref,
    high_ref,
):
    lons = tiles * LANES
    cells = kv * tiles * rows
    sort_halo(pair_ref, cross_ref, low_ref, high_ref)
    at_y, rows_y = lax.axis_index("gy"), lax.axis_size("gy")
    inside = (
        jnp.where(at_y > 0, 1.0, 0.0).astype(jnp.float32),
        jnp.where(at_y < rows_y - 1, 1.0, 0.0).astype(jnp.float32),
    )
    ext_ref[...] = jnp.zeros_like(ext_ref)
    for tile in range(tiles):
        lanes = slice(tile * LANES, (tile + 1) * LANES)
        here = slice(tile * rows, (tile + 1) * rows)
        mask = ocean_ref[here, :].astype(jnp.float32)
        ext_ref[0, rows : 2 * rows, lanes] = north_ref[here, :] * mask
        ext_ref[1, rows : 2 * rows, lanes] = east_ref[here, :] * mask
        ext_ref[2, rows : 2 * rows, lanes] = mask
        for block, ref in ((0, low_ref), (2, high_ref)):
            across = slice(block * rows, (block + 1) * rows)
            for kind in range(2):
                start = cells + (kind * tiles + tile) * rows
                ext_ref[kind, across, lanes] = ref[start : start + rows, :] * inside[block // 2]
            ext_ref[2, across, lanes] = jnp.where(ext_ref[0, across, lanes] > 0.0, 1.0, 0.0)
    total = ext_ref.shape[1]
    ocean = ext_ref[2]
    north_face = ext_ref[0] * pltpu.roll(ocean, total - 1, 0)
    east_face = ext_ref[1] * pltpu.roll(ocean, lons - 1, 1)
    south_face = pltpu.roll(north_face, 1, 0)
    west_face = pltpu.roll(east_face, 1, 1)
    coef_ref[0] = ocean - north_face - south_face - east_face - west_face
    coef_ref[1] = north_face
    coef_ref[2] = south_face
    coef_ref[3] = east_face
    coef_ref[4] = west_face
    low = lane_low((8, LANES))
    for half in range(kv // 8):
        grown = [
            native_rows(ref, row, rows, tiles, half)
            for ref in (low_ref, own_ref, high_ref)
            for row in range(rows)
        ]
        done = lateral_rows(grown, coef_ref, rows)
        for pair in range(rows // 2):
            at = pair * kv + half * 8
            for tile in range(tiles):
                first = done[2 * pair][:, tile * LANES : (tile + 1) * LANES]
                second = done[2 * pair + 1][:, tile * LANES : (tile + 1) * LANES]
                packed_ref[2 * tile, at : at + 8, :] = jnp.where(
                    low, first, pltpu.roll(second, LANES // 2, 1)
                )
                packed_ref[2 * tile + 1, at : at + 8, :] = jnp.where(
                    low, pltpu.roll(first, LANES // 2, 1), second
                )


def second_lateral_kernel(
    kv,
    rows,
    tiles,
    own_ref,
    pair_ref,
    cross_ref,
    coef_ref,
    direction_ref,
    residual_ref,
    image_ref,
    sums_ref,
    low_ref,
    high_ref,
):
    sort_halo(pair_ref, cross_ref, low_ref, high_ref)
    low = lane_low((8, LANES))
    totals = [jnp.zeros((8, tiles * LANES), jnp.float32) for _ in range(4)]
    for half in range(kv // 8):
        grown = []
        for ref in (low_ref, own_ref, high_ref):
            for pair in range(rows // 2):
                firsts, seconds = [], []
                at = pair * kv + half * 8
                for tile in range(tiles):
                    even = ref[2 * tile, at : at + 8, :]
                    odd = ref[2 * tile + 1, at : at + 8, :]
                    firsts.append(jnp.where(low, even, pltpu.roll(odd, LANES // 2, 1)))
                    seconds.append(jnp.where(low, pltpu.roll(even, LANES // 2, 1), odd))
                grown.append(jnp.concatenate(firsts, axis=1))
                grown.append(jnp.concatenate(seconds, axis=1))
        done = lateral_rows(grown, coef_ref, rows)
        for row in range(rows):
            direction = native_rows(direction_ref, row, rows, tiles, half)
            residual = native_rows(residual_ref, row, rows, tiles, half)
            image = direction + done[row]
            for tile in range(tiles):
                image_ref[pl.ds((half * 8 * tiles + tile) * rows + row, 8, stride=tiles * rows), :] = image[
                    :, tile * LANES : (tile + 1) * LANES
                ]
            totals[0] = totals[0] + residual * residual
            totals[1] = totals[1] + direction * image
            totals[2] = totals[2] + residual * image
            totals[3] = totals[3] + image * image
    lane = lax.broadcasted_iota(jnp.int32, (1, LANES), 1)
    line = jnp.zeros((1, LANES), jnp.float32)
    for at, total in enumerate(totals):
        line = jnp.where(lane == at, jnp.sum(total), line)
    for device in range(sums_ref.shape[0]):
        sums_ref[device] = line


def update_kernel(sums_ref, direction_ref, solution_ref, residual_ref, image_ref, sol_ref, res_ref, dir_ref):
    line = jnp.sum(sums_ref[...], axis=0)
    lane = lax.broadcasted_iota(jnp.int32, line.shape, 1)

    def pick(at):
        return jnp.sum(jnp.where(lane == at, line, 0.0), axis=1, keepdims=True)

    norm_now, curvature, cross, square = pick(0), pick(1), pick(2), pick(3)
    alpha = norm_now / curvature
    norm_next = norm_now - 2.0 * alpha * cross + alpha * alpha * square
    beta = norm_next / norm_now
    direction = direction_ref[...]
    residual_next = residual_ref[...] - alpha * image_ref[...]
    sol_ref[...] = solution_ref[...] + alpha * direction
    res_ref[...] = residual_next
    dir_ref[...] = residual_next + beta * direction


def split(value):
    high = value.astype(jnp.bfloat16)
    return high, (value - high.astype(jnp.float32)).astype(jnp.bfloat16)


def dot_parts(left, right, contract):
    dims = (contract, ((), ()))
    total = lax.dot_general(left[0], right[0], dims, preferred_element_type=jnp.float32)
    total = total + lax.dot_general(left[0], right[1], dims, preferred_element_type=jnp.float32)
    return total + lax.dot_general(left[1], right[0], dims, preferred_element_type=jnp.float32)


def prepare_kernel(
    devices,
    capacity,
    lon_cols,
    vert_ref,
    owner_ref,
    row_ref,
    col_ref,
    frac_ref,
    factor_ref,
    high_ref,
    low_ref,
):
    vertical_factors_of(vert_ref, factor_ref)
    count = owner_ref.shape[1]
    slots = devices * capacity
    me = lax.axis_index("gy") * lax.axis_size("gx") + lax.axis_index("gx")
    apart = jnp.bitwise_xor(owner_ref[...], me)
    place = jnp.bitwise_and(apart, 1) * (devices // 2) + jnp.right_shift(apart, 1)
    named = lax.broadcasted_iota(jnp.int32, (devices, count), 0) == place
    before = lax.broadcasted_iota(jnp.int32, (count, count), 0) <= lax.broadcasted_iota(
        jnp.int32, (count, count), 1
    )
    running = jnp.dot(
        jnp.where(named, 1.0, 0.0).astype(jnp.bfloat16),
        jnp.where(before, 1.0, 0.0).astype(jnp.bfloat16),
        preferred_element_type=jnp.float32,
    )
    rank = jnp.sum(jnp.where(named, running, 0.0), axis=0, keepdims=True) - 1.0
    slot = place * capacity + rank.astype(jnp.int32)
    chosen = jnp.where(
        lax.broadcasted_iota(jnp.int32, (slots, count), 0) == slot, 1.0, 0.0
    ).astype(jnp.bfloat16)
    lat_frac = frac_ref[0:1, :]
    lon_frac = frac_ref[1:2, :]
    cell = (row_ref[...] * lon_cols + col_ref[...]).astype(jnp.float32)
    values = jnp.concatenate(
        [
            (1.0 - lat_frac) * (1.0 - lon_frac),
            (1.0 - lat_frac) * lon_frac,
            lat_frac * (1.0 - lon_frac),
            lat_frac * lon_frac,
            cell,
            jnp.zeros((3, count), jnp.float32),
        ],
        axis=0,
    )
    high, rest = split(values)
    low, rest = split(values - high.astype(jnp.float32))
    parts = jnp.concatenate([high.astype(jnp.float32), low.astype(jnp.float32), rest.astype(jnp.float32)], axis=0)
    placed = lax.dot_general(
        parts.astype(jnp.bfloat16), chosen, (((1,), (1,)), ((), ())), preferred_element_type=jnp.float32
    )
    placed = placed[0:8] + placed[8:16] + placed[16:24]
    first = jnp.round(placed[4:5, :]).astype(jnp.int32)
    away = lax.broadcasted_iota(jnp.int32, high_ref.shape, 0) - first
    interp = jnp.where(
        away == 0,
        placed[0:1, :],
        jnp.where(
            away == 1,
            placed[1:2, :],
            jnp.where(away == lon_cols, placed[2:3, :], jnp.where(away == lon_cols + 1, placed[3:4, :], 0.0)),
        ),
    )
    high_ref[...], low_ref[...] = split(interp)


def vertical_factors_of(vert_ref, factor_ref):
    layers = vert_ref.shape[0]
    top = lax.broadcasted_iota(jnp.int32, (8, LANES), 0) < 4
    coef = [jnp.where(top, vert_ref[layer, 0:1, :], vert_ref[layer, 1:2, :]) for layer in range(layers)]
    ratio = None
    for layer in range(layers):
        diagonal = 1.0 + coef[layer]
        if layer > 0:
            diagonal = diagonal + coef[layer - 1] - coef[layer - 1] * ratio
        inverse = 1.0 / diagonal
        ratio = coef[layer] * inverse
        factor_ref[0, layer] = inverse
        factor_ref[1, layer] = coef[layer - 1] * inverse if layer > 0 else jnp.zeros_like(inverse)
        factor_ref[2, layer] = ratio


def solve_columns(read, write, factor_ref, layers):
    forward = []
    for layer in range(layers):
        value = read(layer) * factor_ref[0, layer]
        if layer > 0:
            value = value + factor_ref[1, layer] * forward[-1]
        forward.append(value)
    value = forward[-1]
    write(layers - 1, value)
    for layer in range(layers - 2, -1, -1):
        value = forward[layer] + factor_ref[2, layer] * value
        write(layer, value)


def packed_at(layer, held):
    return pl.ds((layer // held) * 8 * held + layer % held, 8, stride=held)


def weigh(profile, matrices, capacity):
    kv = profile.shape[0]
    owners = LANES // capacity
    mine = lax.broadcasted_iota(jnp.int32, (kv, LANES), 1) // capacity
    tiles = []
    for tile in range(profile.shape[1] // LANES):
        values = profile[:, tile * LANES : (tile + 1) * LANES]
        masked = jnp.concatenate([jnp.where(mine == owner, values, 0.0) for owner in range(owners)], axis=0)
        beside = jnp.concatenate([matrices(tile * owners + owner) for owner in range(owners)], axis=1)
        tiles.append(dot_parts(split(beside), split(masked), ((1,), (0,))))
    return jnp.concatenate(tiles, axis=1)


def smooth_kernel(layers, held, packed_ref, factor_ref, column_ref):
    def read(layer):
        return packed_ref[packed_at(layer, held), :]

    def write(layer, value):
        column_ref[pl.ds(layer, 8, stride=layers), :] = value

    solve_columns(read, write, factor_ref, layers)


def profile_kernel(capacity, column_ref, high_ref, low_ref, *refs):
    near_refs, (weighted_ref, profile_ref) = refs[:-2], refs[-2:]
    kv, half = profile_ref.shape
    size = near_refs[0].shape[0]
    columns = jnp.concatenate([column_ref[0:kv, :], column_ref[kv : 2 * kv, :]], axis=1)
    profile = dot_parts(split(columns), (high_ref[...], low_ref[...]), ((1,), (0,)))
    profile_ref[...] = profile[:, half:]
    weighted_ref[...] = weigh(
        profile[:, :half], lambda at: unpack_symmetric(near_refs[at // size][at % size]), capacity
    )


def spread_kernel(
    layers, held, capacity, near_ref, profile_ref, factor_ref, high_ref, low_ref, far_ref, out_ref, column_ref
):
    kv = near_ref.shape[0]
    weighted = jnp.concatenate([near_ref[...], weigh(profile_ref[...], lambda at: unpack_symmetric(far_ref[at]), capacity)], axis=1)
    spread = dot_parts(split(weighted), (high_ref[...], low_ref[...]), ((1,), (1,)))
    column_ref[0:kv, :] = spread[:, :LANES]
    column_ref[kv : 2 * kv, :] = spread[:, LANES:]

    def read(layer):
        return column_ref[pl.ds(layer, 8, stride=layers), :]

    def write(layer, value):
        out_ref[packed_at(layer, held), :] = value

    solve_columns(read, write, factor_ref, layers)


def vmem(count):
    return [pl.BlockSpec(memory_space=pltpu.VMEM)] * count


def call(kernel, out_shape, inputs, scratch=(), after=0, hbm=False, flops=1_000_000, mib=8):
    specs = [pl.BlockSpec(memory_space=pl.ANY)] * after + vmem(len(inputs) - after)
    outs = vmem(len(out_shape) if isinstance(out_shape, tuple) else 1)
    if hbm:
        specs, outs = ([pl.BlockSpec(memory_space=pltpu.HBM)] * len(x) for x in (specs, outs))
    moved = sum(math.prod(x.shape) * 4 for x in inputs)
    return pl.pallas_call(
        kernel,
        out_shape=out_shape,
        in_specs=specs,
        out_specs=tuple(outs) if isinstance(out_shape, tuple) else outs[0],
        scratch_shapes=list(scratch),
        compiler_params=pltpu.CompilerParams(vmem_limit_bytes=mib * 1024 * 1024),
        cost_estimate=pl.CostEstimate(flops=flops, bytes_accessed=moved, transcendentals=0),
    )(*inputs)


def f32(*shape):
    return jax.ShapeDtypeStruct(shape, jnp.float32)


def from_neighbours(block):
    count = lax.axis_size("gy")
    pair = lax.ppermute(block, "gy", [(i, i ^ 1) for i in range(count)])
    cross = lax.ppermute(block, "gy", [(i, (i + (1 if i % 2 else -1)) % count) for i in range(count)])
    return pair, cross


def apart_by(block, axis, stride):
    return lax.ppermute(block, axis, [(i, i ^ stride) for i in range(lax.axis_size(axis))])


def per_device_gathered(
    direction,
    solution,
    residual,
    north_coef,
    east_coef,
    ocean,
    vert_coef,
    obs_owner,
    obs_row,
    obs_col,
    obs_frac,
    error_inverse,
):
    var_count, held, rows, lons = direction.shape
    kv = var_count * held
    tiles = lons // LANES
    layers, _, lon_cols = vert_coef.shape
    rows_y, cols_x = lax.axis_size("gy"), lax.axis_size("gx")
    device_count = rows_y * cols_x
    obs_count = obs_row.shape[-1]
    capacity = 2 * obs_count // device_count
    wide = error_inverse.shape[-1]
    cells = rows * lon_cols

    direction_n = to_native(direction)
    residual_n = to_native(residual)
    solution_n = to_native(solution)
    faces = [to_native(x[None, None]) for x in (north_coef, east_coef, ocean)]
    own = call(
        functools.partial(halo_kernel, 4),
        f32(direction_n.shape[0] + 2 * faces[0].shape[0], LANES),
        (direction_n, *faces),
        scratch=(
            pltpu.VMEM((direction_n.shape[0] + 2 * faces[0].shape[0], LANES), jnp.float32),
            pltpu.VMEM(faces[0].shape, jnp.int32),
            pltpu.SemaphoreType.DMA((2, 7)),
        ),
        hbm=True,
        mib=56,
    )
    pair, cross = from_neighbours(own)

    matrix = error_inverse.reshape(1, wide, wide)
    blocks = [matrix] + [apart_by(matrix, "gx", stride) for stride in range(2, cols_x, 2)]
    halves = jax.ShapeDtypeStruct((cells, device_count * capacity), jnp.bfloat16)
    factors, *interp = call(
        functools.partial(prepare_kernel, device_count, capacity, lon_cols),
        (f32(3, layers, 8, LANES), halves, halves),
        (
            vert_coef.reshape(layers, cells // LANES, LANES),
            obs_owner.reshape(1, obs_count),
            obs_row.reshape(1, obs_count),
            obs_col.reshape(1, obs_count),
            obs_frac.reshape(2, obs_count),
        ),
        flops=20_000_000,
        mib=16,
    )
    extended = 3 * rows + (-3 * rows) % 8
    packed, coef = call(
        functools.partial(first_lateral_kernel, kv, rows, tiles),
        (f32(cols_x, 2 * kv, LANES), f32(5, extended, lons)),
        (interp[0], direction_n, *faces, pair, cross),
        after=1,
        scratch=(
            pltpu.VMEM((3, extended, lons), jnp.float32),
            pltpu.VMEM(own.shape, jnp.float32),
            pltpu.VMEM(own.shape, jnp.float32),
        ),
        flops=4_000_000,
    )
    held_blocks = call(
        hold_kernel, f32(len(blocks), wide - 8, wide), (packed, *blocks), after=1
    )
    fetched = [held_blocks] + [apart_by(held_blocks, "gy", stride) for stride in range(1, rows_y)]
    columns = lax.all_to_all(packed, "gx", split_axis=0, concat_axis=0, tiled=True)
    smoothed = call(
        functools.partial(smooth_kernel, layers, held),
        f32(2 * wide, LANES),
        (columns.reshape(cols_x * 2 * kv, LANES), factors),
        flops=1000,
    )
    far = apart_by(
        call(
            join_kernel, f32(device_count // 2, wide // 2 + 8, wide), (columns, *fetched), after=1
        ),
        "gx",
        1,
    )
    half = device_count // 2 * capacity
    weighted, profile = call(
        functools.partial(profile_kernel, capacity),
        (f32(wide, half), f32(wide, half)),
        (smoothed, *interp, *fetched),
        flops=400_000_000,
        mib=16,
    )
    spread = call(
        functools.partial(spread_kernel, layers, held, capacity),
        f32(cols_x * 2 * kv, LANES),
        (weighted, profile, factors, *interp, far),
        scratch=(pltpu.VMEM((2 * wide, LANES), jnp.float32),),
        flops=400_000_000,
        mib=16,
    )
    tile = lax.all_to_all(
        spread.reshape(cols_x, 2 * kv, LANES), "gx", split_axis=0, concat_axis=0, tiled=True
    )
    pair, cross = from_neighbours(tile)
    image, sums = call(
        functools.partial(second_lateral_kernel, kv, rows, tiles),
        (f32(*direction_n.shape), f32(device_count, 1, LANES)),
        (tile, pair, cross, coef, direction_n, residual_n),
        scratch=(pltpu.VMEM(tile.shape, jnp.float32), pltpu.VMEM(tile.shape, jnp.float32)),
        flops=4_000_000,
    )
    sums = lax.all_to_all(sums, ("gy", "gx"), split_axis=0, concat_axis=0, tiled=True)
    after = call(
        update_kernel,
        (f32(*direction_n.shape),) * 3,
        (sums, direction_n, solution_n, residual_n, image),
    )
    return tuple(from_native(x, direction.shape) for x in after)


def gathers(mesh, shapes):
    rows_y, cols_x = mesh.shape["gy"], mesh.shape["gx"]
    devices = rows_y * cols_x
    if any(size < 2 or size & (size - 1) for size in (rows_y, cols_x)):
        return False
    direction, vert_coef, obs_row, error_inverse = shapes
    var_count, layers, lat_rows, lons = direction
    rows, held = lat_rows // rows_y, layers // cols_x
    obs_count, wide = obs_row[-1], error_inverse[-1]
    capacity = 2 * obs_count // devices
    return (
        rows == NSTEP == 4
        and var_count == 4
        and (var_count * held) % 8 == 0
        and lons // cols_x * 2 == LANES
        and wide == LANES
        and capacity > 0
        and LANES % capacity == 0
        and devices // 2 % (LANES // capacity) == 0
        and devices * wide * wide * 4 <= 8 * 1024 * 1024
    )


def padded(cells, sides, width):
    for axis, dim in sides:
        count = lax.axis_size(axis)
        ends = count - 1
        head = lax.slice_in_dim(cells, 0, width, axis=dim)
        tail = lax.slice_in_dim(cells, cells.shape[dim] - width, cells.shape[dim], axis=dim)
        cells = jnp.concatenate(
            [
                lax.ppermute(tail, axis, [(i, (i + 1) % count) for i in range(ends)]),
                cells,
                lax.ppermute(head, axis, [((i + 1) % count, i) for i in range(ends)]),
            ],
            axis=dim,
        )
    return cells


def lateral_faces(north_ext, east_ext, ocean_ext):
    ocean_next = jnp.concatenate([ocean_ext[1:], jnp.zeros_like(ocean_ext[:1])], axis=0)
    north_face = north_ext * ocean_ext * ocean_next
    east_face = east_ext * ocean_ext * jnp.roll(ocean_ext, -1, axis=1)
    return (north_face, east_face, ocean_ext)


def diffuse_once(values_grid, north_face, east_face, ocean_ext):
    north_flux = north_face[:-1] * (values_grid[:, :, 1:, :] - values_grid[:, :, :-1, :])
    east_flux = east_face * (jnp.roll(values_grid, -1, axis=3) - values_grid)
    lateral = east_flux - jnp.roll(east_flux, 1, axis=3)
    return (
        ocean_ext[1:-1] * values_grid[:, :, 1:-1, :]
        + north_flux[:, :, 1:, :]
        - north_flux[:, :, :-1, :]
        + lateral[:, :, 1:-1, :]
    )


def lateral_pass(values_tile, faces):
    north_face, east_face, ocean_ext = faces
    grown = padded(values_tile, (("gy", 2),), NSTEP)
    total_rows = grown.shape[2]
    for step_index in range(NSTEP):
        upper = total_rows - step_index
        grown = diffuse_once(
            grown,
            north_face[step_index:upper],
            east_face[step_index:upper],
            ocean_ext[step_index:upper],
        )
    return grown


def vertical_factors(vert_coef):
    inverse_rows = []
    upper_ratio = []
    for layer_index in range(vert_coef.shape[0]):
        diagonal = 1.0 + vert_coef[layer_index]
        if layer_index > 0:
            diagonal = (
                diagonal + vert_coef[layer_index - 1] + vert_coef[layer_index - 1] * upper_ratio[-1]
            )
        inverse = 1.0 / diagonal
        inverse_rows.append(inverse)
        upper_ratio.append(-vert_coef[layer_index] * inverse)
    return (inverse_rows, upper_ratio)


def vertical_solve(values_col, vert_coef, factors):
    inverse_rows, upper_ratio = factors
    layers = values_col.shape[1]
    forward = []
    for layer_index in range(layers):
        source = values_col[:, layer_index]
        if layer_index > 0:
            source = source + vert_coef[layer_index - 1] * forward[-1]
        forward.append(source * inverse_rows[layer_index])
    result = [forward[-1]]
    for layer_index in range(layers - 2, -1, -1):
        result.append(forward[layer_index] - upper_ratio[layer_index] * result[-1])
    return jnp.stack(result[::-1], axis=1)


def observe_weigh_spread(columns, obs_owner, obs_row, obs_col, obs_frac, error_inverse):
    var_count, lev_count, lat_rows, lon_cols = columns.shape
    kv_width = var_count * lev_count
    rows_y = lax.axis_size("gy")
    cols_x = lax.axis_size("gx")
    device_count = rows_y * cols_x
    obs_count = obs_row.shape[-1]
    capacity = 2 * obs_count // device_count
    flat = columns.reshape(kv_width, lat_rows * lon_cols)
    cell = obs_row.reshape(-1) * lon_cols + obs_col.reshape(-1)
    corners = (cell, cell + 1, cell + lon_cols, cell + lon_cols + 1)
    lat_frac = obs_frac[0, 0, 0]
    lon_frac = obs_frac[0, 0, 1]
    weights = (
        (1.0 - lat_frac) * (1.0 - lon_frac),
        (1.0 - lat_frac) * lon_frac,
        lat_frac * (1.0 - lon_frac),
        lat_frac * lon_frac,
    )
    profile = weights[0] * jnp.take(flat, corners[0], axis=1)
    for corner_index in range(1, 4):
        profile = profile + weights[corner_index] * jnp.take(flat, corners[corner_index], axis=1)
    owners = obs_owner.reshape(-1)
    onehot = (owners[:, None] == jnp.arange(device_count, dtype=jnp.int32)[None, :]).astype(
        jnp.int32
    )
    running = jnp.cumsum(onehot, axis=0)
    rank_in = jnp.sum(running * onehot, axis=1) - 1
    slot = owners * capacity + rank_in
    outgoing = jnp.zeros((device_count * capacity, kv_width), jnp.float32).at[slot].set(profile.T)
    outgoing = outgoing.reshape(rows_y, cols_x, capacity, kv_width)
    matrix = error_inverse.reshape(kv_width, kv_width)
    arrived = lax.all_to_all(
        lax.all_to_all(outgoing, "gy", split_axis=0, concat_axis=0, tiled=True),
        "gx",
        split_axis=1,
        concat_axis=1,
        tiled=True,
    )
    weighted = jnp.dot(
        arrived.reshape(-1, kv_width),
        matrix,
        precision=lax.Precision.HIGHEST,
        preferred_element_type=jnp.float32,
    ).reshape(rows_y, cols_x, capacity, kv_width)
    returned = lax.all_to_all(
        lax.all_to_all(weighted, "gy", split_axis=0, concat_axis=0, tiled=True),
        "gx",
        split_axis=1,
        concat_axis=1,
        tiled=True,
    )
    back = returned.reshape(device_count * capacity, kv_width)[slot].T
    spread = jnp.zeros((kv_width, lat_rows * lon_cols), jnp.float32)
    for corner_index in range(4):
        spread = spread.at[:, corners[corner_index]].add(weights[corner_index] * back)
    return spread.reshape(var_count, lev_count, lat_rows, lon_cols)


def per_device(
    direction,
    solution,
    residual,
    north_coef,
    east_coef,
    ocean,
    vert_coef,
    obs_owner,
    obs_row,
    obs_col,
    obs_frac,
    error_inverse,
):
    stacked = jnp.stack([north_coef, east_coef, ocean.astype(jnp.float32)])
    reach = NSTEP
    grown_coef = padded(stacked, (("gy", 1),), reach)
    faces = lateral_faces(grown_coef[0], grown_coef[1], grown_coef[2])
    factors = vertical_factors(vert_coef)
    smoothed = lateral_pass(direction, faces)
    columns = lax.all_to_all(smoothed, "gx", split_axis=3, concat_axis=1, tiled=True)
    columns = vertical_solve(columns, vert_coef, factors)
    spread = observe_weigh_spread(columns, obs_owner, obs_row, obs_col, obs_frac, error_inverse)
    spread = vertical_solve(spread, vert_coef, factors)
    tiles = lax.all_to_all(spread, "gx", split_axis=1, concat_axis=3, tiled=True)
    image = direction + lateral_pass(tiles, faces)
    norm_now, curvature = lax.psum(
        (jnp.sum(residual * residual), jnp.sum(direction * image)), ("gy", "gx")
    )
    alpha = norm_now / curvature
    residual_next = residual - alpha * image
    norm_next = lax.psum(jnp.sum(residual_next * residual_next), ("gy", "gx"))
    solution_next = solution + alpha * direction
    direction_next = residual_next + norm_next / norm_now * direction
    return (solution_next, residual_next, direction_next)


def solution(mesh):
    in_specs = (
        P(None, "gx", "gy", None),
        P(None, "gx", "gy", None),
        P(None, "gx", "gy", None),
        P("gy", None),
        P("gy", None),
        P("gy", None),
        P(None, "gy", "gx"),
        P("gy", "gx", None, None),
        P("gy", "gx", None),
        P("gy", "gx", None),
        P("gy", "gx", None, None),
        P("gy", "gx", None, None),
    )
    out_specs = (P(None, "gx", "gy", None),) * 3

    def step(*arrays):
        shapes = [arrays[at].shape for at in (0, 6, 8, 11)]
        local = per_device_gathered if gathers(mesh, shapes) else per_device
        return jax.shard_map(
            local, mesh=mesh, in_specs=in_specs, out_specs=out_specs, check_vma=False
        )(*arrays)

    return step
```

```python
import functools
import math

import jax
import jax.numpy as jnp
from jax import lax
from jax.experimental import pallas as pl
from jax.experimental.pallas import tpu as pltpu
from jax.sharding import PartitionSpec as P

NSTEP = 4
LANES = 128


def to_native(tile):
    kv, rows, lons = tile.shape[0] * tile.shape[1], tile.shape[2], tile.shape[3]
    return tile.reshape(kv, rows, lons // LANES, LANES).swapaxes(1, 2).reshape(-1, LANES)


def from_native(flat, shape):
    kv, rows, lons = shape[0] * shape[1], shape[2], shape[3]
    return flat.reshape(kv, lons // LANES, rows, LANES).swapaxes(1, 2).reshape(shape)


def native_rows(ref, row, rows, tiles, half):
    parts = [
        ref[pl.ds((half * 8 * tiles + tile) * rows + row, 8, stride=tiles * rows), :]
        for tile in range(tiles)
    ]
    return jnp.concatenate(parts, axis=1)


def lane_low(shape):
    return lax.broadcasted_iota(jnp.int32, shape, 1) < LANES // 2


def lateral_rows(rows, coef, reach):
    for step in range(reach):
        after = []
        for i in range(1, len(rows) - 1):
            at = step + i
            u = rows[i]
            width = u.shape[1]
            after.append(
                coef[0, at : at + 1, :] * u
                + coef[1, at : at + 1, :] * rows[i + 1]
                + coef[2, at : at + 1, :] * rows[i - 1]
                + coef[3, at : at + 1, :] * pltpu.roll(u, width - 1, 1)
                + coef[4, at : at + 1, :] * pltpu.roll(u, 1, 1)
            )
        rows = after
    return rows


def by_parity(pair_ref, cross_ref, body):
    odd = lax.rem(lax.axis_index("gy"), 2) == 1
    pl.when(odd)(lambda: body(pair_ref, cross_ref))
    pl.when(jnp.logical_not(odd))(lambda: body(cross_ref, pair_ref))


def triangle_masks():
    shape = (LANES // 2, LANES)
    lane = lax.broadcasted_iota(jnp.int32, shape, 1)
    return lane, lane - lax.broadcasted_iota(jnp.int32, shape, 0)


def pack_symmetric(matrix, packed_ref):
    half = LANES // 2
    lane, away = triangle_masks()
    top, bottom = matrix[:half], matrix[half:]
    corner = jnp.where(away <= 0, top, pltpu.roll(bottom, half, 1))
    packed_ref[0:half, :] = jnp.where(lane < half, corner, top)
    diagonal = jnp.sum(jnp.where(away == half, bottom, 0.0), axis=0, keepdims=True)
    packed_ref[half:, :] = jnp.broadcast_to(diagonal, (packed_ref.shape[0] - half, LANES))


def unpack_symmetric(packed):
    half = LANES // 2
    lane, away = triangle_masks()
    rows, diagonal = packed[:half], packed[half : half + 1]
    turned = jnp.concatenate([rows, rows], axis=0).T
    top = jnp.where((lane < half) & (away > 0), turned[:half], rows)
    corner = jnp.where(
        away > half, pltpu.roll(rows, half, 1), jnp.where(away == half, diagonal, turned[:half])
    )
    return jnp.concatenate([top, jnp.where(lane < half, turned[half:], corner)], axis=0)


def halo_kernel(
    chunks, direction_ref, north_ref, east_ref, ocean_ref, own_ref, stage_ref, mask_ref, sems
):
    cells, size = direction_ref.shape[0], north_ref.shape[0]
    rows = cells // chunks
    spans = [(at * rows, rows) for at in range(chunks)] + [(cells, 2 * size)]
    faces = [
        pltpu.make_async_copy(ref, to, sems.at[0, at])
        for at, (ref, to) in enumerate(
            (
                (ocean_ref, mask_ref),
                (north_ref, stage_ref.at[pl.ds(cells, size)]),
                (east_ref, stage_ref.at[pl.ds(cells + size, size)]),
            )
        )
    ]
    arrive = [
        pltpu.make_async_copy(
            direction_ref.at[pl.ds(start, count)], stage_ref.at[pl.ds(start, count)], sems.at[0, 3 + at]
        )
        for at, (start, count) in enumerate(spans[:-1])
    ]
    leave = [
        pltpu.make_async_copy(
            stage_ref.at[pl.ds(start, count)], own_ref.at[pl.ds(start, count)], sems.at[1, at]
        )
        for at, (start, count) in enumerate(spans)
    ]
    for copy in arrive + faces:
        copy.start()
    for at, copy in enumerate(arrive):
        copy.wait()
        leave[at].start()
    for copy in faces:
        copy.wait()
    mask = mask_ref[...].astype(jnp.float32)
    for kind in range(2):
        here = slice(cells + kind * size, cells + (kind + 1) * size)
        stage_ref[here, :] = stage_ref[here, :] * mask
    leave[-1].start()
    for copy in leave:
        copy.wait()


def join_kernel(_, *refs):
    blocks, (out_ref,) = refs[:-1], refs[-1:]
    size = blocks[0].shape[0]
    for at, block in enumerate(blocks):
        out_ref[at * size : (at + 1) * size] = block[:, : out_ref.shape[1], :]


def hold_kernel(_, *refs):
    blocks, (packed_ref,) = refs[:-1], refs[-1:]
    for at, block in enumerate(blocks):
        pack_symmetric(block[0], packed_ref.at[at])


def first_lateral_kernel(
    kv,
    rows,
    tiles,
    _,
    own_ref,
    north_ref,
    east_ref,
    ocean_ref,
    pair_ref,
    cross_ref,
    packed_ref,
    coef_ref,
    ext_ref,
):
    lons = tiles * LANES
    cells = kv * tiles * rows

    def body(low_ref, high_ref):
        at_y, rows_y = lax.axis_index("gy"), lax.axis_size("gy")
        inside = (
            jnp.where(at_y > 0, 1.0, 0.0).astype(jnp.float32),
            jnp.where(at_y < rows_y - 1, 1.0, 0.0).astype(jnp.float32),
        )
        ext_ref[...] = jnp.zeros_like(ext_ref)
        for tile in range(tiles):
            lanes = slice(tile * LANES, (tile + 1) * LANES)
            here = slice(tile * rows, (tile + 1) * rows)
            mask = ocean_ref[here, :].astype(jnp.float32)
            ext_ref[0, rows : 2 * rows, lanes] = north_ref[here, :] * mask
            ext_ref[1, rows : 2 * rows, lanes] = east_ref[here, :] * mask
            ext_ref[2, rows : 2 * rows, lanes] = mask
            for block, ref in ((0, low_ref), (2, high_ref)):
                across = slice(block * rows, (block + 1) * rows)
                for kind in range(2):
                    start = cells + (kind * tiles + tile) * rows
                    ext_ref[kind, across, lanes] = ref[start : start + rows, :] * inside[block // 2]
                ext_ref[2, across, lanes] = jnp.where(ext_ref[0, across, lanes] > 0.0, 1.0, 0.0)
        total = ext_ref.shape[1]
        ocean = ext_ref[2]
        north_face = ext_ref[0] * pltpu.roll(ocean, total - 1, 0)
        east_face = ext_ref[1] * pltpu.roll(ocean, lons - 1, 1)
        south_face = pltpu.roll(north_face, 1, 0)
        west_face = pltpu.roll(east_face, 1, 1)
        coef_ref[0] = ocean - north_face - south_face - east_face - west_face
        coef_ref[1] = north_face
        coef_ref[2] = south_face
        coef_ref[3] = east_face
        coef_ref[4] = west_face
        low = lane_low((8, LANES))
        for half in range(kv // 8):
            grown = [
                native_rows(ref, row, rows, tiles, half)
                for ref in (low_ref, own_ref, high_ref)
                for row in range(rows)
            ]
            done = lateral_rows(grown, coef_ref, rows)
            for pair in range(rows // 2):
                at = pair * kv + half * 8
                for tile in range(tiles):
                    first = done[2 * pair][:, tile * LANES : (tile + 1) * LANES]
                    second = done[2 * pair + 1][:, tile * LANES : (tile + 1) * LANES]
                    packed_ref[2 * tile, at : at + 8, :] = jnp.where(
                        low, first, pltpu.roll(second, LANES // 2, 1)
                    )
                    packed_ref[2 * tile + 1, at : at + 8, :] = jnp.where(
                        low, pltpu.roll(first, LANES // 2, 1), second
                    )

    by_parity(pair_ref, cross_ref, body)


def second_lateral_kernel(
    kv,
    rows,
    tiles,
    own_ref,
    pair_ref,
    cross_ref,
    coef_ref,
    direction_ref,
    residual_ref,
    image_ref,
    sums_ref,
):

    def body(low_ref, high_ref):
        low = lane_low((8, LANES))
        totals = [jnp.zeros((8, tiles * LANES), jnp.float32) for _ in range(4)]
        for half in range(kv // 8):
            grown = []
            for ref in (low_ref, own_ref, high_ref):
                for pair in range(rows // 2):
                    firsts, seconds = [], []
                    at = pair * kv + half * 8
                    for tile in range(tiles):
                        even = ref[2 * tile, at : at + 8, :]
                        odd = ref[2 * tile + 1, at : at + 8, :]
                        firsts.append(jnp.where(low, even, pltpu.roll(odd, LANES // 2, 1)))
                        seconds.append(jnp.where(low, pltpu.roll(even, LANES // 2, 1), odd))
                    grown.append(jnp.concatenate(firsts, axis=1))
                    grown.append(jnp.concatenate(seconds, axis=1))
            done = lateral_rows(grown, coef_ref, rows)
            for row in range(rows):
                direction = native_rows(direction_ref, row, rows, tiles, half)
                residual = native_rows(residual_ref, row, rows, tiles, half)
                image = direction + done[row]
                for tile in range(tiles):
                    image_ref[pl.ds((half * 8 * tiles + tile) * rows + row, 8, stride=tiles * rows), :] = image[
                        :, tile * LANES : (tile + 1) * LANES
                    ]
                totals[0] = totals[0] + residual * residual
                totals[1] = totals[1] + direction * image
                totals[2] = totals[2] + residual * image
                totals[3] = totals[3] + image * image
        lane = lax.broadcasted_iota(jnp.int32, (1, LANES), 1)
        line = jnp.zeros((1, LANES), jnp.float32)
        for at, total in enumerate(totals):
            line = jnp.where(lane == at, jnp.sum(total), line)
        for device in range(sums_ref.shape[0]):
            sums_ref[device] = line

    by_parity(pair_ref, cross_ref, body)


def update_kernel(sums_ref, direction_ref, solution_ref, residual_ref, image_ref, sol_ref, res_ref, dir_ref):
    line = jnp.sum(sums_ref[...], axis=0)
    lane = lax.broadcasted_iota(jnp.int32, line.shape, 1)

    def pick(at):
        return jnp.sum(jnp.where(lane == at, line, 0.0), axis=1, keepdims=True)

    norm_now, curvature, cross, square = pick(0), pick(1), pick(2), pick(3)
    alpha = norm_now / curvature
    norm_next = norm_now - 2.0 * alpha * cross + alpha * alpha * square
    beta = norm_next / norm_now
    direction = direction_ref[...]
    residual_next = residual_ref[...] - alpha * image_ref[...]
    sol_ref[...] = solution_ref[...] + alpha * direction
    res_ref[...] = residual_next
    dir_ref[...] = residual_next + beta * direction


def split(value):
    high = value.astype(jnp.bfloat16)
    return high, (value - high.astype(jnp.float32)).astype(jnp.bfloat16)


def dot_parts(left, right, contract):
    dims = (contract, ((), ()))
    total = lax.dot_general(left[0], right[0], dims, preferred_element_type=jnp.float32)
    total = total + lax.dot_general(left[0], right[1], dims, preferred_element_type=jnp.float32)
    return total + lax.dot_general(left[1], right[0], dims, preferred_element_type=jnp.float32)


def prepare_kernel(
    devices,
    capacity,
    lon_cols,
    vert_ref,
    owner_ref,
    row_ref,
    col_ref,
    frac_ref,
    factor_ref,
    high_ref,
    low_ref,
):
    vertical_factors_of(vert_ref, factor_ref)
    count = owner_ref.shape[1]
    slots = devices * capacity
    me = lax.axis_index("gy") * lax.axis_size("gx") + lax.axis_index("gx")
    apart = jnp.bitwise_xor(owner_ref[...], me)
    place = jnp.bitwise_and(apart, 1) * (devices // 2) + jnp.right_shift(apart, 1)
    named = lax.broadcasted_iota(jnp.int32, (devices, count), 0) == place
    before = lax.broadcasted_iota(jnp.int32, (count, count), 0) <= lax.broadcasted_iota(
        jnp.int32, (count, count), 1
    )
    running = jnp.dot(
        jnp.where(named, 1.0, 0.0).astype(jnp.bfloat16),
        jnp.where(before, 1.0, 0.0).astype(jnp.bfloat16),
        preferred_element_type=jnp.float32,
    )
    rank = jnp.sum(jnp.where(named, running, 0.0), axis=0, keepdims=True) - 1.0
    slot = place * capacity + rank.astype(jnp.int32)
    chosen = jnp.where(
        lax.broadcasted_iota(jnp.int32, (slots, count), 0) == slot, 1.0, 0.0
    ).astype(jnp.bfloat16)
    lat_frac = frac_ref[0:1, :]
    lon_frac = frac_ref[1:2, :]
    cell = (row_ref[...] * lon_cols + col_ref[...]).astype(jnp.float32)
    values = jnp.concatenate(
        [
            (1.0 - lat_frac) * (1.0 - lon_frac),
            (1.0 - lat_frac) * lon_frac,
            lat_frac * (1.0 - lon_frac),
            lat_frac * lon_frac,
            cell,
            jnp.zeros((3, count), jnp.float32),
        ],
        axis=0,
    )
    high, rest = split(values)
    low, rest = split(values - high.astype(jnp.float32))
    parts = jnp.concatenate([high.astype(jnp.float32), low.astype(jnp.float32), rest.astype(jnp.float32)], axis=0)
    placed = lax.dot_general(
        parts.astype(jnp.bfloat16), chosen, (((1,), (1,)), ((), ())), preferred_element_type=jnp.float32
    )
    placed = placed[0:8] + placed[8:16] + placed[16:24]
    first = jnp.round(placed[4:5, :]).astype(jnp.int32)
    away = lax.broadcasted_iota(jnp.int32, high_ref.shape, 0) - first
    interp = jnp.where(
        away == 0,
        placed[0:1, :],
        jnp.where(
            away == 1,
            placed[1:2, :],
            jnp.where(away == lon_cols, placed[2:3, :], jnp.where(away == lon_cols + 1, placed[3:4, :], 0.0)),
        ),
    )
    high_ref[...], low_ref[...] = split(interp)


def vertical_factors_of(vert_ref, factor_ref):
    layers = vert_ref.shape[0]
    top = lax.broadcasted_iota(jnp.int32, (8, LANES), 0) < 4
    coef = [jnp.where(top, vert_ref[layer, 0:1, :], vert_ref[layer, 1:2, :]) for layer in range(layers)]
    ratio = None
    for layer in range(layers):
        diagonal = 1.0 + coef[layer]
        if layer > 0:
            diagonal = diagonal + coef[layer - 1] - coef[layer - 1] * ratio
        inverse = 1.0 / diagonal
        ratio = coef[layer] * inverse
        factor_ref[0, layer] = inverse
        factor_ref[1, layer] = coef[layer - 1] * inverse if layer > 0 else jnp.zeros_like(inverse)
        factor_ref[2, layer] = ratio


def solve_columns(read, write, factor_ref, layers):
    forward = []
    for layer in range(layers):
        value = read(layer) * factor_ref[0, layer]
        if layer > 0:
            value = value + factor_ref[1, layer] * forward[-1]
        forward.append(value)
    value = forward[-1]
    write(layers - 1, value)
    for layer in range(layers - 2, -1, -1):
        value = forward[layer] + factor_ref[2, layer] * value
        write(layer, value)


def packed_at(layer, held):
    return pl.ds((layer // held) * 8 * held + layer % held, 8, stride=held)


def weigh(profile, matrices, capacity):
    kv = profile.shape[0]
    owners = LANES // capacity
    mine = lax.broadcasted_iota(jnp.int32, (kv, LANES), 1) // capacity
    tiles = []
    for tile in range(profile.shape[1] // LANES):
        values = profile[:, tile * LANES : (tile + 1) * LANES]
        masked = jnp.concatenate([jnp.where(mine == owner, values, 0.0) for owner in range(owners)], axis=0)
        beside = jnp.concatenate([matrices(tile * owners + owner) for owner in range(owners)], axis=1)
        tiles.append(dot_parts(split(beside), split(masked), ((1,), (0,))))
    return jnp.concatenate(tiles, axis=1)


def smooth_kernel(layers, held, packed_ref, factor_ref, column_ref):
    def read(layer):
        return packed_ref[packed_at(layer, held), :]

    def write(layer, value):
        column_ref[pl.ds(layer, 8, stride=layers), :] = value

    solve_columns(read, write, factor_ref, layers)


def profile_kernel(capacity, column_ref, high_ref, low_ref, *refs):
    near_refs, (weighted_ref, profile_ref) = refs[:-2], refs[-2:]
    kv, half = profile_ref.shape
    size = near_refs[0].shape[0]
    columns = jnp.concatenate([column_ref[0:kv, :], column_ref[kv : 2 * kv, :]], axis=1)
    profile = dot_parts(split(columns), (high_ref[...], low_ref[...]), ((1,), (0,)))
    profile_ref[...] = profile[:, half:]
    weighted_ref[...] = weigh(
        profile[:, :half], lambda at: unpack_symmetric(near_refs[at // size][at % size]), capacity
    )


def spread_kernel(
    layers, held, capacity, near_ref, profile_ref, factor_ref, high_ref, low_ref, far_ref, out_ref, column_ref
):
    kv = near_ref.shape[0]
    weighted = jnp.concatenate([near_ref[...], weigh(profile_ref[...], lambda at: unpack_symmetric(far_ref[at]), capacity)], axis=1)
    spread = dot_parts(split(weighted), (high_ref[...], low_ref[...]), ((1,), (1,)))
    column_ref[0:kv, :] = spread[:, :LANES]
    column_ref[kv : 2 * kv, :] = spread[:, LANES:]

    def read(layer):
        return column_ref[pl.ds(layer, 8, stride=layers), :]

    def write(layer, value):
        out_ref[packed_at(layer, held), :] = value

    solve_columns(read, write, factor_ref, layers)


def vmem(count):
    return [pl.BlockSpec(memory_space=pltpu.VMEM)] * count


def call(kernel, out_shape, inputs, scratch=(), after=0, hbm=False, flops=1_000_000, mib=8):
    specs = [pl.BlockSpec(memory_space=pl.ANY)] * after + vmem(len(inputs) - after)
    outs = vmem(len(out_shape) if isinstance(out_shape, tuple) else 1)
    if hbm:
        specs, outs = ([pl.BlockSpec(memory_space=pltpu.HBM)] * len(x) for x in (specs, outs))
    moved = sum(math.prod(x.shape) * 4 for x in inputs)
    return pl.pallas_call(
        kernel,
        out_shape=out_shape,
        in_specs=specs,
        out_specs=tuple(outs) if isinstance(out_shape, tuple) else outs[0],
        scratch_shapes=list(scratch),
        compiler_params=pltpu.CompilerParams(vmem_limit_bytes=mib * 1024 * 1024),
        cost_estimate=pl.CostEstimate(flops=flops, bytes_accessed=moved, transcendentals=0),
    )(*inputs)


def f32(*shape):
    return jax.ShapeDtypeStruct(shape, jnp.float32)


def from_neighbours(block):
    count = lax.axis_size("gy")
    pair = lax.ppermute(block, "gy", [(i, i ^ 1) for i in range(count)])
    cross = lax.ppermute(block, "gy", [(i, (i + (1 if i % 2 else -1)) % count) for i in range(count)])
    return pair, cross


def apart_by(block, axis, stride):
    return lax.ppermute(block, axis, [(i, i ^ stride) for i in range(lax.axis_size(axis))])


def per_device_gathered(
    direction,
    solution,
    residual,
    north_coef,
    east_coef,
    ocean,
    vert_coef,
    obs_owner,
    obs_row,
    obs_col,
    obs_frac,
    error_inverse,
):
    var_count, held, rows, lons = direction.shape
    kv = var_count * held
    tiles = lons // LANES
    layers, _, lon_cols = vert_coef.shape
    rows_y, cols_x = lax.axis_size("gy"), lax.axis_size("gx")
    device_count = rows_y * cols_x
    obs_count = obs_row.shape[-1]
    capacity = 2 * obs_count // device_count
    wide = error_inverse.shape[-1]
    cells = rows * lon_cols

    direction_n = to_native(direction)
    residual_n = to_native(residual)
    solution_n = to_native(solution)
    faces = [to_native(x[None, None]) for x in (north_coef, east_coef, ocean)]
    own = call(
        functools.partial(halo_kernel, 4),
        f32(direction_n.shape[0] + 2 * faces[0].shape[0], LANES),
        (direction_n, *faces),
        scratch=(
            pltpu.VMEM((direction_n.shape[0] + 2 * faces[0].shape[0], LANES), jnp.float32),
            pltpu.VMEM(faces[0].shape, jnp.int32),
            pltpu.SemaphoreType.DMA((2, 7)),
        ),
        hbm=True,
        mib=56,
    )
    pair, cross = from_neighbours(own)

    matrix = error_inverse.reshape(1, wide, wide)
    blocks = [matrix] + [apart_by(matrix, "gx", stride) for stride in range(2, cols_x, 2)]
    halves = jax.ShapeDtypeStruct((cells, device_count * capacity), jnp.bfloat16)
    factors, *interp = call(
        functools.partial(prepare_kernel, device_count, capacity, lon_cols),
        (f32(3, layers, 8, LANES), halves, halves),
        (
            vert_coef.reshape(layers, cells // LANES, LANES),
            obs_owner.reshape(1, obs_count),
            obs_row.reshape(1, obs_count),
            obs_col.reshape(1, obs_count),
            obs_frac.reshape(2, obs_count),
        ),
        flops=20_000_000,
        mib=16,
    )
    extended = 3 * rows + (-3 * rows) % 8
    packed, coef = call(
        functools.partial(first_lateral_kernel, kv, rows, tiles),
        (f32(cols_x, 2 * kv, LANES), f32(5, extended, lons)),
        (interp[0], direction_n, *faces, pair, cross),
        after=1,
        scratch=(
            pltpu.VMEM((3, extended, lons), jnp.float32),
        ),
        flops=4_000_000,
    )
    held_blocks = call(
        hold_kernel, f32(len(blocks), wide - 8, wide), (packed, *blocks), after=1
    )
    fetched = [held_blocks] + [apart_by(held_blocks, "gy", stride) for stride in range(1, rows_y)]
    columns = lax.all_to_all(packed, "gx", split_axis=0, concat_axis=0, tiled=True)
    smoothed = call(
        functools.partial(smooth_kernel, layers, held),
        f32(2 * wide, LANES),
        (columns.reshape(cols_x * 2 * kv, LANES), factors),
        flops=1000,
    )
    far = apart_by(
        call(
            join_kernel, f32(device_count // 2, wide // 2 + 8, wide), (columns, *fetched), after=1
        ),
        "gx",
        1,
    )
    half = device_count // 2 * capacity
    weighted, profile = call(
        functools.partial(profile_kernel, capacity),
        (f32(wide, half), f32(wide, half)),
        (smoothed, *interp, *fetched),
        flops=400_000_000,
        mib=16,
    )
    spread = call(
        functools.partial(spread_kernel, layers, held, capacity),
        f32(cols_x * 2 * kv, LANES),
        (weighted, profile, factors, *interp, far),
        scratch=(pltpu.VMEM((2 * wide, LANES), jnp.float32),),
        flops=400_000_000,
        mib=16,
    )
    tile = lax.all_to_all(
        spread.reshape(cols_x, 2 * kv, LANES), "gx", split_axis=0, concat_axis=0, tiled=True
    )
    pair, cross = from_neighbours(tile)
    image, sums = call(
        functools.partial(second_lateral_kernel, kv, rows, tiles),
        (f32(*direction_n.shape), f32(device_count, 1, LANES)),
        (tile, pair, cross, coef, direction_n, residual_n),
        flops=4_000_000,
    )
    sums = lax.all_to_all(sums, ("gy", "gx"), split_axis=0, concat_axis=0, tiled=True)
    after = call(
        update_kernel,
        (f32(*direction_n.shape),) * 3,
        (sums, direction_n, solution_n, residual_n, image),
    )
    return tuple(from_native(x, direction.shape) for x in after)


def gathers(mesh, shapes):
    rows_y, cols_x = mesh.shape["gy"], mesh.shape["gx"]
    devices = rows_y * cols_x
    if any(size < 2 or size & (size - 1) for size in (rows_y, cols_x)):
        return False
    direction, vert_coef, obs_row, error_inverse = shapes
    var_count, layers, lat_rows, lons = direction
    rows, held = lat_rows // rows_y, layers // cols_x
    obs_count, wide = obs_row[-1], error_inverse[-1]
    capacity = 2 * obs_count // devices
    return (
        rows == NSTEP == 4
        and var_count == 4
        and (var_count * held) % 8 == 0
        and lons // cols_x * 2 == LANES
        and wide == LANES
        and capacity > 0
        and LANES % capacity == 0
        and devices // 2 % (LANES // capacity) == 0
        and devices * wide * wide * 4 <= 8 * 1024 * 1024
    )


def padded(cells, sides, width):
    for axis, dim in sides:
        count = lax.axis_size(axis)
        ends = count - 1
        head = lax.slice_in_dim(cells, 0, width, axis=dim)
        tail = lax.slice_in_dim(cells, cells.shape[dim] - width, cells.shape[dim], axis=dim)
        cells = jnp.concatenate(
            [
                lax.ppermute(tail, axis, [(i, (i + 1) % count) for i in range(ends)]),
                cells,
                lax.ppermute(head, axis, [((i + 1) % count, i) for i in range(ends)]),
            ],
            axis=dim,
        )
    return cells


def lateral_faces(north_ext, east_ext, ocean_ext):
    ocean_next = jnp.concatenate([ocean_ext[1:], jnp.zeros_like(ocean_ext[:1])], axis=0)
    north_face = north_ext * ocean_ext * ocean_next
    east_face = east_ext * ocean_ext * jnp.roll(ocean_ext, -1, axis=1)
    return (north_face, east_face, ocean_ext)


def diffuse_once(values_grid, north_face, east_face, ocean_ext):
    north_flux = north_face[:-1] * (values_grid[:, :, 1:, :] - values_grid[:, :, :-1, :])
    east_flux = east_face * (jnp.roll(values_grid, -1, axis=3) - values_grid)
    lateral = east_flux - jnp.roll(east_flux, 1, axis=3)
    return (
        ocean_ext[1:-1] * values_grid[:, :, 1:-1, :]
        + north_flux[:, :, 1:, :]
        - north_flux[:, :, :-1, :]
        + lateral[:, :, 1:-1, :]
    )


def lateral_pass(values_tile, faces):
    north_face, east_face, ocean_ext = faces
    grown = padded(values_tile, (("gy", 2),), NSTEP)
    total_rows = grown.shape[2]
    for step_index in range(NSTEP):
        upper = total_rows - step_index
        grown = diffuse_once(
            grown,
            north_face[step_index:upper],
            east_face[step_index:upper],
            ocean_ext[step_index:upper],
        )
    return grown


def vertical_factors(vert_coef):
    inverse_rows = []
    upper_ratio = []
    for layer_index in range(vert_coef.shape[0]):
        diagonal = 1.0 + vert_coef[layer_index]
        if layer_index > 0:
            diagonal = (
                diagonal + vert_coef[layer_index - 1] + vert_coef[layer_index - 1] * upper_ratio[-1]
            )
        inverse = 1.0 / diagonal
        inverse_rows.append(inverse)
        upper_ratio.append(-vert_coef[layer_index] * inverse)
    return (inverse_rows, upper_ratio)


def vertical_solve(values_col, vert_coef, factors):
    inverse_rows, upper_ratio = factors
    layers = values_col.shape[1]
    forward = []
    for layer_index in range(layers):
        source = values_col[:, layer_index]
        if layer_index > 0:
            source = source + vert_coef[layer_index - 1] * forward[-1]
        forward.append(source * inverse_rows[layer_index])
    result = [forward[-1]]
    for layer_index in range(layers - 2, -1, -1):
        result.append(forward[layer_index] - upper_ratio[layer_index] * result[-1])
    return jnp.stack(result[::-1], axis=1)


def observe_weigh_spread(columns, obs_owner, obs_row, obs_col, obs_frac, error_inverse):
    var_count, lev_count, lat_rows, lon_cols = columns.shape
    kv_width = var_count * lev_count
    rows_y = lax.axis_size("gy")
    cols_x = lax.axis_size("gx")
    device_count = rows_y * cols_x
    obs_count = obs_row.shape[-1]
    capacity = 2 * obs_count // device_count
    flat = columns.reshape(kv_width, lat_rows * lon_cols)
    cell = obs_row.reshape(-1) * lon_cols + obs_col.reshape(-1)
    corners = (cell, cell + 1, cell + lon_cols, cell + lon_cols + 1)
    lat_frac = obs_frac[0, 0, 0]
    lon_frac = obs_frac[0, 0, 1]
    weights = (
        (1.0 - lat_frac) * (1.0 - lon_frac),
        (1.0 - lat_frac) * lon_frac,
        lat_frac * (1.0 - lon_frac),
        lat_frac * lon_frac,
    )
    profile = weights[0] * jnp.take(flat, corners[0], axis=1)
    for corner_index in range(1, 4):
        profile = profile + weights[corner_index] * jnp.take(flat, corners[corner_index], axis=1)
    owners = obs_owner.reshape(-1)
    onehot = (owners[:, None] == jnp.arange(device_count, dtype=jnp.int32)[None, :]).astype(
        jnp.int32
    )
    running = jnp.cumsum(onehot, axis=0)
    rank_in = jnp.sum(running * onehot, axis=1) - 1
    slot = owners * capacity + rank_in
    outgoing = jnp.zeros((device_count * capacity, kv_width), jnp.float32).at[slot].set(profile.T)
    outgoing = outgoing.reshape(rows_y, cols_x, capacity, kv_width)
    matrix = error_inverse.reshape(kv_width, kv_width)
    arrived = lax.all_to_all(
        lax.all_to_all(outgoing, "gy", split_axis=0, concat_axis=0, tiled=True),
        "gx",
        split_axis=1,
        concat_axis=1,
        tiled=True,
    )
    weighted = jnp.dot(
        arrived.reshape(-1, kv_width),
        matrix,
        precision=lax.Precision.HIGHEST,
        preferred_element_type=jnp.float32,
    ).reshape(rows_y, cols_x, capacity, kv_width)
    returned = lax.all_to_all(
        lax.all_to_all(weighted, "gy", split_axis=0, concat_axis=0, tiled=True),
        "gx",
        split_axis=1,
        concat_axis=1,
        tiled=True,
    )
    back = returned.reshape(device_count * capacity, kv_width)[slot].T
    spread = jnp.zeros((kv_width, lat_rows * lon_cols), jnp.float32)
    for corner_index in range(4):
        spread = spread.at[:, corners[corner_index]].add(weights[corner_index] * back)
    return spread.reshape(var_count, lev_count, lat_rows, lon_cols)


def per_device(
    direction,
    solution,
    residual,
    north_coef,
    east_coef,
    ocean,
    vert_coef,
    obs_owner,
    obs_row,
    obs_col,
    obs_frac,
    error_inverse,
):
    stacked = jnp.stack([north_coef, east_coef, ocean.astype(jnp.float32)])
    reach = NSTEP
    grown_coef = padded(stacked, (("gy", 1),), reach)
    faces = lateral_faces(grown_coef[0], grown_coef[1], grown_coef[2])
    factors = vertical_factors(vert_coef)
    smoothed = lateral_pass(direction, faces)
    columns = lax.all_to_all(smoothed, "gx", split_axis=3, concat_axis=1, tiled=True)
    columns = vertical_solve(columns, vert_coef, factors)
    spread = observe_weigh_spread(columns, obs_owner, obs_row, obs_col, obs_frac, error_inverse)
    spread = vertical_solve(spread, vert_coef, factors)
    tiles = lax.all_to_all(spread, "gx", split_axis=1, concat_axis=3, tiled=True)
    image = direction + lateral_pass(tiles, faces)
    norm_now, curvature = lax.psum(
        (jnp.sum(residual * residual), jnp.sum(direction * image)), ("gy", "gx")
    )
    alpha = norm_now / curvature
    residual_next = residual - alpha * image
    norm_next = lax.psum(jnp.sum(residual_next * residual_next), ("gy", "gx"))
    solution_next = solution + alpha * direction
    direction_next = residual_next + norm_next / norm_now * direction
    return (solution_next, residual_next, direction_next)


def solution(mesh):
    in_specs = (
        P(None, "gx", "gy", None),
        P(None, "gx", "gy", None),
        P(None, "gx", "gy", None),
        P("gy", None),
        P("gy", None),
        P("gy", None),
        P(None, "gy", "gx"),
        P("gy", "gx", None, None),
        P("gy", "gx", None),
        P("gy", "gx", None),
        P("gy", "gx", None, None),
        P("gy", "gx", None, None),
    )
    out_specs = (P(None, "gx", "gy", None),) * 3

    def step(*arrays):
        shapes = [arrays[at].shape for at in (0, 6, 8, 11)]
        local = per_device_gathered if gathers(mesh, shapes) else per_device
        return jax.shard_map(
            local, mesh=mesh, in_specs=in_specs, out_specs=out_specs, check_vma=False
        )(*arrays)

    return step
```

```python
import functools
import math

import jax
import jax.numpy as jnp
from jax import lax
from jax.experimental import pallas as pl
from jax.experimental.pallas import tpu as pltpu
from jax.sharding import PartitionSpec as P

NSTEP = 4
LANES = 128


def to_native(tile):
    kv, rows, lons = tile.shape[0] * tile.shape[1], tile.shape[2], tile.shape[3]
    return tile.reshape(kv, rows, lons // LANES, LANES).swapaxes(1, 2).reshape(-1, LANES)


def from_native(flat, shape):
    kv, rows, lons = shape[0] * shape[1], shape[2], shape[3]
    return flat.reshape(kv, lons // LANES, rows, LANES).swapaxes(1, 2).reshape(shape)


def native_rows(ref, row, rows, tiles, half):
    parts = [
        ref[pl.ds((half * 8 * tiles + tile) * rows + row, 8, stride=tiles * rows), :]
        for tile in range(tiles)
    ]
    return jnp.concatenate(parts, axis=1)


def lane_low(shape):
    return lax.broadcasted_iota(jnp.int32, shape, 1) < LANES // 2


def lateral_rows(rows, coef, reach):
    for step in range(reach):
        after = []
        for i in range(1, len(rows) - 1):
            at = step + i
            u = rows[i]
            width = u.shape[1]
            after.append(
                coef[0, at : at + 1, :] * u
                + coef[1, at : at + 1, :] * rows[i + 1]
                + coef[2, at : at + 1, :] * rows[i - 1]
                + coef[3, at : at + 1, :] * pltpu.roll(u, width - 1, 1)
                + coef[4, at : at + 1, :] * pltpu.roll(u, 1, 1)
            )
        rows = after
    return rows


def sort_halo(pair_ref, cross_ref, low_ref, high_ref):
    odd = lax.rem(lax.axis_index("gy"), 2) == 1

    @pl.when(odd)
    def _():
        low_ref[...] = pair_ref[...]
        high_ref[...] = cross_ref[...]

    @pl.when(jnp.logical_not(odd))
    def _():
        low_ref[...] = cross_ref[...]
        high_ref[...] = pair_ref[...]


def triangle_masks():
    shape = (LANES // 2, LANES)
    lane = lax.broadcasted_iota(jnp.int32, shape, 1)
    return lane, lane - lax.broadcasted_iota(jnp.int32, shape, 0)


def pack_symmetric(matrix, packed_ref):
    half = LANES // 2
    lane, away = triangle_masks()
    top, bottom = matrix[:half], matrix[half:]
    corner = jnp.where(away <= 0, top, pltpu.roll(bottom, half, 1))
    packed_ref[0:half, :] = jnp.where(lane < half, corner, top)
    diagonal = jnp.sum(jnp.where(away == half, bottom, 0.0), axis=0, keepdims=True)
    packed_ref[half:, :] = jnp.broadcast_to(diagonal, (packed_ref.shape[0] - half, LANES))


def unpack_symmetric(packed):
    half = LANES // 2
    lane, away = triangle_masks()
    rows, diagonal = packed[:half], packed[half : half + 1]
    turned = jnp.concatenate([rows, rows], axis=0).T
    top = jnp.where((lane < half) & (away > 0), turned[:half], rows)
    corner = jnp.where(
        away > half, pltpu.roll(rows, half, 1), jnp.where(away == half, diagonal, turned[:half])
    )
    return jnp.concatenate([top, jnp.where(lane < half, turned[half:], corner)], axis=0)


def halo_kernel(
    chunks, direction_ref, north_ref, east_ref, ocean_ref, own_ref, stage_ref, mask_ref, sems
):
    cells, size = direction_ref.shape[0], north_ref.shape[0]
    rows = cells // chunks
    spans = [(at * rows, rows) for at in range(chunks)] + [(cells, 2 * size)]
    faces = [
        pltpu.make_async_copy(ref, to, sems.at[0, at])
        for at, (ref, to) in enumerate(
            (
                (ocean_ref, mask_ref),
                (north_ref, stage_ref.at[pl.ds(cells, size)]),
                (east_ref, stage_ref.at[pl.ds(cells + size, size)]),
            )
        )
    ]
    arrive = [
        pltpu.make_async_copy(
            direction_ref.at[pl.ds(start, count)], stage_ref.at[pl.ds(start, count)], sems.at[0, 3 + at]
        )
        for at, (start, count) in enumerate(spans[:-1])
    ]
    leave = [
        pltpu.make_async_copy(
            stage_ref.at[pl.ds(start, count)], own_ref.at[pl.ds(start, count)], sems.at[1, at]
        )
        for at, (start, count) in enumerate(spans)
    ]
    for copy in arrive + faces:
        copy.start()
    for at, copy in enumerate(arrive):
        copy.wait()
        leave[at].start()
    for copy in faces:
        copy.wait()
    mask = mask_ref[...].astype(jnp.float32)
    for kind in range(2):
        here = slice(cells + kind * size, cells + (kind + 1) * size)
        stage_ref[here, :] = stage_ref[here, :] * mask
    leave[-1].start()
    for copy in leave:
        copy.wait()


def join_kernel(_, *refs):
    blocks, (out_ref,) = refs[:-1], refs[-1:]
    size = blocks[0].shape[0]
    for at, block in enumerate(blocks):
        out_ref[at * size : (at + 1) * size] = block[:, : out_ref.shape[1], :]


def hold_kernel(_, *refs):
    blocks, (packed_ref,) = refs[:-1], refs[-1:]
    for at, block in enumerate(blocks):
        pack_symmetric(block[0], packed_ref.at[at])


def first_lateral_kernel(
    kv,
    rows,
    tiles,
    _,
    own_ref,
    north_ref,
    east_ref,
    ocean_ref,
    pair_ref,
    cross_ref,
    packed_ref,
    coef_ref,
    ext_ref,
    low_ref,
    high_ref,
):
    lons = tiles * LANES
    cells = kv * tiles * rows
    sort_halo(pair_ref, cross_ref, low_ref, high_ref)
    at_y, rows_y = lax.axis_index("gy"), lax.axis_size("gy")
    inside = (
        jnp.where(at_y > 0, 1.0, 0.0).astype(jnp.float32),
        jnp.where(at_y < rows_y - 1, 1.0, 0.0).astype(jnp.float32),
    )
    ext_ref[...] = jnp.zeros_like(ext_ref)
    for tile in range(tiles):
        lanes = slice(tile * LANES, (tile + 1) * LANES)
        here = slice(tile * rows, (tile + 1) * rows)
        mask = ocean_ref[here, :].astype(jnp.float32)
        ext_ref[0, rows : 2 * rows, lanes] = north_ref[here, :] * mask
        ext_ref[1, rows : 2 * rows, lanes] = east_ref[here, :] * mask
        ext_ref[2, rows : 2 * rows, lanes] = mask
        for block, ref in ((0, low_ref), (2, high_ref)):
            across = slice(block * rows, (block + 1) * rows)
            for kind in range(2):
                start = cells + (kind * tiles + tile) * rows
                ext_ref[kind, across, lanes] = ref[start : start + rows, :] * inside[block // 2]
            ext_ref[2, across, lanes] = jnp.where(ext_ref[0, across, lanes] > 0.0, 1.0, 0.0)
    total = ext_ref.shape[1]
    ocean = ext_ref[2]
    north_face = ext_ref[0] * pltpu.roll(ocean, total - 1, 0)
    east_face = ext_ref[1] * pltpu.roll(ocean, lons - 1, 1)
    south_face = pltpu.roll(north_face, 1, 0)
    west_face = pltpu.roll(east_face, 1, 1)
    coef_ref[0] = ocean - north_face - south_face - east_face - west_face
    coef_ref[1] = north_face
    coef_ref[2] = south_face
    coef_ref[3] = east_face
    coef_ref[4] = west_face
    low = lane_low((8, LANES))
    for half in range(kv // 8):
        grown = [
            native_rows(ref, row, rows, tiles, half)
            for ref in (low_ref, own_ref, high_ref)
            for row in range(rows)
        ]
        done = lateral_rows(grown, coef_ref, rows)
        for pair in range(rows // 2):
            at = pair * kv + half * 8
            for tile in range(tiles):
                first = done[2 * pair][:, tile * LANES : (tile + 1) * LANES]
                second = done[2 * pair + 1][:, tile * LANES : (tile + 1) * LANES]
                packed_ref[2 * tile, at : at + 8, :] = jnp.where(
                    low, first, pltpu.roll(second, LANES // 2, 1)
                )
                packed_ref[2 * tile + 1, at : at + 8, :] = jnp.where(
                    low, pltpu.roll(first, LANES // 2, 1), second
                )


def second_lateral_kernel(
    kv,
    rows,
    tiles,
    own_ref,
    pair_ref,
    cross_ref,
    coef_ref,
    direction_ref,
    residual_ref,
    image_ref,
    sums_ref,
    low_ref,
    high_ref,
):
    sort_halo(pair_ref, cross_ref, low_ref, high_ref)
    low = lane_low((8, LANES))
    totals = [jnp.zeros((8, tiles * LANES), jnp.float32) for _ in range(4)]
    for half in range(kv // 8):
        grown = []
        for ref in (low_ref, own_ref, high_ref):
            for pair in range(rows // 2):
                firsts, seconds = [], []
                at = pair * kv + half * 8
                for tile in range(tiles):
                    even = ref[2 * tile, at : at + 8, :]
                    odd = ref[2 * tile + 1, at : at + 8, :]
                    firsts.append(jnp.where(low, even, pltpu.roll(odd, LANES // 2, 1)))
                    seconds.append(jnp.where(low, pltpu.roll(even, LANES // 2, 1), odd))
                grown.append(jnp.concatenate(firsts, axis=1))
                grown.append(jnp.concatenate(seconds, axis=1))
        done = lateral_rows(grown, coef_ref, rows)
        for row in range(rows):
            direction = native_rows(direction_ref, row, rows, tiles, half)
            residual = native_rows(residual_ref, row, rows, tiles, half)
            image = direction + done[row]
            for tile in range(tiles):
                image_ref[pl.ds((half * 8 * tiles + tile) * rows + row, 8, stride=tiles * rows), :] = image[
                    :, tile * LANES : (tile + 1) * LANES
                ]
            totals[0] = totals[0] + residual * residual
            totals[1] = totals[1] + direction * image
            totals[2] = totals[2] + residual * image
            totals[3] = totals[3] + image * image
    lane = lax.broadcasted_iota(jnp.int32, (1, LANES), 1)
    line = jnp.zeros((1, LANES), jnp.float32)
    for at, total in enumerate(totals):
        line = jnp.where(lane == at, jnp.sum(total), line)
    for device in range(sums_ref.shape[0]):
        sums_ref[device] = line


def update_kernel(sums_ref, direction_ref, solution_ref, residual_ref, image_ref, sol_ref, res_ref, dir_ref):
    line = jnp.sum(sums_ref[...], axis=0)
    lane = lax.broadcasted_iota(jnp.int32, line.shape, 1)

    def pick(at):
        return jnp.sum(jnp.where(lane == at, line, 0.0), axis=1, keepdims=True)

    norm_now, curvature, cross, square = pick(0), pick(1), pick(2), pick(3)
    alpha = norm_now / curvature
    norm_next = norm_now - 2.0 * alpha * cross + alpha * alpha * square
    beta = norm_next / norm_now
    direction = direction_ref[...]
    residual_next = residual_ref[...] - alpha * image_ref[...]
    sol_ref[...] = solution_ref[...] + alpha * direction
    res_ref[...] = residual_next
    dir_ref[...] = residual_next + beta * direction


def split(value):
    high = value.astype(jnp.bfloat16)
    return high, (value - high.astype(jnp.float32)).astype(jnp.bfloat16)


def dot_parts(left, right, contract):
    dims = (contract, ((), ()))
    total = lax.dot_general(left[0], right[0], dims, preferred_element_type=jnp.float32)
    total = total + lax.dot_general(left[0], right[1], dims, preferred_element_type=jnp.float32)
    return total + lax.dot_general(left[1], right[0], dims, preferred_element_type=jnp.float32)


def prepare_kernel(
    devices,
    capacity,
    lon_cols,
    vert_ref,
    owner_ref,
    row_ref,
    col_ref,
    frac_ref,
    factor_ref,
    high_ref,
    low_ref,
):
    vertical_factors_of(vert_ref, factor_ref)
    count = owner_ref.shape[1]
    slots = devices * capacity
    me = lax.axis_index("gy") * lax.axis_size("gx") + lax.axis_index("gx")
    apart = jnp.bitwise_xor(owner_ref[...], me)
    place = jnp.bitwise_and(apart, 1) * (devices // 2) + jnp.right_shift(apart, 1)
    named = lax.broadcasted_iota(jnp.int32, (devices, count), 0) == place
    before = lax.broadcasted_iota(jnp.int32, (count, count), 0) <= lax.broadcasted_iota(
        jnp.int32, (count, count), 1
    )
    running = jnp.dot(
        jnp.where(named, 1.0, 0.0).astype(jnp.bfloat16),
        jnp.where(before, 1.0, 0.0).astype(jnp.bfloat16),
        preferred_element_type=jnp.float32,
    )
    rank = jnp.sum(jnp.where(named, running, 0.0), axis=0, keepdims=True) - 1.0
    slot = place * capacity + rank.astype(jnp.int32)
    chosen = jnp.where(
        lax.broadcasted_iota(jnp.int32, (slots, count), 0) == slot, 1.0, 0.0
    ).astype(jnp.bfloat16)
    lat_frac = frac_ref[0:1, :]
    lon_frac = frac_ref[1:2, :]
    cell = (row_ref[...] * lon_cols + col_ref[...]).astype(jnp.float32)
    values = jnp.concatenate(
        [
            (1.0 - lat_frac) * (1.0 - lon_frac),
            (1.0 - lat_frac) * lon_frac,
            lat_frac * (1.0 - lon_frac),
            lat_frac * lon_frac,
            cell,
            jnp.zeros((3, count), jnp.float32),
        ],
        axis=0,
    )
    high, rest = split(values)
    low, rest = split(values - high.astype(jnp.float32))
    parts = jnp.concatenate([high.astype(jnp.float32), low.astype(jnp.float32), rest.astype(jnp.float32)], axis=0)
    placed = lax.dot_general(
        parts.astype(jnp.bfloat16), chosen, (((1,), (1,)), ((), ())), preferred_element_type=jnp.float32
    )
    placed = placed[0:8] + placed[8:16] + placed[16:24]
    first = jnp.round(placed[4:5, :]).astype(jnp.int32)
    away = lax.broadcasted_iota(jnp.int32, high_ref.shape, 0) - first
    interp = jnp.where(
        away == 0,
        placed[0:1, :],
        jnp.where(
            away == 1,
            placed[1:2, :],
            jnp.where(away == lon_cols, placed[2:3, :], jnp.where(away == lon_cols + 1, placed[3:4, :], 0.0)),
        ),
    )
    high_ref[...], low_ref[...] = split(interp)


def vertical_factors_of(vert_ref, factor_ref):
    layers = vert_ref.shape[0]
    top = lax.broadcasted_iota(jnp.int32, (8, LANES), 0) < 4
    coef = [jnp.where(top, vert_ref[layer, 0:1, :], vert_ref[layer, 1:2, :]) for layer in range(layers)]
    ratio = None
    for layer in range(layers):
        diagonal = 1.0 + coef[layer]
        if layer > 0:
            diagonal = diagonal + coef[layer - 1] - coef[layer - 1] * ratio
        inverse = 1.0 / diagonal
        ratio = coef[layer] * inverse
        factor_ref[0, layer] = inverse
        factor_ref[1, layer] = coef[layer - 1] * inverse if layer > 0 else jnp.zeros_like(inverse)
        factor_ref[2, layer] = ratio


def solve_columns(read, write, factor_ref, layers):
    forward = []
    for layer in range(layers):
        value = read(layer) * factor_ref[0, layer]
        if layer > 0:
            value = value + factor_ref[1, layer] * forward[-1]
        forward.append(value)
    value = forward[-1]
    write(layers - 1, value)
    for layer in range(layers - 2, -1, -1):
        value = forward[layer] + factor_ref[2, layer] * value
        write(layer, value)


def packed_at(layer, held):
    return pl.ds((layer // held) * 8 * held + layer % held, 8, stride=held)


def weigh(profile, matrices, capacity):
    kv = profile.shape[0]
    owners = LANES // capacity
    mine = lax.broadcasted_iota(jnp.int32, (kv, LANES), 1) // capacity
    tiles = []
    for tile in range(profile.shape[1] // LANES):
        values = profile[:, tile * LANES : (tile + 1) * LANES]
        masked = jnp.concatenate([jnp.where(mine == owner, values, 0.0) for owner in range(owners)], axis=0)
        beside = jnp.concatenate([matrices(tile * owners + owner) for owner in range(owners)], axis=1)
        tiles.append(dot_parts(split(beside), split(masked), ((1,), (0,))))
    return jnp.concatenate(tiles, axis=1)


def smooth_kernel(layers, held, packed_ref, factor_ref, column_ref):
    def read(layer):
        return packed_ref[packed_at(layer, held), :]

    def write(layer, value):
        column_ref[pl.ds(layer, 8, stride=layers), :] = value

    solve_columns(read, write, factor_ref, layers)


def profile_kernel(capacity, column_ref, high_ref, low_ref, *refs):
    near_refs, (spread_ref, profile_ref) = refs[:-2], refs[-2:]
    kv, half = profile_ref.shape
    size = near_refs[0].shape[0]
    columns = jnp.concatenate([column_ref[0:kv, :], column_ref[kv : 2 * kv, :]], axis=1)
    profile = dot_parts(split(columns), (high_ref[...], low_ref[...]), ((1,), (0,)))
    profile_ref[...] = profile[:, half:]
    weighted = weigh(
        profile[:, :half], lambda at: unpack_symmetric(near_refs[at // size][at % size]), capacity
    )
    spread_ref[...] = dot_parts(split(weighted), (high_ref[:, :half], low_ref[:, :half]), ((1,), (1,)))


def spread_kernel(
    layers, held, capacity, near_ref, profile_ref, factor_ref, high_ref, low_ref, far_ref, out_ref, column_ref
):
    kv = near_ref.shape[0]
    half = profile_ref.shape[1]
    weighted = weigh(profile_ref[...], lambda at: unpack_symmetric(far_ref[at]), capacity)
    spread = near_ref[...] + dot_parts(
        split(weighted), (high_ref[:, half:], low_ref[:, half:]), ((1,), (1,))
    )
    column_ref[0:kv, :] = spread[:, :LANES]
    column_ref[kv : 2 * kv, :] = spread[:, LANES:]

    def read(layer):
        return column_ref[pl.ds(layer, 8, stride=layers), :]

    def write(layer, value):
        out_ref[packed_at(layer, held), :] = value

    solve_columns(read, write, factor_ref, layers)


def vmem(count):
    return [pl.BlockSpec(memory_space=pltpu.VMEM)] * count


def call(kernel, out_shape, inputs, scratch=(), after=0, hbm=False, flops=1_000_000, mib=8):
    specs = [pl.BlockSpec(memory_space=pl.ANY)] * after + vmem(len(inputs) - after)
    outs = vmem(len(out_shape) if isinstance(out_shape, tuple) else 1)
    if hbm:
        specs, outs = ([pl.BlockSpec(memory_space=pltpu.HBM)] * len(x) for x in (specs, outs))
    moved = sum(math.prod(x.shape) * 4 for x in inputs)
    return pl.pallas_call(
        kernel,
        out_shape=out_shape,
        in_specs=specs,
        out_specs=tuple(outs) if isinstance(out_shape, tuple) else outs[0],
        scratch_shapes=list(scratch),
        compiler_params=pltpu.CompilerParams(vmem_limit_bytes=mib * 1024 * 1024),
        cost_estimate=pl.CostEstimate(flops=flops, bytes_accessed=moved, transcendentals=0),
    )(*inputs)


def f32(*shape):
    return jax.ShapeDtypeStruct(shape, jnp.float32)


def from_neighbours(block):
    count = lax.axis_size("gy")
    pair = lax.ppermute(block, "gy", [(i, i ^ 1) for i in range(count)])
    cross = lax.ppermute(block, "gy", [(i, (i + (1 if i % 2 else -1)) % count) for i in range(count)])
    return pair, cross


def apart_by(block, axis, stride):
    return lax.ppermute(block, axis, [(i, i ^ stride) for i in range(lax.axis_size(axis))])


def per_device_gathered(
    direction,
    solution,
    residual,
    north_coef,
    east_coef,
    ocean,
    vert_coef,
    obs_owner,
    obs_row,
    obs_col,
    obs_frac,
    error_inverse,
):
    var_count, held, rows, lons = direction.shape
    kv = var_count * held
    tiles = lons // LANES
    layers, _, lon_cols = vert_coef.shape
    rows_y, cols_x = lax.axis_size("gy"), lax.axis_size("gx")
    device_count = rows_y * cols_x
    obs_count = obs_row.shape[-1]
    capacity = 2 * obs_count // device_count
    wide = error_inverse.shape[-1]
    cells = rows * lon_cols

    direction_n = to_native(direction)
    residual_n = to_native(residual)
    solution_n = to_native(solution)
    faces = [to_native(x[None, None]) for x in (north_coef, east_coef, ocean)]
    own = call(
        functools.partial(halo_kernel, 4),
        f32(direction_n.shape[0] + 2 * faces[0].shape[0], LANES),
        (direction_n, *faces),
        scratch=(
            pltpu.VMEM((direction_n.shape[0] + 2 * faces[0].shape[0], LANES), jnp.float32),
            pltpu.VMEM(faces[0].shape, jnp.int32),
            pltpu.SemaphoreType.DMA((2, 7)),
        ),
        hbm=True,
        mib=56,
    )
    pair, cross = from_neighbours(own)

    matrix = error_inverse.reshape(1, wide, wide)
    blocks = [matrix] + [apart_by(matrix, "gx", stride) for stride in range(2, cols_x, 2)]
    halves = jax.ShapeDtypeStruct((cells, device_count * capacity), jnp.bfloat16)
    factors, *interp = call(
        functools.partial(prepare_kernel, device_count, capacity, lon_cols),
        (f32(3, layers, 8, LANES), halves, halves),
        (
            vert_coef.reshape(layers, cells // LANES, LANES),
            obs_owner.reshape(1, obs_count),
            obs_row.reshape(1, obs_count),
            obs_col.reshape(1, obs_count),
            obs_frac.reshape(2, obs_count),
        ),
        flops=20_000_000,
        mib=16,
    )
    extended = 3 * rows + (-3 * rows) % 8
    packed, coef = call(
        functools.partial(first_lateral_kernel, kv, rows, tiles),
        (f32(cols_x, 2 * kv, LANES), f32(5, extended, lons)),
        (interp[0], direction_n, *faces, pair, cross),
        after=1,
        scratch=(
            pltpu.VMEM((3, extended, lons), jnp.float32),
            pltpu.VMEM(own.shape, jnp.float32),
            pltpu.VMEM(own.shape, jnp.float32),
        ),
        flops=4_000_000,
    )
    held_blocks = call(
        hold_kernel, f32(len(blocks), wide - 8, wide), (packed, *blocks), after=1
    )
    fetched = [held_blocks] + [apart_by(held_blocks, "gy", stride) for stride in range(1, rows_y)]
    columns = lax.all_to_all(packed, "gx", split_axis=0, concat_axis=0, tiled=True)
    smoothed = call(
        functools.partial(smooth_kernel, layers, held),
        f32(2 * wide, LANES),
        (columns.reshape(cols_x * 2 * kv, LANES), factors),
        flops=1000,
    )
    far = apart_by(
        call(
            join_kernel, f32(device_count // 2, wide // 2 + 8, wide), (columns, *fetched), after=1
        ),
        "gx",
        1,
    )
    half = device_count // 2 * capacity
    weighted, profile = call(
        functools.partial(profile_kernel, capacity),
        (f32(wide, cells), f32(wide, half)),
        (smoothed, *interp, *fetched),
        flops=400_000_000,
        mib=16,
    )
    spread = call(
        functools.partial(spread_kernel, layers, held, capacity),
        f32(cols_x * 2 * kv, LANES),
        (weighted, profile, factors, *interp, far),
        scratch=(pltpu.VMEM((2 * wide, LANES), jnp.float32),),
        flops=400_000_000,
        mib=16,
    )
    tile = lax.all_to_all(
        spread.reshape(cols_x, 2 * kv, LANES), "gx", split_axis=0, concat_axis=0, tiled=True
    )
    pair, cross = from_neighbours(tile)
    image, sums = call(
        functools.partial(second_lateral_kernel, kv, rows, tiles),
        (f32(*direction_n.shape), f32(device_count, 1, LANES)),
        (tile, pair, cross, coef, direction_n, residual_n),
        scratch=(pltpu.VMEM(tile.shape, jnp.float32), pltpu.VMEM(tile.shape, jnp.float32)),
        flops=4_000_000,
    )
    sums = lax.all_to_all(sums, ("gy", "gx"), split_axis=0, concat_axis=0, tiled=True)
    after = call(
        update_kernel,
        (f32(*direction_n.shape),) * 3,
        (sums, direction_n, solution_n, residual_n, image),
    )
    return tuple(from_native(x, direction.shape) for x in after)


def gathers(mesh, shapes):
    rows_y, cols_x = mesh.shape["gy"], mesh.shape["gx"]
    devices = rows_y * cols_x
    if any(size < 2 or size & (size - 1) for size in (rows_y, cols_x)):
        return False
    direction, vert_coef, obs_row, error_inverse = shapes
    var_count, layers, lat_rows, lons = direction
    rows, held = lat_rows // rows_y, layers // cols_x
    obs_count, wide = obs_row[-1], error_inverse[-1]
    capacity = 2 * obs_count // devices
    return (
        rows == NSTEP == 4
        and var_count == 4
        and (var_count * held) % 8 == 0
        and lons // cols_x * 2 == LANES
        and wide == LANES
        and capacity > 0
        and LANES % capacity == 0
        and devices // 2 % (LANES // capacity) == 0
        and devices * wide * wide * 4 <= 8 * 1024 * 1024
    )


def padded(cells, sides, width):
    for axis, dim in sides:
        count = lax.axis_size(axis)
        ends = count - 1
        head = lax.slice_in_dim(cells, 0, width, axis=dim)
        tail = lax.slice_in_dim(cells, cells.shape[dim] - width, cells.shape[dim], axis=dim)
        cells = jnp.concatenate(
            [
                lax.ppermute(tail, axis, [(i, (i + 1) % count) for i in range(ends)]),
                cells,
                lax.ppermute(head, axis, [((i + 1) % count, i) for i in range(ends)]),
            ],
            axis=dim,
        )
    return cells


def lateral_faces(north_ext, east_ext, ocean_ext):
    ocean_next = jnp.concatenate([ocean_ext[1:], jnp.zeros_like(ocean_ext[:1])], axis=0)
    north_face = north_ext * ocean_ext * ocean_next
    east_face = east_ext * ocean_ext * jnp.roll(ocean_ext, -1, axis=1)
    return (north_face, east_face, ocean_ext)


def diffuse_once(values_grid, north_face, east_face, ocean_ext):
    north_flux = north_face[:-1] * (values_grid[:, :, 1:, :] - values_grid[:, :, :-1, :])
    east_flux = east_face * (jnp.roll(values_grid, -1, axis=3) - values_grid)
    lateral = east_flux - jnp.roll(east_flux, 1, axis=3)
    return (
        ocean_ext[1:-1] * values_grid[:, :, 1:-1, :]
        + north_flux[:, :, 1:, :]
        - north_flux[:, :, :-1, :]
        + lateral[:, :, 1:-1, :]
    )


def lateral_pass(values_tile, faces):
    north_face, east_face, ocean_ext = faces
    grown = padded(values_tile, (("gy", 2),), NSTEP)
    total_rows = grown.shape[2]
    for step_index in range(NSTEP):
        upper = total_rows - step_index
        grown = diffuse_once(
            grown,
            north_face[step_index:upper],
            east_face[step_index:upper],
            ocean_ext[step_index:upper],
        )
    return grown


def vertical_factors(vert_coef):
    inverse_rows = []
    upper_ratio = []
    for layer_index in range(vert_coef.shape[0]):
        diagonal = 1.0 + vert_coef[layer_index]
        if layer_index > 0:
            diagonal = (
                diagonal + vert_coef[layer_index - 1] + vert_coef[layer_index - 1] * upper_ratio[-1]
            )
        inverse = 1.0 / diagonal
        inverse_rows.append(inverse)
        upper_ratio.append(-vert_coef[layer_index] * inverse)
    return (inverse_rows, upper_ratio)


def vertical_solve(values_col, vert_coef, factors):
    inverse_rows, upper_ratio = factors
    layers = values_col.shape[1]
    forward = []
    for layer_index in range(layers):
        source = values_col[:, layer_index]
        if layer_index > 0:
            source = source + vert_coef[layer_index - 1] * forward[-1]
        forward.append(source * inverse_rows[layer_index])
    result = [forward[-1]]
    for layer_index in range(layers - 2, -1, -1):
        result.append(forward[layer_index] - upper_ratio[layer_index] * result[-1])
    return jnp.stack(result[::-1], axis=1)


def observe_weigh_spread(columns, obs_owner, obs_row, obs_col, obs_frac, error_inverse):
    var_count, lev_count, lat_rows, lon_cols = columns.shape
    kv_width = var_count * lev_count
    rows_y = lax.axis_size("gy")
    cols_x = lax.axis_size("gx")
    device_count = rows_y * cols_x
    obs_count = obs_row.shape[-1]
    capacity = 2 * obs_count // device_count
    flat = columns.reshape(kv_width, lat_rows * lon_cols)
    cell = obs_row.reshape(-1) * lon_cols + obs_col.reshape(-1)
    corners = (cell, cell + 1, cell + lon_cols, cell + lon_cols + 1)
    lat_frac = obs_frac[0, 0, 0]
    lon_frac = obs_frac[0, 0, 1]
    weights = (
        (1.0 - lat_frac) * (1.0 - lon_frac),
        (1.0 - lat_frac) * lon_frac,
        lat_frac * (1.0 - lon_frac),
        lat_frac * lon_frac,
    )
    profile = weights[0] * jnp.take(flat, corners[0], axis=1)
    for corner_index in range(1, 4):
        profile = profile + weights[corner_index] * jnp.take(flat, corners[corner_index], axis=1)
    owners = obs_owner.reshape(-1)
    onehot = (owners[:, None] == jnp.arange(device_count, dtype=jnp.int32)[None, :]).astype(
        jnp.int32
    )
    running = jnp.cumsum(onehot, axis=0)
    rank_in = jnp.sum(running * onehot, axis=1) - 1
    slot = owners * capacity + rank_in
    outgoing = jnp.zeros((device_count * capacity, kv_width), jnp.float32).at[slot].set(profile.T)
    outgoing = outgoing.reshape(rows_y, cols_x, capacity, kv_width)
    matrix = error_inverse.reshape(kv_width, kv_width)
    arrived = lax.all_to_all(
        lax.all_to_all(outgoing, "gy", split_axis=0, concat_axis=0, tiled=True),
        "gx",
        split_axis=1,
        concat_axis=1,
        tiled=True,
    )
    weighted = jnp.dot(
        arrived.reshape(-1, kv_width),
        matrix,
        precision=lax.Precision.HIGHEST,
        preferred_element_type=jnp.float32,
    ).reshape(rows_y, cols_x, capacity, kv_width)
    returned = lax.all_to_all(
        lax.all_to_all(weighted, "gy", split_axis=0, concat_axis=0, tiled=True),
        "gx",
        split_axis=1,
        concat_axis=1,
        tiled=True,
    )
    back = returned.reshape(device_count * capacity, kv_width)[slot].T
    spread = jnp.zeros((kv_width, lat_rows * lon_cols), jnp.float32)
    for corner_index in range(4):
        spread = spread.at[:, corners[corner_index]].add(weights[corner_index] * back)
    return spread.reshape(var_count, lev_count, lat_rows, lon_cols)


def per_device(
    direction,
    solution,
    residual,
    north_coef,
    east_coef,
    ocean,
    vert_coef,
    obs_owner,
    obs_row,
    obs_col,
    obs_frac,
    error_inverse,
):
    stacked = jnp.stack([north_coef, east_coef, ocean.astype(jnp.float32)])
    reach = NSTEP
    grown_coef = padded(stacked, (("gy", 1),), reach)
    faces = lateral_faces(grown_coef[0], grown_coef[1], grown_coef[2])
    factors = vertical_factors(vert_coef)
    smoothed = lateral_pass(direction, faces)
    columns = lax.all_to_all(smoothed, "gx", split_axis=3, concat_axis=1, tiled=True)
    columns = vertical_solve(columns, vert_coef, factors)
    spread = observe_weigh_spread(columns, obs_owner, obs_row, obs_col, obs_frac, error_inverse)
    spread = vertical_solve(spread, vert_coef, factors)
    tiles = lax.all_to_all(spread, "gx", split_axis=1, concat_axis=3, tiled=True)
    image = direction + lateral_pass(tiles, faces)
    norm_now, curvature = lax.psum(
        (jnp.sum(residual * residual), jnp.sum(direction * image)), ("gy", "gx")
    )
    alpha = norm_now / curvature
    residual_next = residual - alpha * image
    norm_next = lax.psum(jnp.sum(residual_next * residual_next), ("gy", "gx"))
    solution_next = solution + alpha * direction
    direction_next = residual_next + norm_next / norm_now * direction
    return (solution_next, residual_next, direction_next)


def solution(mesh):
    in_specs = (
        P(None, "gx", "gy", None),
        P(None, "gx", "gy", None),
        P(None, "gx", "gy", None),
        P("gy", None),
        P("gy", None),
        P("gy", None),
        P(None, "gy", "gx"),
        P("gy", "gx", None, None),
        P("gy", "gx", None),
        P("gy", "gx", None),
        P("gy", "gx", None, None),
        P("gy", "gx", None, None),
    )
    out_specs = (P(None, "gx", "gy", None),) * 3

    def step(*arrays):
        shapes = [arrays[at].shape for at in (0, 6, 8, 11)]
        local = per_device_gathered if gathers(mesh, shapes) else per_device
        return jax.shard_map(
            local, mesh=mesh, in_specs=in_specs, out_specs=out_specs, check_vma=False
        )(*arrays)

    return step
```
